32 devices in a mesh: rep: 2 (over x), seq: 16 (over z, y, core).
Axes of the slice: x: 2, y: 2, z: 4, core: 2. Of those that a mesh axis runs over, the one named last changes fastest.
Arguments:
- keys: bfloat16 [2048, 5120], P(('rep', 'seq')), parts along dimension 0, may hold values from -36 to 36
- values: bfloat16 [2048, 5120], P(('rep', 'seq')), parts along dimension 0, may hold values from -6 to 6
- queries: bfloat16 [2, 1024, 5120], P(None, ('rep', 'seq')), parts along dimension 1, may hold values from -6 to 6
Outputs:
- attended: bfloat16 [2, 1024, 5120], P(None, ('rep', 'seq')), parts along dimension 1
The draws below stay inside these ranges and needn't reach their ends.
There are 2 independent parts, one for each index of `rep`. The reference program is written for one: setup_inputs(seed, part) draws one part's arguments, and reference() takes and returns one part's arrays. A program takes and returns all parts, laid end to end along the dimension named above; each array names one. Nothing has to cross between parts.
All inputs are finite; a program needn't handle non-finite values.
Results may differ from the reference program's by a relative error of at most 0.0038.
Values may be sent and summed in bfloat16 or wider, within the bound.
No kernel may reach another device: no remote copies, remote signals or barrier semaphores. Data moves between devices by JAX's collectives and lax.ppermute only.
A program may use at most 128 MiB of HBM per device.

```python
import math
import jax
import jax.numpy as jnp
from jax import lax

D = 5120
HEADS = 40
HEAD_DIM = 128
CTX_DEV = 64
QUERY_TOKENS = 512
LAYERS = 2
CONTEXT = 1024


key_floor = 2.0


aligned_gain = 0.8


def shared_pattern(key):
    return jnp.sign(jax.random.normal(jax.random.fold_in(key, 41), (D,), jnp.float32))


def drawn_positions(key):
    block_count = CONTEXT // CTX_DEV
    offsets = jax.random.randint(jax.random.fold_in(key, 42), (block_count,), 4, CTX_DEV)
    return jnp.arange(block_count, dtype=jnp.int32) * CTX_DEV + offsets


def draw_keys(key, part):
    row_scale = jnp.exp(jax.random.uniform(jax.random.fold_in(key, 22), (CONTEXT, 1), jnp.float32, math.log(2.5), math.log(6.0)))
    base = jnp.clip(jax.random.normal(jax.random.fold_in(key, 21), (CONTEXT, D), jnp.float32), -6.0, 6.0)
    drawn = base * row_scale
    positions = drawn_positions(key)
    floor_rows = jnp.broadcast_to(key_floor * shared_pattern(key)[None], (positions.shape[0], D))
    drawn = drawn.at[positions].set(floor_rows)
    return drawn.astype(jnp.bfloat16)


def draw_queries(key, part):
    aligned = jnp.arange(QUERY_TOKENS, dtype=jnp.int32) % 4 == 2
    noise = jax.random.normal(jax.random.fold_in(key, 32), (LAYERS, QUERY_TOKENS, D), jnp.float32)
    matched = jnp.clip(aligned_gain * shared_pattern(key)[None, None] + 0.25 * noise, -6.0, 6.0)
    drawn = jnp.clip(jax.random.normal(jax.random.fold_in(key, 31), (LAYERS, QUERY_TOKENS, D), jnp.float32), -6.0, 6.0)
    drawn = jnp.where(aligned[None, :, None], matched, drawn)
    return drawn.astype(jnp.bfloat16)


def level_of(key, extent, cuts, least, top_value):
    def one(dim, shards_of):
        steps = jax.random.uniform(jax.random.fold_in(jax.random.fold_in(key, 6), dim), (shards_of,), jnp.float32, least / len(cuts), top_value / len(cuts))
        return jnp.repeat(jnp.exp(steps), extent[dim] // shards_of).reshape((-1,) + (1,) * (len(extent) - dim - 1))

    gain = one(*cuts[0])
    for cut in cuts[1:]:
        gain = gain * one(*cut)
    return gain


def gaussian(own_key, dims, spread, most, pieces=(), held_as=jnp.bfloat16):
    loudness = level_of(own_key, dims, pieces, -0.22, 0.18) if pieces else 1.0
    values = jax.random.normal(own_key, dims, jnp.float32) * spread * loudness
    return jnp.minimum(jnp.maximum(values, -most), most).astype(held_as)


def setup_inputs(seed: int = 0, part: int = 0) -> dict:
    streams_of = jax.random.split(jax.random.key(seed), 4)
    part_keys = jax.random.split(jax.random.fold_in(streams_of[3], part), 4)
    keys = draw_keys(jax.random.fold_in(jax.random.fold_in(streams_of[3], part), 71), part)
    values = gaussian(part_keys[1], (CONTEXT, D), 1.0, 6.0, ((0, 16),))
    queries = draw_queries(jax.random.fold_in(jax.random.fold_in(streams_of[3], part), 71), part)
    return dict(keys=keys, values=values, queries=queries)


def reference(keys, values, queries):
    scale = 1.0 / math.sqrt(HEAD_DIM)
    layer_outs = []
    for layer in range(LAYERS):
        query_layer = queries[layer]

        def one_head(head):
            start = head * HEAD_DIM
            q_head = lax.dynamic_slice_in_dim(query_layer, start, HEAD_DIM, 1)
            k_head = lax.dynamic_slice_in_dim(keys, start, HEAD_DIM, 1)
            v_head = lax.dynamic_slice_in_dim(values, start, HEAD_DIM, 1)
            scores = lax.dot_general(q_head, k_head, (((1,), (1,)), ((), ())), preferred_element_type=jnp.float32) * scale
            peak = lax.optimization_barrier(jnp.max(scores, axis=1))
            expo = jnp.exp(scores - peak[:, None])
            total = lax.optimization_barrier(jnp.sum(expo, axis=1))
            summed = jnp.dot(expo.astype(jnp.bfloat16), v_head, preferred_element_type=jnp.float32)
            return (summed / total[:, None]).astype(jnp.bfloat16)
        per_head = lax.map(one_head, jnp.arange(HEADS, dtype=jnp.int32))
        layer_outs.append(jnp.transpose(per_head, (1, 0, 2)).reshape(QUERY_TOKENS, D))
    return jnp.stack(layer_outs)
```

```python
import functools
import math

import jax
import jax.numpy as jnp
from jax import lax
from jax.experimental import pallas as pl
from jax.experimental.pallas import tpu as pltpu
from jax.sharding import Mesh, PartitionSpec as P

HEAD_DIM = 128
GROUPS = 8
SUB = 128
F32 = jnp.float32


def attend_head(partial, q_ref, ka_ref, va_ref, kb_ref, vb_ref, o_ref, *stat_refs):
    src, rows, _ = q_ref.shape
    q = q_ref[...].reshape(src * rows, HEAD_DIM)
    ka, va, kb, vb = (r[...].reshape(-1, HEAD_DIM) for r in (ka_ref, va_ref, kb_ref, vb_ref))
    factor = math.log2(math.e) / math.sqrt(HEAD_DIM)
    nt = (((1,), (1,)), ((), ()))
    outs = []
    for at in range(0, src * rows, SUB):
        part = q[at : at + SUB]
        sa = lax.dot_general(part, ka, nt, preferred_element_type=F32)
        sb = lax.dot_general(part, kb, nt, preferred_element_type=F32)
        peak = jnp.maximum(jnp.max(sa, axis=1, keepdims=True), jnp.max(sb, axis=1, keepdims=True))
        ea = jnp.exp2((sa - peak) * factor)
        eb = jnp.exp2((sb - peak) * factor)
        total = jnp.sum(ea, axis=1, keepdims=True) + jnp.sum(eb, axis=1, keepdims=True)
        acc = jnp.dot(ea.astype(jnp.bfloat16), va, preferred_element_type=F32)
        acc = acc + jnp.dot(eb.astype(jnp.bfloat16), vb, preferred_element_type=F32)
        if not partial:
            acc = acc / total
        outs.append(acc)
        if partial:
            stat_refs[0][at : at + SUB] = jnp.broadcast_to(peak * factor, (SUB, HEAD_DIM))
            stat_refs[1][at : at + SUB] = jnp.broadcast_to(total, (SUB, HEAD_DIM))
    o_ref[...] = jnp.concatenate(outs, axis=0).reshape(o_ref.shape).astype(o_ref.dtype)


def attend(got, other, rows_kv, rows_q, partial):
    chips, _, width = got.shape
    heads = width // HEAD_DIM
    own_kv = got[:, : 2 * rows_kv].reshape(chips, 2, rows_kv, width)
    own_q = got[:, 2 * rows_kv :]
    other = other.reshape(chips, 2, rows_kv, width)

    def kv(which):
        return pl.BlockSpec((chips, None, rows_kv, HEAD_DIM), lambda h: (0, which, 0, h))

    q_spec = pl.BlockSpec((chips, rows_q, HEAD_DIM), lambda h: (0, 0, h))
    dtype = F32 if partial else jnp.bfloat16
    out_shape = [jax.ShapeDtypeStruct((chips, rows_q, width), dtype)]
    out_specs = [pl.BlockSpec((chips, rows_q, HEAD_DIM), lambda h: (0, 0, h))]
    if partial:
        out_shape += [jax.ShapeDtypeStruct((heads, chips * rows_q, HEAD_DIM), F32)] * 2
        out_specs += [pl.BlockSpec((None, chips * rows_q, HEAD_DIM), lambda h: (h, 0, 0))] * 2
    queries, keys = chips * rows_q, 2 * chips * rows_kv
    return pl.pallas_call(
        functools.partial(attend_head, partial),
        grid=(heads,),
        in_specs=[q_spec, kv(0), kv(1), kv(0), kv(1)],
        out_specs=out_specs,
        out_shape=out_shape,
        compiler_params=pltpu.CompilerParams(vmem_limit_bytes=40 * 2**20),
        cost_estimate=pl.CostEstimate(
            flops=4 * queries * keys * width,
            bytes_accessed=2 * width * (2 * queries + 2 * keys),
            transcendentals=heads * queries * keys,
        ),
    )(own_q, own_kv, own_kv, other, other)


def local(keys, values, queries):
    chips = lax.axis_size("chip")
    blocks = chips // GROUPS
    ctx_rows, width = keys.shape
    gw = width // GROUPS
    heads = gw // HEAD_DIM
    layers, tok_rows, _ = queries.shape
    rows_q = layers * tok_rows
    rows_kv = ctx_rows // blocks
    partial = blocks > 1

    def by_chip(array):
        return jnp.swapaxes(array.reshape(rows_kv, chips, gw), 0, 1)

    q = jnp.swapaxes(queries.reshape(rows_q, GROUPS, gw), 0, 1)
    q = jnp.broadcast_to(q[None], (blocks, GROUPS, rows_q, gw)).reshape(chips, rows_q, gw)
    packed = jnp.concatenate([by_chip(keys), by_chip(values), q], axis=1)
    got = lax.all_to_all(packed, "chip", split_axis=0, concat_axis=0, tiled=True)
    other = lax.ppermute(got[:, : 2 * rows_kv], "core", [(0, 1), (1, 0)])
    outs = attend(got, other, rows_kv, rows_q, partial)
    if not partial:
        back = lax.all_to_all(outs[0], "chip", split_axis=0, concat_axis=0, tiled=True)
        return jnp.swapaxes(back, 0, 1).reshape(layers, tok_rows, width)
    stats = [jnp.moveaxis(s[:, :, 0].reshape(heads, chips, rows_q), 0, 2) for s in outs[1:]]
    stats = jnp.concatenate(stats, axis=2)
    stats = jnp.pad(stats, ((0, 0), (0, 0), (0, -2 * heads % HEAD_DIM)))
    sent = jnp.concatenate([outs[0], stats], axis=2)
    back = lax.all_to_all(sent, "chip", split_axis=0, concat_axis=0, tiled=True)
    back = back.reshape(blocks, GROUPS, rows_q, -1)
    summed = back[..., :gw].reshape(blocks, GROUPS, rows_q, heads, HEAD_DIM)
    peak = back[..., gw : gw + heads]
    total = back[..., gw + heads : gw + 2 * heads]
    share = jnp.exp2(peak - jnp.max(peak, axis=0))
    denom = jnp.sum(share * total, axis=0)
    numer = jnp.sum(share[..., None] * summed, axis=0)
    result = (numer / denom[..., None]).astype(jnp.bfloat16)
    return jnp.swapaxes(result.reshape(GROUPS, rows_q, gw), 0, 1).reshape(layers, tok_rows, width)


def solution(mesh):
    rep, seq = mesh.shape["rep"], mesh.shape["seq"]
    by_core = Mesh(mesh.devices.reshape(rep, seq // 2, 2), ("rep", "chip", "core"))
    rows = ("rep", "chip", "core")
    return jax.shard_map(
        local,
        mesh=by_core,
        in_specs=(P(rows, None), P(rows, None), P(None, rows, None)),
        out_specs=P(None, rows, None),
        check_vma=False,
    )
```

```python
import functools
import math

import jax
import jax.numpy as jnp
from jax import lax
from jax.experimental import pallas as pl
from jax.experimental.pallas import tpu as pltpu
from jax.sharding import Mesh, PartitionSpec as P

HEAD_DIM = 128
GROUPS = 8
SUB = 128
F32 = jnp.float32
BF16 = jnp.bfloat16
VMEM = pl.BlockSpec(memory_space=pltpu.VMEM)
SMEM = pl.BlockSpec(memory_space=pltpu.SMEM)
PARAMS = pltpu.CompilerParams(vmem_limit_bytes=40 * 2**20)


def softmax_rows(q, ka, va, kb, vb):
    factor = math.log2(math.e) / math.sqrt(HEAD_DIM)
    nt = (((1,), (1,)), ((), ()))
    sa = lax.dot_general(q, ka, nt, preferred_element_type=F32)
    sb = lax.dot_general(q, kb, nt, preferred_element_type=F32)
    peak = jnp.maximum(jnp.max(sa, axis=1, keepdims=True), jnp.max(sb, axis=1, keepdims=True))
    ea = jnp.exp2((sa - peak) * factor)
    eb = jnp.exp2((sb - peak) * factor)
    total = jnp.sum(ea, axis=1, keepdims=True) + jnp.sum(eb, axis=1, keepdims=True)
    acc = jnp.dot(ea.astype(BF16), va, preferred_element_type=F32)
    acc = acc + jnp.dot(eb.astype(BF16), vb, preferred_element_type=F32)
    return acc, peak * factor, total


def pack_body(rows, gw, chip_ref, keys_ref, values_ref, queries_ref, *out_refs):
    for k, out_ref in enumerate(out_refs):
        col = pl.ds(pl.multiple_of((chip_ref[0] ^ k) * gw, HEAD_DIM), gw)
        out_ref[:rows] = keys_ref[:, col]
        out_ref[rows : 2 * rows] = values_ref[:, col]
        out_ref[2 * rows :] = queries_ref[:, col]


def unpack_body(gw, chip_ref, *refs):
    out_ref = refs[-1]
    for k, piece_ref in enumerate(refs[:-1]):
        out_ref[:, pl.ds(pl.multiple_of((chip_ref[0] ^ k) * gw, HEAD_DIM), gw)] = piece_ref[...]


def attend_body(chips, rows, *refs):
    own, other, outs = refs[:chips], refs[chips : 2 * chips], refs[2 * chips :]
    heads = own[0].shape[1] // HEAD_DIM
    rows_q = own[0].shape[0] - 2 * rows
    for h in range(heads):
        col = slice(h * HEAD_DIM, (h + 1) * HEAD_DIM)

        def gather(pieces, at):
            return jnp.concatenate([r[at : at + rows, col] for r in pieces], axis=0)

        ka, va, kb, vb = gather(own, 0), gather(own, rows), gather(other, 0), gather(other, rows)
        step = SUB // rows_q
        for first in range(0, chips, step):
            q = jnp.concatenate([r[2 * rows :, col] for r in own[first : first + step]], axis=0)
            acc, _, total = softmax_rows(q, ka, va, kb, vb)
            acc = (acc / total).astype(BF16)
            for n in range(step):
                outs[first + n][:, col] = acc[n * rows_q : (n + 1) * rows_q]


def local_permutes(keys, values, queries):
    chips = lax.axis_size("chip")
    rows, width = keys.shape
    gw = width // chips
    layers, tok_rows, _ = queries.shape
    rows_q = layers * tok_rows
    chip = lax.axis_index("chip").reshape(1).astype(jnp.int32)

    def across(piece, k):
        return lax.ppermute(piece, "chip", [(i, i ^ k) for i in range(chips)]) if k else piece

    packed = pl.pallas_call(
        functools.partial(pack_body, rows, gw),
        in_specs=[SMEM, VMEM, VMEM, VMEM],
        out_specs=[VMEM] * chips,
        out_shape=[jax.ShapeDtypeStruct((2 * rows + rows_q, gw), BF16)] * chips,
        compiler_params=PARAMS,
    )(chip, keys, values, queries.reshape(rows_q, width))
    order = sorted(range(chips), key=lambda k: -k)
    own = {k: across(packed[k], k) for k in order}
    other = {k: lax.ppermute(own[k][: 2 * rows], "core", [(0, 1), (1, 0)]) for k in reversed(order)}
    outs = pl.pallas_call(
        functools.partial(attend_body, chips, rows),
        in_specs=[VMEM] * (2 * chips),
        out_specs=[VMEM] * chips,
        out_shape=[jax.ShapeDtypeStruct((rows_q, gw), BF16)] * chips,
        compiler_params=PARAMS,
    )(*[own[k] for k in range(chips)], *[other[k] for k in range(chips)])
    back = {k: across(outs[k], k) for k in order}
    result = pl.pallas_call(
        functools.partial(unpack_body, gw),
        in_specs=[SMEM] + [VMEM] * chips,
        out_specs=VMEM,
        out_shape=jax.ShapeDtypeStruct((rows_q, width), BF16),
        compiler_params=PARAMS,
    )(chip, *[back[k] for k in range(chips)])
    return result.reshape(layers, tok_rows, width)


def partial_head(q_ref, ka_ref, va_ref, kb_ref, vb_ref, o_ref, peak_ref, total_ref):
    src, rows, _ = q_ref.shape
    q = q_ref[...].reshape(src * rows, HEAD_DIM)
    kv = [r[...].reshape(-1, HEAD_DIM) for r in (ka_ref, va_ref, kb_ref, vb_ref)]
    outs = []
    for at in range(0, src * rows, SUB):
        acc, peak, total = softmax_rows(q[at : at + SUB], *kv)
        outs.append(acc)
        peak_ref[at : at + SUB] = jnp.broadcast_to(peak, (SUB, HEAD_DIM))
        total_ref[at : at + SUB] = jnp.broadcast_to(total, (SUB, HEAD_DIM))
    o_ref[...] = jnp.concatenate(outs, axis=0).reshape(o_ref.shape)


def partial_attend(got, other, rows_kv, rows_q):
    chips, _, width = got.shape
    heads = width // HEAD_DIM
    own_kv = got[:, : 2 * rows_kv].reshape(chips, 2, rows_kv, width)
    own_q = got[:, 2 * rows_kv :]
    other = other.reshape(chips, 2, rows_kv, width)

    def kv(which):
        return pl.BlockSpec((chips, None, rows_kv, HEAD_DIM), lambda h: (0, which, 0, h))

    q_spec = pl.BlockSpec((chips, rows_q, HEAD_DIM), lambda h: (0, 0, h))
    stat_spec = pl.BlockSpec((None, chips * rows_q, HEAD_DIM), lambda h: (h, 0, 0))
    stat = jax.ShapeDtypeStruct((heads, chips * rows_q, HEAD_DIM), F32)
    return pl.pallas_call(
        partial_head,
        grid=(heads,),
        in_specs=[q_spec, kv(0), kv(1), kv(0), kv(1)],
        out_specs=[q_spec, stat_spec, stat_spec],
        out_shape=[jax.ShapeDtypeStruct((chips, rows_q, width), F32), stat, stat],
        compiler_params=PARAMS,
    )(own_q, own_kv, own_kv, other, other)


def local_blocks(keys, values, queries):
    chips = lax.axis_size("chip")
    blocks = chips // GROUPS
    ctx_rows, width = keys.shape
    gw = width // GROUPS
    heads = gw // HEAD_DIM
    layers, tok_rows, _ = queries.shape
    rows_q = layers * tok_rows
    rows_kv = ctx_rows // blocks

    def by_chip(array):
        return jnp.swapaxes(array.reshape(rows_kv, chips, gw), 0, 1)

    q = jnp.swapaxes(queries.reshape(rows_q, GROUPS, gw), 0, 1)
    q = jnp.broadcast_to(q[None], (blocks, GROUPS, rows_q, gw)).reshape(chips, rows_q, gw)
    packed = jnp.concatenate([by_chip(keys), by_chip(values), q], axis=1)
    got = lax.all_to_all(packed, "chip", split_axis=0, concat_axis=0, tiled=True)
    other = lax.ppermute(got[:, : 2 * rows_kv], "core", [(0, 1), (1, 0)])
    outs = partial_attend(got, other, rows_kv, rows_q)
    stats = [jnp.moveaxis(s[:, :, 0].reshape(heads, chips, rows_q), 0, 2) for s in outs[1:]]
    stats = jnp.concatenate(stats, axis=2)
    stats = jnp.pad(stats, ((0, 0), (0, 0), (0, -2 * heads % HEAD_DIM)))
    sent = jnp.concatenate([outs[0], stats], axis=2)
    back = lax.all_to_all(sent, "chip", split_axis=0, concat_axis=0, tiled=True)
    back = back.reshape(blocks, GROUPS, rows_q, -1)
    summed = back[..., :gw].reshape(blocks, GROUPS, rows_q, heads, HEAD_DIM)
    peak = back[..., gw : gw + heads]
    total = back[..., gw + heads : gw + 2 * heads]
    share = jnp.exp2(peak - jnp.max(peak, axis=0))
    denom = jnp.sum(share * total, axis=0)
    numer = jnp.sum(share[..., None] * summed, axis=0)
    result = (numer / denom[..., None]).astype(BF16)
    return jnp.swapaxes(result.reshape(GROUPS, rows_q, gw), 0, 1).reshape(layers, tok_rows, width)


def solution(mesh):
    rep, seq = mesh.shape["rep"], mesh.shape["seq"]
    chips = seq // 2
    by_core = Mesh(mesh.devices.reshape(rep, chips, 2), ("rep", "chip", "core"))
    rows = ("rep", "chip", "core")
    return jax.shard_map(
        local_permutes if chips == GROUPS else local_blocks,
        mesh=by_core,
        in_specs=(P(rows, None), P(rows, None), P(None, rows, None)),
        out_specs=P(None, rows, None),
        check_vma=False,
    )
```

```python
import functools
import math

import jax
import jax.numpy as jnp
from jax import lax
from jax.experimental import pallas as pl
from jax.experimental.pallas import tpu as pltpu
from jax.sharding import Mesh, PartitionSpec as P

HEAD_DIM = 128
GROUPS = 8
SUB = 128
F32 = jnp.float32
BF16 = jnp.bfloat16
VMEM = pl.BlockSpec(memory_space=pltpu.VMEM)
ANY = pl.BlockSpec(memory_space=pl.ANY)
SMEM = pl.BlockSpec(memory_space=pltpu.SMEM)
PARAMS = pltpu.CompilerParams(vmem_limit_bytes=40 * 2**20)


def softmax_rows(q, ka, va, kb, vb):
    factor = math.log2(math.e) / math.sqrt(HEAD_DIM)
    nt = (((1,), (1,)), ((), ()))
    sa = lax.dot_general(q, ka, nt, preferred_element_type=F32)
    sb = lax.dot_general(q, kb, nt, preferred_element_type=F32)
    peak = jnp.maximum(jnp.max(sa, axis=1, keepdims=True), jnp.max(sb, axis=1, keepdims=True))
    ea = jnp.exp2((sa - peak) * factor)
    eb = jnp.exp2((sb - peak) * factor)
    total = jnp.sum(ea, axis=1, keepdims=True) + jnp.sum(eb, axis=1, keepdims=True)
    acc = jnp.dot(ea.astype(BF16), va, preferred_element_type=F32)
    acc = acc + jnp.dot(eb.astype(BF16), vb, preferred_element_type=F32)
    return acc, peak * factor, total


def pack_body(order, gw, chip_ref, *refs):
    arrays, out_refs, sems = refs[:3], refs[3:-1], refs[-1]
    copies = []
    for k in order:
        col = pl.ds(pl.multiple_of((chip_ref[0] ^ k) * gw, HEAD_DIM), gw)
        at = 0
        for n, array in enumerate(arrays):
            to = out_refs[k].at[at : at + array.shape[0]]
            copies.append(pltpu.make_async_copy(array.at[:, col], to, sems.at[k, n]))
            at += array.shape[0]
    for copy in copies:
        copy.start()
    for copy in copies:
        copy.wait()


def unpack_body(gw, chip_ref, *refs):
    out_ref = refs[-1]
    for k, piece_ref in enumerate(refs[:-1]):
        out_ref[:, pl.ds(pl.multiple_of((chip_ref[0] ^ k) * gw, HEAD_DIM), gw)] = piece_ref[...]


def attend_body(chips, rows, *refs):
    own, other, outs = refs[:chips], refs[chips : 2 * chips], refs[2 * chips :]
    heads = own[0].shape[1] // HEAD_DIM
    rows_q = own[0].shape[0] - 2 * rows
    for h in range(heads):
        col = slice(h * HEAD_DIM, (h + 1) * HEAD_DIM)

        def gather(pieces, at):
            return jnp.concatenate([r[at : at + rows, col] for r in pieces], axis=0)

        ka, va, kb, vb = gather(own, 0), gather(own, rows), gather(other, 0), gather(other, rows)
        step = SUB // rows_q
        for first in range(0, chips, step):
            q = jnp.concatenate([r[2 * rows :, col] for r in own[first : first + step]], axis=0)
            acc, _, total = softmax_rows(q, ka, va, kb, vb)
            acc = (acc / total).astype(BF16)
            for n in range(step):
                outs[first + n][:, col] = acc[n * rows_q : (n + 1) * rows_q]


def local_permutes(keys, values, queries):
    chips = lax.axis_size("chip")
    rows, width = keys.shape
    gw = width // chips
    layers, tok_rows, _ = queries.shape
    rows_q = layers * tok_rows
    chip = lax.axis_index("chip").reshape(1).astype(jnp.int32)

    def across(piece, k):
        return lax.ppermute(piece, "chip", [(i, i ^ k) for i in range(chips)]) if k else piece

    order = (1, 7, 2, 6, 3, 5, 4, 0)
    packed = pl.pallas_call(
        functools.partial(pack_body, order, gw),
        in_specs=[SMEM, ANY, ANY, ANY],
        out_specs=[VMEM] * chips,
        out_shape=[jax.ShapeDtypeStruct((2 * rows + rows_q, gw), BF16)] * chips,
        scratch_shapes=[pltpu.SemaphoreType.DMA((chips, 3))],
        compiler_params=PARAMS,
    )(chip, keys, values, queries.reshape(rows_q, width))
    own = {k: across(packed[k], k) for k in order}
    other = {k: lax.ppermute(own[k][: 2 * rows], "core", [(0, 1), (1, 0)]) for k in (0,) + order[:-1]}
    outs = pl.pallas_call(
        functools.partial(attend_body, chips, rows),
        in_specs=[VMEM] * (2 * chips),
        out_specs=[VMEM] * chips,
        out_shape=[jax.ShapeDtypeStruct((rows_q, gw), BF16)] * chips,
        compiler_params=PARAMS,
    )(*[own[k] for k in range(chips)], *[other[k] for k in range(chips)])
    back = {k: across(outs[k], k) for k in order}
    result = pl.pallas_call(
        functools.partial(unpack_body, gw),
        in_specs=[SMEM] + [VMEM] * chips,
        out_specs=VMEM,
        out_shape=jax.ShapeDtypeStruct((rows_q, width), BF16),
        compiler_params=PARAMS,
    )(chip, *[back[k] for k in range(chips)])
    return result.reshape(layers, tok_rows, width)


def partial_head(q_ref, ka_ref, va_ref, kb_ref, vb_ref, o_ref, peak_ref, total_ref):
    src, rows, _ = q_ref.shape
    q = q_ref[...].reshape(src * rows, HEAD_DIM)
    kv = [r[...].reshape(-1, HEAD_DIM) for r in (ka_ref, va_ref, kb_ref, vb_ref)]
    outs = []
    for at in range(0, src * rows, SUB):
        acc, peak, total = softmax_rows(q[at : at + SUB], *kv)
        outs.append(acc)
        peak_ref[at : at + SUB] = jnp.broadcast_to(peak, (SUB, HEAD_DIM))
        total_ref[at : at + SUB] = jnp.broadcast_to(total, (SUB, HEAD_DIM))
    o_ref[...] = jnp.concatenate(outs, axis=0).reshape(o_ref.shape)


def partial_attend(got, other, rows_kv, rows_q):
    chips, _, width = got.shape
    heads = width // HEAD_DIM
    own_kv = got[:, : 2 * rows_kv].reshape(chips, 2, rows_kv, width)
    own_q = got[:, 2 * rows_kv :]
    other = other.reshape(chips, 2, rows_kv, width)

    def kv(which):
        return pl.BlockSpec((chips, None, rows_kv, HEAD_DIM), lambda h: (0, which, 0, h))

    q_spec = pl.BlockSpec((chips, rows_q, HEAD_DIM), lambda h: (0, 0, h))
    stat_spec = pl.BlockSpec((None, chips * rows_q, HEAD_DIM), lambda h: (h, 0, 0))
    stat = jax.ShapeDtypeStruct((heads, chips * rows_q, HEAD_DIM), F32)
    return pl.pallas_call(
        partial_head,
        grid=(heads,),
        in_specs=[q_spec, kv(0), kv(1), kv(0), kv(1)],
        out_specs=[q_spec, stat_spec, stat_spec],
        out_shape=[jax.ShapeDtypeStruct((chips, rows_q, width), F32), stat, stat],
        compiler_params=PARAMS,
    )(own_q, own_kv, own_kv, other, other)


def local_blocks(keys, values, queries):
    chips = lax.axis_size("chip")
    blocks = chips // GROUPS
    ctx_rows, width = keys.shape
    gw = width // GROUPS
    heads = gw // HEAD_DIM
    layers, tok_rows, _ = queries.shape
    rows_q = layers * tok_rows
    rows_kv = ctx_rows // blocks

    def by_chip(array):
        return jnp.swapaxes(array.reshape(rows_kv, chips, gw), 0, 1)

    q = jnp.swapaxes(queries.reshape(rows_q, GROUPS, gw), 0, 1)
    q = jnp.broadcast_to(q[None], (blocks, GROUPS, rows_q, gw)).reshape(chips, rows_q, gw)
    packed = jnp.concatenate([by_chip(keys), by_chip(values), q], axis=1)
    got = lax.all_to_all(packed, "chip", split_axis=0, concat_axis=0, tiled=True)
    other = lax.ppermute(got[:, : 2 * rows_kv], "core", [(0, 1), (1, 0)])
    outs = partial_attend(got, other, rows_kv, rows_q)
    stats = [jnp.moveaxis(s[:, :, 0].reshape(heads, chips, rows_q), 0, 2) for s in outs[1:]]
    stats = jnp.concatenate(stats, axis=2)
    stats = jnp.pad(stats, ((0, 0), (0, 0), (0, -2 * heads % HEAD_DIM)))
    sent = jnp.concatenate([outs[0], stats], axis=2)
    back = lax.all_to_all(sent, "chip", split_axis=0, concat_axis=0, tiled=True)
    back = back.reshape(blocks, GROUPS, rows_q, -1)
    summed = back[..., :gw].reshape(blocks, GROUPS, rows_q, heads, HEAD_DIM)
    peak = back[..., gw : gw + heads]
    total = back[..., gw + heads : gw + 2 * heads]
    share = jnp.exp2(peak - jnp.max(peak, axis=0))
    denom = jnp.sum(share * total, axis=0)
    numer = jnp.sum(share[..., None] * summed, axis=0)
    result = (numer / denom[..., None]).astype(BF16)
    return jnp.swapaxes(result.reshape(GROUPS, rows_q, gw), 0, 1).reshape(layers, tok_rows, width)


def solution(mesh):
    rep, seq = mesh.shape["rep"], mesh.shape["seq"]
    chips = seq // 2
    by_core = Mesh(mesh.devices.reshape(rep, chips, 2), ("rep", "chip", "core"))
    rows = ("rep", "chip", "core")
    return jax.shard_map(
        local_permutes if chips == GROUPS else local_blocks,
        mesh=by_core,
        in_specs=(P(rows, None), P(rows, None), P(None, rows, None)),
        out_specs=P(None, rows, None),
        check_vma=False,
    )
```

```python
import functools
import math

import jax
import jax.numpy as jnp
from jax import lax
from jax.experimental import pallas as pl
from jax.experimental.pallas import tpu as pltpu
from jax.sharding import Mesh, PartitionSpec as P

HEAD_DIM = 128
GROUPS = 8
SUB = 128
F32 = jnp.float32
BF16 = jnp.bfloat16
VMEM = pl.BlockSpec(memory_space=pltpu.VMEM)
HBM = pl.BlockSpec(memory_space=pltpu.HBM)
SMEM = pl.BlockSpec(memory_space=pltpu.SMEM)
FREE = pl.CostEstimate(flops=0, bytes_accessed=0, transcendentals=0)
PARAMS = pltpu.CompilerParams(vmem_limit_bytes=40 * 2**20)


def softmax_rows(q, ka, va, kb, vb):
    factor = math.log2(math.e) / math.sqrt(HEAD_DIM)
    nt = (((1,), (1,)), ((), ()))
    sa = lax.dot_general(q, ka, nt, preferred_element_type=F32)
    sb = lax.dot_general(q, kb, nt, preferred_element_type=F32)
    peak = jnp.max(jnp.maximum(sa, sb), axis=1, keepdims=True)
    ea = jnp.exp2((sa - peak) * factor).astype(BF16)
    eb = jnp.exp2((sb - peak) * factor).astype(BF16)
    both = jnp.dot(ea, va, preferred_element_type=F32) + jnp.dot(eb, vb, preferred_element_type=F32)
    return both[:, :HEAD_DIM], peak * factor, both[:, HEAD_DIM:]


def beside_ones(v):
    return jnp.concatenate([v, jnp.ones_like(v)], axis=1)


FAR = (6, 7, 4, 5)
LAST = (6, 7)
NEAR = (2, 3, 1)


def pack_body(rows, gw, layout, chip_ref, *refs):
    arrays, out_refs, sems = refs[:3], refs[3:-1], refs[-1]
    copies = []
    for out_ref, (k, parts) in zip(out_refs, layout):
        col = pl.ds(pl.multiple_of((chip_ref[0] ^ k) * gw, HEAD_DIM), gw)
        for at, n in enumerate(parts):
            to = out_ref.at[at * rows : (at + 1) * rows]
            copies.append(pltpu.make_async_copy(arrays[n].at[:, col], to, sems.at[len(copies)]))
    for copy in copies:
        copy.start()
    for copy in copies:
        copy.wait()


def merge_body(rows, *refs):
    out_ref = refs[-1]
    for n, piece in enumerate(refs[:-1]):
        for which in range(2):
            out_ref[which, n * rows : (n + 1) * rows] = piece[which * rows : (which + 1) * rows]


def unpack_body(gw, order, chip_ref, *refs):
    out_ref = refs[-1]
    for k, piece_ref in zip(order, refs[:-1]):
        out_ref[:, pl.ds(pl.multiple_of((chip_ref[0] ^ k) * gw, HEAD_DIM), gw)] = piece_ref[...]


def attend_body(count, rows, own, other, *refs):
    queries, outs = refs[:count], refs[count:]
    for h in range(own.shape[2] // HEAD_DIM):
        col = slice(h * HEAD_DIM, (h + 1) * HEAD_DIM)
        q = jnp.concatenate([r[r.shape[0] - rows :, col] for r in queries], axis=0)
        va, vb = beside_ones(own[1, :, col]), beside_ones(other[1, :, col])
        acc, _, total = softmax_rows(q, own[0, :, col], va, other[0, :, col], vb)
        acc = (acc / total).astype(BF16)
        for n, out in enumerate(outs):
            out[:, col] = acc[n * rows : (n + 1) * rows]


def local_permutes(keys, values, queries):
    chips = lax.axis_size("chip")
    rows, width = keys.shape
    gw = width // chips
    layers, tok_rows, _ = queries.shape
    rows_q = layers * tok_rows
    assert rows_q == rows
    chip = lax.axis_index("chip").reshape(1).astype(jnp.int32)

    def across(piece, k):
        return lax.ppermute(piece, "chip", [(i, i ^ k) for i in range(chips)]) if k else piece

    def call(body, n_in, out_shape, smem=0, **more):
        return pl.pallas_call(
            body,
            in_specs=[SMEM] * smem + [VMEM] * n_in,
            out_specs=jax.tree.map(lambda _: VMEM, out_shape),
            out_shape=out_shape,
            compiler_params=PARAMS,
            cost_estimate=FREE,
            **more,
        )

    def shape(*dims):
        return jax.ShapeDtypeStruct(dims, BF16)

    layout = [(k, (0, 1) if k in LAST else (0, 1, 2)) for k in FAR + NEAR + (0,)]
    layout += [(k, (2,)) for k in LAST]
    packed = pl.pallas_call(
        functools.partial(pack_body, rows, gw, layout),
        in_specs=[SMEM, HBM, HBM, HBM],
        out_specs=[VMEM] * len(layout),
        out_shape=[shape(len(parts) * rows, gw) for _, parts in layout],
        scratch_shapes=[pltpu.SemaphoreType.DMA((3 * chips,))],
        compiler_params=pltpu.CompilerParams(vmem_limit_bytes=60 * 2**20),
        cost_estimate=FREE,
    )(chip, keys, values, queries.reshape(rows_q, width))
    got = [across(piece, k) for piece, (k, _) in zip(packed, layout)]
    late = dict(zip(LAST, got[chips:]))
    got = {k: piece for piece, (k, _) in zip(got[:chips], layout)}
    own = call(functools.partial(merge_body, rows), chips, shape(2, chips * rows, gw))(*got.values())
    other = lax.ppermute(own, "core", [(0, 1), (1, 0)])

    def attend(ks, after=()):
        pieces = [late.get(k, got[k]) for k in ks]
        if after:
            pieces = lax.optimization_barrier((*pieces, *after))[: len(pieces)]
        body = functools.partial(attend_body, len(ks), rows)
        outs = call(body, 2 + len(ks), [shape(rows, gw)] * len(ks))(own, other, *pieces)
        return dict(zip(ks, outs))

    outs = attend((4, 5))
    outs |= attend(NEAR + (0,), (outs[4],))
    outs |= attend(LAST, (outs[0],))
    order = (4, 5) + NEAR + LAST + (0,)
    back = {k: across(outs[k], k) for k in (4, 5) + NEAR + (0,)}
    for k, before in zip(LAST, (4, 5)):
        back[k] = across(lax.optimization_barrier((outs[k], back[before]))[0], k)
    body = functools.partial(unpack_body, gw, order)
    result = call(body, chips, shape(rows_q, width), smem=1)(chip, *[back[k] for k in order])
    return result.reshape(layers, tok_rows, width)


def partial_head(q_ref, ka_ref, va_ref, kb_ref, vb_ref, o_ref, peak_ref, total_ref):
    src, rows, _ = q_ref.shape
    q = q_ref[...].reshape(src * rows, HEAD_DIM)
    ka, va, kb, vb = (r[...].reshape(-1, HEAD_DIM) for r in (ka_ref, va_ref, kb_ref, vb_ref))
    kv = ka, beside_ones(va), kb, beside_ones(vb)
    outs = []
    for at in range(0, src * rows, SUB):
        acc, peak, total = softmax_rows(q[at : at + SUB], *kv)
        outs.append(acc)
        peak_ref[at : at + SUB] = jnp.broadcast_to(peak, (SUB, HEAD_DIM))
        total_ref[at : at + SUB] = total
    o_ref[...] = jnp.concatenate(outs, axis=0).reshape(o_ref.shape)


def partial_attend(got, other, rows_kv, rows_q):
    chips, _, width = got.shape
    heads = width // HEAD_DIM
    own_kv = got[:, : 2 * rows_kv].reshape(chips, 2, rows_kv, width)
    own_q = got[:, 2 * rows_kv :]
    other = other.reshape(chips, 2, rows_kv, width)

    def kv(which):
        return pl.BlockSpec((chips, None, rows_kv, HEAD_DIM), lambda h: (0, which, 0, h))

    q_spec = pl.BlockSpec((chips, rows_q, HEAD_DIM), lambda h: (0, 0, h))
    stat_spec = pl.BlockSpec((None, chips * rows_q, HEAD_DIM), lambda h: (h, 0, 0))
    stat = jax.ShapeDtypeStruct((heads, chips * rows_q, HEAD_DIM), F32)
    return pl.pallas_call(
        partial_head,
        grid=(heads,),
        in_specs=[q_spec, kv(0), kv(1), kv(0), kv(1)],
        out_specs=[q_spec, stat_spec, stat_spec],
        out_shape=[jax.ShapeDtypeStruct((chips, rows_q, width), F32), stat, stat],
        compiler_params=PARAMS,
    )(own_q, own_kv, own_kv, other, other)


def local_blocks(keys, values, queries):
    chips = lax.axis_size("chip")
    blocks = chips // GROUPS
    ctx_rows, width = keys.shape
    gw = width // GROUPS
    heads = gw // HEAD_DIM
    layers, tok_rows, _ = queries.shape
    rows_q = layers * tok_rows
    rows_kv = ctx_rows // blocks

    def by_chip(array):
        return jnp.swapaxes(array.reshape(rows_kv, chips, gw), 0, 1)

    q = jnp.swapaxes(queries.reshape(rows_q, GROUPS, gw), 0, 1)
    q = jnp.broadcast_to(q[None], (blocks, GROUPS, rows_q, gw)).reshape(chips, rows_q, gw)
    packed = jnp.concatenate([by_chip(keys), by_chip(values), q], axis=1)
    got = lax.all_to_all(packed, "chip", split_axis=0, concat_axis=0, tiled=True)
    other = lax.ppermute(got[:, : 2 * rows_kv], "core", [(0, 1), (1, 0)])
    outs = partial_attend(got, other, rows_kv, rows_q)
    stats = [jnp.moveaxis(s[:, :, 0].reshape(heads, chips, rows_q), 0, 2) for s in outs[1:]]
    stats = jnp.concatenate(stats, axis=2)
    stats = jnp.pad(stats, ((0, 0), (0, 0), (0, -2 * heads % HEAD_DIM)))
    sent = jnp.concatenate([outs[0], stats], axis=2)
    back = lax.all_to_all(sent, "chip", split_axis=0, concat_axis=0, tiled=True)
    back = back.reshape(blocks, GROUPS, rows_q, -1)
    summed = back[..., :gw].reshape(blocks, GROUPS, rows_q, heads, HEAD_DIM)
    peak = back[..., gw : gw + heads]
    total = back[..., gw + heads : gw + 2 * heads]
    share = jnp.exp2(peak - jnp.max(peak, axis=0))
    denom = jnp.sum(share * total, axis=0)
    numer = jnp.sum(share[..., None] * summed, axis=0)
    result = (numer / denom[..., None]).astype(BF16)
    return jnp.swapaxes(result.reshape(GROUPS, rows_q, gw), 0, 1).reshape(layers, tok_rows, width)


def solution(mesh):
    rep, seq = mesh.shape["rep"], mesh.shape["seq"]
    chips = seq // 2
    by_core = Mesh(mesh.devices.reshape(rep, chips, 2), ("rep", "chip", "core"))
    rows = ("rep", "chip", "core")
    return jax.shard_map(
        local_permutes if chips == GROUPS else local_blocks,
        mesh=by_core,
        in_specs=(P(rows, None), P(rows, None), P(None, rows, None)),
        out_specs=P(None, rows, None),
        check_vma=False,
    )
```

```python
import functools
import math

import jax
import jax.numpy as jnp
from jax import lax
from jax.experimental import pallas as pl
from jax.experimental.pallas import tpu as pltpu
from jax.sharding import Mesh, PartitionSpec as P

HEAD_DIM = 128
GROUPS = 8
SUB = 128
F32 = jnp.float32
BF16 = jnp.bfloat16
VMEM = pl.BlockSpec(memory_space=pltpu.VMEM)
HBM = pl.BlockSpec(memory_space=pltpu.HBM)
SMEM = pl.BlockSpec(memory_space=pltpu.SMEM)
FREE = pl.CostEstimate(flops=0, bytes_accessed=0, transcendentals=0)
PARAMS = pltpu.CompilerParams(vmem_limit_bytes=40 * 2**20)


def softmax_rows(q, ka, va, kb, vb):
    factor = math.log2(math.e) / math.sqrt(HEAD_DIM)
    nt = (((1,), (1,)), ((), ()))
    sa = lax.dot_general(q, ka, nt, preferred_element_type=F32)
    sb = lax.dot_general(q, kb, nt, preferred_element_type=F32)
    peak = jnp.max(jnp.maximum(sa, sb), axis=1, keepdims=True)
    ea = jnp.exp2((sa - peak) * factor).astype(BF16)
    eb = jnp.exp2((sb - peak) * factor).astype(BF16)
    both = jnp.dot(ea, va, preferred_element_type=F32) + jnp.dot(eb, vb, preferred_element_type=F32)
    return both[:, :HEAD_DIM], peak * factor, both[:, HEAD_DIM:]


def beside_ones(v):
    return jnp.concatenate([v, jnp.ones_like(v)], axis=1)


FIRST = (6, 2, 7)
REST = (1, 4, 5, 3, 0)
LAST = (6, 7)
NEAR = (2, 3, 1)


def pack_body(rows, gw, layout, chip_ref, *refs):
    arrays, out_refs, sems = refs[:3], refs[3:-1], refs[-1]
    copies = []
    for out_ref, (k, parts) in zip(out_refs, layout):
        col = pl.ds(pl.multiple_of((chip_ref[0] ^ k) * gw, HEAD_DIM), gw)
        for at, n in enumerate(parts):
            to = out_ref.at[at * rows : (at + 1) * rows]
            copies.append(pltpu.make_async_copy(arrays[n].at[:, col], to, sems.at[len(copies)]))
    for copy in copies:
        copy.start()
    for copy in copies:
        copy.wait()


def merge_body(rows, *refs):
    out_ref = refs[-1]
    for n, piece in enumerate(refs[:-1]):
        for which in range(2):
            out_ref[which, n * rows : (n + 1) * rows] = piece[which * rows : (which + 1) * rows]


def unpack_body(gw, order, chip_ref, *refs):
    out_ref = refs[-1]
    for k, piece_ref in zip(order, refs[:-1]):
        out_ref[:, pl.ds(pl.multiple_of((chip_ref[0] ^ k) * gw, HEAD_DIM), gw)] = piece_ref[...]


def attend_body(count, rows, own, other, *refs):
    queries, outs = refs[:count], refs[count:]
    for h in range(own.shape[2] // HEAD_DIM):
        col = slice(h * HEAD_DIM, (h + 1) * HEAD_DIM)
        q = jnp.concatenate([r[r.shape[0] - rows :, col] for r in queries], axis=0)
        va, vb = beside_ones(own[1, :, col]), beside_ones(other[1, :, col])
        acc, _, total = softmax_rows(q, own[0, :, col], va, other[0, :, col], vb)
        acc = (acc / total).astype(BF16)
        for n, out in enumerate(outs):
            out[:, col] = acc[n * rows : (n + 1) * rows]


def local_permutes(keys, values, queries):
    chips = lax.axis_size("chip")
    rows, width = keys.shape
    gw = width // chips
    layers, tok_rows, _ = queries.shape
    rows_q = layers * tok_rows
    assert rows_q == rows
    chip = lax.axis_index("chip").reshape(1).astype(jnp.int32)

    def across(piece, k):
        return lax.ppermute(piece, "chip", [(i, i ^ k) for i in range(chips)]) if k else piece

    def call(body, n_in, out_shape, smem=0, **more):
        return pl.pallas_call(
            body,
            in_specs=[SMEM] * smem + [VMEM] * n_in,
            out_specs=jax.tree.map(lambda _: VMEM, out_shape),
            out_shape=out_shape,
            compiler_params=PARAMS,
            cost_estimate=FREE,
            **more,
        )

    def shape(*dims):
        return jax.ShapeDtypeStruct(dims, BF16)

    sources = [keys, values, queries.reshape(rows_q, width)]
    sources = [pltpu.with_memory_space_constraint(a, pltpu.HBM) for a in sources]

    def pack(layout, after=()):
        arrays = lax.optimization_barrier((*sources, *after))[:3] if after else sources
        return pl.pallas_call(
            functools.partial(pack_body, rows, gw, layout),
            in_specs=[SMEM, HBM, HBM, HBM],
            out_specs=[VMEM] * len(layout),
            out_shape=[shape(len(parts) * rows, gw) for _, parts in layout],
            scratch_shapes=[pltpu.SemaphoreType.DMA((sum(len(parts) for _, parts in layout),))],
            compiler_params=PARAMS,
            cost_estimate=FREE,
        )(chip, *arrays)

    layout = [(k, (0, 1) if k in LAST else (0, 1, 2)) for k in FIRST + REST]
    layout += [(k, (2,)) for k in LAST]
    packed = pack(layout[: len(FIRST)])
    packed += pack(layout[len(FIRST) :], packed[:1])
    got = [across(piece, k) for piece, (k, _) in zip(packed, layout)]
    late = dict(zip(LAST, got[chips:]))
    got = {k: piece for piece, (k, _) in zip(got[:chips], layout)}
    own = call(functools.partial(merge_body, rows), chips, shape(2, chips * rows, gw))(*got.values())
    other = lax.ppermute(own, "core", [(0, 1), (1, 0)])

    def attend(ks, after=()):
        pieces = [late.get(k, got[k]) for k in ks]
        if after:
            pieces = lax.optimization_barrier((*pieces, *after))[: len(pieces)]
        body = functools.partial(attend_body, len(ks), rows)
        outs = call(body, 2 + len(ks), [shape(rows, gw)] * len(ks))(own, other, *pieces)
        return dict(zip(ks, outs))

    outs = attend((4, 5))
    outs |= attend(NEAR + (0,), (outs[4],))
    outs |= attend(LAST, (outs[0],))
    order = (4, 5) + LAST + NEAR + (0,)
    back = {k: across(outs[k], k) for k in (4, 5) + LAST + (0,)}
    for k, before in zip(NEAR, (5, 4, 4)):
        back[k] = across(lax.optimization_barrier((outs[k], outs[LAST[0]], back[before]))[0], k)
    body = functools.partial(unpack_body, gw, order)
    result = call(body, chips, shape(rows_q, width), smem=1)(chip, *[back[k] for k in order])
    return result.reshape(layers, tok_rows, width)


def partial_head(q_ref, ka_ref, va_ref, kb_ref, vb_ref, o_ref, peak_ref, total_ref):
    src, rows, _ = q_ref.shape
    q = q_ref[...].reshape(src * rows, HEAD_DIM)
    ka, va, kb, vb = (r[...].reshape(-1, HEAD_DIM) for r in (ka_ref, va_ref, kb_ref, vb_ref))
    kv = ka, beside_ones(va), kb, beside_ones(vb)
    outs = []
    for at in range(0, src * rows, SUB):
        acc, peak, total = softmax_rows(q[at : at + SUB], *kv)
        outs.append(acc)
        peak_ref[at : at + SUB] = jnp.broadcast_to(peak, (SUB, HEAD_DIM))
        total_ref[at : at + SUB] = total
    o_ref[...] = jnp.concatenate(outs, axis=0).reshape(o_ref.shape)


def partial_attend(got, other, rows_kv, rows_q):
    chips, _, width = got.shape
    heads = width // HEAD_DIM
    own_kv = got[:, : 2 * rows_kv].reshape(chips, 2, rows_kv, width)
    own_q = got[:, 2 * rows_kv :]
    other = other.reshape(chips, 2, rows_kv, width)

    def kv(which):
        return pl.BlockSpec((chips, None, rows_kv, HEAD_DIM), lambda h: (0, which, 0, h))

    q_spec = pl.BlockSpec((chips, rows_q, HEAD_DIM), lambda h: (0, 0, h))
    stat_spec = pl.BlockSpec((None, chips * rows_q, HEAD_DIM), lambda h: (h, 0, 0))
    stat = jax.ShapeDtypeStruct((heads, chips * rows_q, HEAD_DIM), F32)
    return pl.pallas_call(
        partial_head,
        grid=(heads,),
        in_specs=[q_spec, kv(0), kv(1), kv(0), kv(1)],
        out_specs=[q_spec, stat_spec, stat_spec],
        out_shape=[jax.ShapeDtypeStruct((chips, rows_q, width), F32), stat, stat],
        compiler_params=PARAMS,
    )(own_q, own_kv, own_kv, other, other)


def local_blocks(keys, values, queries):
    chips = lax.axis_size("chip")
    blocks = chips // GROUPS
    ctx_rows, width = keys.shape
    gw = width // GROUPS
    heads = gw // HEAD_DIM
    layers, tok_rows, _ = queries.shape
    rows_q = layers * tok_rows
    rows_kv = ctx_rows // blocks

    def by_chip(array):
        return jnp.swapaxes(array.reshape(rows_kv, chips, gw), 0, 1)

    q = jnp.swapaxes(queries.reshape(rows_q, GROUPS, gw), 0, 1)
    q = jnp.broadcast_to(q[None], (blocks, GROUPS, rows_q, gw)).reshape(chips, rows_q, gw)
    packed = jnp.concatenate([by_chip(keys), by_chip(values), q], axis=1)
    got = lax.all_to_all(packed, "chip", split_axis=0, concat_axis=0, tiled=True)
    other = lax.ppermute(got[:, : 2 * rows_kv], "core", [(0, 1), (1, 0)])
    outs = partial_attend(got, other, rows_kv, rows_q)
    stats = [jnp.moveaxis(s[:, :, 0].reshape(heads, chips, rows_q), 0, 2) for s in outs[1:]]
    stats = jnp.concatenate(stats, axis=2)
    stats = jnp.pad(stats, ((0, 0), (0, 0), (0, -2 * heads % HEAD_DIM)))
    sent = jnp.concatenate([outs[0], stats], axis=2)
    back = lax.all_to_all(sent, "chip", split_axis=0, concat_axis=0, tiled=True)
    back = back.reshape(blocks, GROUPS, rows_q, -1)
    summed = back[..., :gw].reshape(blocks, GROUPS, rows_q, heads, HEAD_DIM)
    peak = back[..., gw : gw + heads]
    total = back[..., gw + heads : gw + 2 * heads]
    share = jnp.exp2(peak - jnp.max(peak, axis=0))
    denom = jnp.sum(share * total, axis=0)
    numer = jnp.sum(share[..., None] * summed, axis=0)
    result = (numer / denom[..., None]).astype(BF16)
    return jnp.swapaxes(result.reshape(GROUPS, rows_q, gw), 0, 1).reshape(layers, tok_rows, width)


def solution(mesh):
    rep, seq = mesh.shape["rep"], mesh.shape["seq"]
    chips = seq // 2
    by_core = Mesh(mesh.devices.reshape(rep, chips, 2), ("rep", "chip", "core"))
    rows = ("rep", "chip", "core")
    return jax.shard_map(
        local_permutes if chips == GROUPS else local_blocks,
        mesh=by_core,
        in_specs=(P(rows, None), P(rows, None), P(None, rows, None)),
        out_specs=P(None, rows, None),
        check_vma=False,
    )
```

```python
import functools
import math

import jax
import jax.numpy as jnp
from jax import lax
from jax.experimental import pallas as pl
from jax.experimental.pallas import tpu as pltpu
from jax.sharding import Mesh, PartitionSpec as P

HEAD_DIM = 128
GROUPS = 8
SUB = 128
F32 = jnp.float32
BF16 = jnp.bfloat16
VMEM = pl.BlockSpec(memory_space=pltpu.VMEM)
HBM = pl.BlockSpec(memory_space=pltpu.HBM)
SMEM = pl.BlockSpec(memory_space=pltpu.SMEM)
FREE = pl.CostEstimate(flops=0, bytes_accessed=0, transcendentals=0)
PARAMS = pltpu.CompilerParams(vmem_limit_bytes=40 * 2**20)


def softmax_rows(q, ka, va, kb, vb):
    factor = math.log2(math.e) / math.sqrt(HEAD_DIM)
    nt = (((1,), (1,)), ((), ()))
    sa = lax.dot_general(q, ka, nt, preferred_element_type=F32)
    sb = lax.dot_general(q, kb, nt, preferred_element_type=F32)
    peak = jnp.max(jnp.maximum(sa, sb), axis=1, keepdims=True)
    ea = jnp.exp2((sa - peak) * factor).astype(BF16)
    eb = jnp.exp2((sb - peak) * factor).astype(BF16)
    both = jnp.dot(ea, va, preferred_element_type=F32) + jnp.dot(eb, vb, preferred_element_type=F32)
    return both[:, :HEAD_DIM], peak * factor, both[:, HEAD_DIM:]


def beside_ones(v):
    return jnp.concatenate([v, jnp.ones_like(v)], axis=1)


FIRST = (6, 2, 7)
REST = (4, 3, 1, 5, 0)
LAST = (6, 7)
NEAR = (2, 3, 1)


def pack_body(rows, gw, layout, chip_ref, *refs):
    arrays, out_refs, sems = refs[:3], refs[3:-1], refs[-1]
    copies = []
    for out_ref, (k, parts) in zip(out_refs, layout):
        col = pl.ds(pl.multiple_of((chip_ref[0] ^ k) * gw, HEAD_DIM), gw)
        for at, n in enumerate(parts):
            to = out_ref.at[at * rows : (at + 1) * rows]
            copies.append(pltpu.make_async_copy(arrays[n].at[:, col], to, sems.at[len(copies)]))
    for copy in copies:
        copy.start()
    for copy in copies:
        copy.wait()


def merge_body(rows, *refs):
    out_ref = refs[-1]
    for n, piece in enumerate(refs[:-1]):
        for which in range(2):
            out_ref[which, n * rows : (n + 1) * rows] = piece[which * rows : (which + 1) * rows]


def unpack_body(gw, order, chip_ref, *refs):
    pieces, out_ref, sems = refs[: len(order)], refs[-2], refs[-1]
    copies = []
    for n, k in enumerate(order):
        col = pl.ds(pl.multiple_of((chip_ref[0] ^ k) * gw, HEAD_DIM), gw)
        copies.append(pltpu.make_async_copy(pieces[n], out_ref.at[:, col], sems.at[n]))
    for copy in copies:
        copy.start()
    for copy in copies:
        copy.wait()


def attend_body(count, rows, own, other, *refs):
    queries, outs = refs[:count], refs[count:]
    for h in range(own.shape[2] // HEAD_DIM):
        col = slice(h * HEAD_DIM, (h + 1) * HEAD_DIM)
        q = jnp.concatenate([r[r.shape[0] - rows :, col] for r in queries], axis=0)
        va, vb = beside_ones(own[1, :, col]), beside_ones(other[1, :, col])
        acc, _, total = softmax_rows(q, own[0, :, col], va, other[0, :, col], vb)
        acc = (acc / total).astype(BF16)
        for n, out in enumerate(outs):
            out[:, col] = acc[n * rows : (n + 1) * rows]


def local_permutes(keys, values, queries):
    chips = lax.axis_size("chip")
    rows, width = keys.shape
    gw = width // chips
    layers, tok_rows, _ = queries.shape
    rows_q = layers * tok_rows
    assert rows_q == rows
    chip = lax.axis_index("chip").reshape(1).astype(jnp.int32)

    def across(piece, k):
        return lax.ppermute(piece, "chip", [(i, i ^ k) for i in range(chips)]) if k else piece

    def call(body, n_in, out_shape, smem=0, **more):
        return pl.pallas_call(
            body,
            in_specs=[SMEM] * smem + [VMEM] * n_in,
            out_specs=jax.tree.map(lambda _: VMEM, out_shape),
            out_shape=out_shape,
            compiler_params=PARAMS,
            cost_estimate=FREE,
            **more,
        )

    def shape(*dims):
        return jax.ShapeDtypeStruct(dims, BF16)

    sources = [keys, values, queries.reshape(rows_q, width)]
    sources = [pltpu.with_memory_space_constraint(a, pltpu.HBM) for a in sources]

    def pack(layout, after=()):
        arrays = lax.optimization_barrier((*sources, *after))[:3] if after else sources
        return pl.pallas_call(
            functools.partial(pack_body, rows, gw, layout),
            in_specs=[SMEM, HBM, HBM, HBM],
            out_specs=[VMEM] * len(layout),
            out_shape=[shape(len(parts) * rows, gw) for _, parts in layout],
            scratch_shapes=[pltpu.SemaphoreType.DMA((sum(len(parts) for _, parts in layout),))],
            compiler_params=PARAMS,
            cost_estimate=FREE,
        )(chip, *arrays)

    layout = [(k, (0, 1) if k in LAST else (0, 1, 2)) for k in FIRST + REST]
    layout += [(k, (2,)) for k in LAST]
    packed = pack(layout[: len(FIRST)])
    packed += pack(layout[len(FIRST) :], packed[:1])
    got = [across(piece, k) for piece, (k, _) in zip(packed, layout)]
    late = dict(zip(LAST, got[chips:]))
    got = {k: piece for piece, (k, _) in zip(got[:chips], layout)}
    own = call(functools.partial(merge_body, rows), chips, shape(2, chips * rows, gw))(*got.values())
    other = lax.ppermute(own, "core", [(0, 1), (1, 0)])

    def attend(ks, after=()):
        pieces = [late.get(k, got[k]) for k in ks]
        if after:
            pieces = lax.optimization_barrier((*pieces, *after))[: len(pieces)]
        body = functools.partial(attend_body, len(ks), rows)
        outs = call(body, 2 + len(ks), [shape(rows, gw)] * len(ks))(own, other, *pieces)
        return dict(zip(ks, outs))

    outs = attend((4, 5))
    outs |= attend(NEAR + (0,), (outs[4],))
    outs |= attend(LAST, (outs[0],))
    back = {k: across(outs[k], k) for k in (4, 5) + LAST + (0,)}
    back[2] = across(lax.optimization_barrier((outs[2], outs[LAST[0]]))[0], 2)
    for k, before in ((3, 5), (1, 4)):
        back[k] = across(lax.optimization_barrier((outs[k], outs[LAST[0]], back[before]))[0], k)

    def unpack(order, so_far=()):
        return pl.pallas_call(
            functools.partial(unpack_body, gw, order),
            in_specs=[SMEM] + [VMEM] * len(order) + [HBM] * len(so_far),
            out_specs=HBM,
            out_shape=shape(rows_q, width),
            scratch_shapes=[pltpu.SemaphoreType.DMA((len(order),))],
            input_output_aliases={1 + len(order): 0} if so_far else {},
            compiler_params=PARAMS,
            cost_estimate=FREE,
        )(chip, *[back[k] for k in order], *so_far)

    result = unpack(LAST + (3, 1), (unpack((0, 4, 5, 2)),))
    return result.reshape(layers, tok_rows, width)


def partial_head(q_ref, ka_ref, va_ref, kb_ref, vb_ref, o_ref, peak_ref, total_ref):
    src, rows, _ = q_ref.shape
    q = q_ref[...].reshape(src * rows, HEAD_DIM)
    ka, va, kb, vb = (r[...].reshape(-1, HEAD_DIM) for r in (ka_ref, va_ref, kb_ref, vb_ref))
    kv = ka, beside_ones(va), kb, beside_ones(vb)
    outs = []
    for at in range(0, src * rows, SUB):
        acc, peak, total = softmax_rows(q[at : at + SUB], *kv)
        outs.append(acc)
        peak_ref[at : at + SUB] = jnp.broadcast_to(peak, (SUB, HEAD_DIM))
        total_ref[at : at + SUB] = total
    o_ref[...] = jnp.concatenate(outs, axis=0).reshape(o_ref.shape)


def partial_attend(got, other, rows_kv, rows_q):
    chips, _, width = got.shape
    heads = width // HEAD_DIM
    own_kv = got[:, : 2 * rows_kv].reshape(chips, 2, rows_kv, width)
    own_q = got[:, 2 * rows_kv :]
    other = other.reshape(chips, 2, rows_kv, width)

    def kv(which):
        return pl.BlockSpec((chips, None, rows_kv, HEAD_DIM), lambda h: (0, which, 0, h))

    q_spec = pl.BlockSpec((chips, rows_q, HEAD_DIM), lambda h: (0, 0, h))
    stat_spec = pl.BlockSpec((None, chips * rows_q, HEAD_DIM), lambda h: (h, 0, 0))
    stat = jax.ShapeDtypeStruct((heads, chips * rows_q, HEAD_DIM), F32)
    return pl.pallas_call(
        partial_head,
        grid=(heads,),
        in_specs=[q_spec, kv(0), kv(1), kv(0), kv(1)],
        out_specs=[q_spec, stat_spec, stat_spec],
        out_shape=[jax.ShapeDtypeStruct((chips, rows_q, width), F32), stat, stat],
        compiler_params=PARAMS,
    )(own_q, own_kv, own_kv, other, other)


def local_blocks(keys, values, queries):
    chips = lax.axis_size("chip")
    blocks = chips // GROUPS
    ctx_rows, width = keys.shape
    gw = width // GROUPS
    heads = gw // HEAD_DIM
    layers, tok_rows, _ = queries.shape
    rows_q = layers * tok_rows
    rows_kv = ctx_rows // blocks

    def by_chip(array):
        return jnp.swapaxes(array.reshape(rows_kv, chips, gw), 0, 1)

    q = jnp.swapaxes(queries.reshape(rows_q, GROUPS, gw), 0, 1)
    q = jnp.broadcast_to(q[None], (blocks, GROUPS, rows_q, gw)).reshape(chips, rows_q, gw)
    packed = jnp.concatenate([by_chip(keys), by_chip(values), q], axis=1)
    got = lax.all_to_all(packed, "chip", split_axis=0, concat_axis=0, tiled=True)
    other = lax.ppermute(got[:, : 2 * rows_kv], "core", [(0, 1), (1, 0)])
    outs = partial_attend(got, other, rows_kv, rows_q)
    stats = [jnp.moveaxis(s[:, :, 0].reshape(heads, chips, rows_q), 0, 2) for s in outs[1:]]
    stats = jnp.concatenate(stats, axis=2)
    stats = jnp.pad(stats, ((0, 0), (0, 0), (0, -2 * heads % HEAD_DIM)))
    sent = jnp.concatenate([outs[0], stats], axis=2)
    back = lax.all_to_all(sent, "chip", split_axis=0, concat_axis=0, tiled=True)
    back = back.reshape(blocks, GROUPS, rows_q, -1)
    summed = back[..., :gw].reshape(blocks, GROUPS, rows_q, heads, HEAD_DIM)
    peak = back[..., gw : gw + heads]
    total = back[..., gw + heads : gw + 2 * heads]
    share = jnp.exp2(peak - jnp.max(peak, axis=0))
    denom = jnp.sum(share * total, axis=0)
    numer = jnp.sum(share[..., None] * summed, axis=0)
    result = (numer / denom[..., None]).astype(BF16)
    return jnp.swapaxes(result.reshape(GROUPS, rows_q, gw), 0, 1).reshape(layers, tok_rows, width)


def solution(mesh):
    rep, seq = mesh.shape["rep"], mesh.shape["seq"]
    chips = seq // 2
    by_core = Mesh(mesh.devices.reshape(rep, chips, 2), ("rep", "chip", "core"))
    rows = ("rep", "chip", "core")
    return jax.shard_map(
        local_permutes if chips == GROUPS else local_blocks,
        mesh=by_core,
        in_specs=(P(rows, None), P(rows, None), P(None, rows, None)),
        out_specs=P(None, rows, None),
        check_vma=False,
    )
```

```python
import functools
import math

import jax
import jax.numpy as jnp
from jax import lax
from jax.experimental import pallas as pl
from jax.experimental.pallas import tpu as pltpu
from jax.sharding import Mesh, PartitionSpec as P

HEAD_DIM = 128
GROUPS = 8
SUB = 128
F32 = jnp.float32
BF16 = jnp.bfloat16
VMEM = pl.BlockSpec(memory_space=pltpu.VMEM)
HBM = pl.BlockSpec(memory_space=pltpu.HBM)
SMEM = pl.BlockSpec(memory_space=pltpu.SMEM)
FREE = pl.CostEstimate(flops=0, bytes_accessed=0, transcendentals=0)
PARAMS = pltpu.CompilerParams(vmem_limit_bytes=40 * 2**20)


def softmax_rows(q, ka, va, kb, vb):
    factor = math.log2(math.e) / math.sqrt(HEAD_DIM)
    nt = (((1,), (1,)), ((), ()))
    sa = lax.dot_general(q, ka, nt, preferred_element_type=F32)
    sb = lax.dot_general(q, kb, nt, preferred_element_type=F32)
    peak = jnp.max(jnp.maximum(sa, sb), axis=1, keepdims=True)
    ea = jnp.exp2((sa - peak) * factor).astype(BF16)
    eb = jnp.exp2((sb - peak) * factor).astype(BF16)
    both = jnp.dot(ea, va, preferred_element_type=F32) + jnp.dot(eb, vb, preferred_element_type=F32)
    return both[:, :HEAD_DIM], peak * factor, both[:, HEAD_DIM:]


def beside_ones(v):
    return jnp.concatenate([v, jnp.ones_like(v)], axis=1)


FIRST = (6, 2, 7)
REST = (4, 3, 1, 5, 0)
LAST = (6, 7)
NEAR = (2, 3, 1)


def pack_body(rows, gw, layout, chip_ref, *refs):
    arrays, out_refs, sems = refs[:3], refs[3:-1], refs[-1]
    copies = []
    for out_ref, (k, parts) in zip(out_refs, layout):
        col = pl.ds(pl.multiple_of((chip_ref[0] ^ k) * gw, HEAD_DIM), gw)
        for at, n in enumerate(parts):
            to = out_ref.at[at * rows : (at + 1) * rows]
            copies.append(pltpu.make_async_copy(arrays[n].at[:, col], to, sems.at[len(copies)]))
    for copy in copies:
        copy.start()
    for copy in copies:
        copy.wait()


def merge_body(rows, *refs):
    out_ref = refs[-1]
    for n, piece in enumerate(refs[:-1]):
        for which in range(2):
            out_ref[which, n * rows : (n + 1) * rows] = piece[which * rows : (which + 1) * rows]


def unpack_body(gw, order, chip_ref, *refs):
    pieces, out_ref, sems = refs[: len(order)], refs[-2], refs[-1]
    copies = []
    for n, k in enumerate(order):
        col = pl.ds(pl.multiple_of((chip_ref[0] ^ k) * gw, HEAD_DIM), gw)
        copies.append(pltpu.make_async_copy(pieces[n], out_ref.at[:, col], sems.at[n]))
    for copy in copies:
        copy.start()
    for copy in copies:
        copy.wait()


def attend_body(count, rows, own, other, *refs):
    queries, outs = refs[:count], refs[count:]
    for h in range(own.shape[2] // HEAD_DIM):
        col = slice(h * HEAD_DIM, (h + 1) * HEAD_DIM)
        q = jnp.concatenate([r[r.shape[0] - rows :, col] for r in queries], axis=0)
        va, vb = beside_ones(own[1, :, col]), beside_ones(other[1, :, col])
        acc, _, total = softmax_rows(q, own[0, :, col], va, other[0, :, col], vb)
        acc = (acc / total).astype(BF16)
        for n, out in enumerate(outs):
            out[:, col] = acc[n * rows : (n + 1) * rows]


def local_permutes(keys, values, queries):
    chips = lax.axis_size("chip")
    rows, width = keys.shape
    gw = width // chips
    layers, tok_rows, _ = queries.shape
    rows_q = layers * tok_rows
    assert rows_q == rows
    chip = lax.axis_index("chip").reshape(1).astype(jnp.int32)

    def across(piece, k):
        return lax.ppermute(piece, "chip", [(i, i ^ k) for i in range(chips)]) if k else piece

    def call(body, n_in, out_shape, smem=0, **more):
        return pl.pallas_call(
            body,
            in_specs=[SMEM] * smem + [VMEM] * n_in,
            out_specs=jax.tree.map(lambda _: VMEM, out_shape),
            out_shape=out_shape,
            compiler_params=PARAMS,
            cost_estimate=FREE,
            **more,
        )

    def shape(*dims):
        return jax.ShapeDtypeStruct(dims, BF16)

    sources = [keys, values, queries.reshape(rows_q, width)]
    sources = [pltpu.with_memory_space_constraint(a, pltpu.HBM) for a in sources]

    def pack(layout, after=()):
        arrays = lax.optimization_barrier((*sources, *after))[:3] if after else sources
        return pl.pallas_call(
            functools.partial(pack_body, rows, gw, layout),
            in_specs=[SMEM, HBM, HBM, HBM],
            out_specs=[VMEM] * len(layout),
            out_shape=[shape(len(parts) * rows, gw) for _, parts in layout],
            scratch_shapes=[pltpu.SemaphoreType.DMA((sum(len(parts) for _, parts in layout),))],
            compiler_params=PARAMS,
            cost_estimate=FREE,
        )(chip, *arrays)

    layout = [(k, (0, 1) if k in LAST else (0, 1, 2)) for k in FIRST + REST]
    layout += [(k, (2,)) for k in LAST]
    packed = pack(layout[: len(FIRST)])
    packed += pack(layout[len(FIRST) :], packed[:1])
    got = [across(piece, k) for piece, (k, _) in zip(packed, layout)]
    late = dict(zip(LAST, got[chips:]))
    got = {k: piece for piece, (k, _) in zip(got[:chips], layout)}
    own = call(functools.partial(merge_body, rows), chips, shape(2, chips * rows, gw))(*got.values())
    other = lax.ppermute(own, "core", [(0, 1), (1, 0)])

    def attend(ks, after=()):
        pieces = [late.get(k, got[k]) for k in ks]
        if after:
            pieces = lax.optimization_barrier((*pieces, *after))[: len(pieces)]
        body = functools.partial(attend_body, len(ks), rows)
        outs = call(body, 2 + len(ks), [shape(rows, gw)] * len(ks))(own, other, *pieces)
        return dict(zip(ks, outs))

    outs = attend((4, 5))
    outs |= attend(NEAR + (0,), (outs[4],))
    outs |= attend(LAST, (outs[0],))
    def send(k, *after):
        return across(lax.optimization_barrier((outs[k], *after))[0], k)

    back = {k: across(outs[k], k) for k in NEAR + (0,)}
    back |= {k: send(k, outs[0]) for k in (4, 5)}
    back |= {7: send(7, back[2]), 6: send(6, back[3])}

    def unpack(order, so_far=()):
        return pl.pallas_call(
            functools.partial(unpack_body, gw, order),
            in_specs=[SMEM] + [VMEM] * len(order) + [HBM] * len(so_far),
            out_specs=HBM,
            out_shape=shape(rows_q, width),
            scratch_shapes=[pltpu.SemaphoreType.DMA((len(order),))],
            input_output_aliases={1 + len(order): 0} if so_far else {},
            compiler_params=PARAMS,
            cost_estimate=FREE,
        )(chip, *[back[k] for k in order], *so_far)

    result = unpack((4, 5) + LAST, (unpack((0,) + NEAR),))
    return result.reshape(layers, tok_rows, width)


def partial_head(q_ref, ka_ref, va_ref, kb_ref, vb_ref, o_ref, peak_ref, total_ref):
    src, rows, _ = q_ref.shape
    q = q_ref[...].reshape(src * rows, HEAD_DIM)
    ka, va, kb, vb = (r[...].reshape(-1, HEAD_DIM) for r in (ka_ref, va_ref, kb_ref, vb_ref))
    kv = ka, beside_ones(va), kb, beside_ones(vb)
    outs = []
    for at in range(0, src * rows, SUB):
        acc, peak, total = softmax_rows(q[at : at + SUB], *kv)
        outs.append(acc)
        peak_ref[at : at + SUB] = jnp.broadcast_to(peak, (SUB, HEAD_DIM))
        total_ref[at : at + SUB] = total
    o_ref[...] = jnp.concatenate(outs, axis=0).reshape(o_ref.shape)


def partial_attend(got, other, rows_kv, rows_q):
    chips, _, width = got.shape
    heads = width // HEAD_DIM
    own_kv = got[:, : 2 * rows_kv].reshape(chips, 2, rows_kv, width)
    own_q = got[:, 2 * rows_kv :]
    other = other.reshape(chips, 2, rows_kv, width)

    def kv(which):
        return pl.BlockSpec((chips, None, rows_kv, HEAD_DIM), lambda h: (0, which, 0, h))

    q_spec = pl.BlockSpec((chips, rows_q, HEAD_DIM), lambda h: (0, 0, h))
    stat_spec = pl.BlockSpec((None, chips * rows_q, HEAD_DIM), lambda h: (h, 0, 0))
    stat = jax.ShapeDtypeStruct((heads, chips * rows_q, HEAD_DIM), F32)
    return pl.pallas_call(
        partial_head,
        grid=(heads,),
        in_specs=[q_spec, kv(0), kv(1), kv(0), kv(1)],
        out_specs=[q_spec, stat_spec, stat_spec],
        out_shape=[jax.ShapeDtypeStruct((chips, rows_q, width), F32), stat, stat],
        compiler_params=PARAMS,
    )(own_q, own_kv, own_kv, other, other)


def local_blocks(keys, values, queries):
    chips = lax.axis_size("chip")
    blocks = chips // GROUPS
    ctx_rows, width = keys.shape
    gw = width // GROUPS
    heads = gw // HEAD_DIM
    layers, tok_rows, _ = queries.shape
    rows_q = layers * tok_rows
    rows_kv = ctx_rows // blocks

    def by_chip(array):
        return jnp.swapaxes(array.reshape(rows_kv, chips, gw), 0, 1)

    q = jnp.swapaxes(queries.reshape(rows_q, GROUPS, gw), 0, 1)
    q = jnp.broadcast_to(q[None], (blocks, GROUPS, rows_q, gw)).reshape(chips, rows_q, gw)
    packed = jnp.concatenate([by_chip(keys), by_chip(values), q], axis=1)
    got = lax.all_to_all(packed, "chip", split_axis=0, concat_axis=0, tiled=True)
    other = lax.ppermute(got[:, : 2 * rows_kv], "core", [(0, 1), (1, 0)])
    outs = partial_attend(got, other, rows_kv, rows_q)
    stats = [jnp.moveaxis(s[:, :, 0].reshape(heads, chips, rows_q), 0, 2) for s in outs[1:]]
    stats = jnp.concatenate(stats, axis=2)
    stats = jnp.pad(stats, ((0, 0), (0, 0), (0, -2 * heads % HEAD_DIM)))
    sent = jnp.concatenate([outs[0], stats], axis=2)
    back = lax.all_to_all(sent, "chip", split_axis=0, concat_axis=0, tiled=True)
    back = back.reshape(blocks, GROUPS, rows_q, -1)
    summed = back[..., :gw].reshape(blocks, GROUPS, rows_q, heads, HEAD_DIM)
    peak = back[..., gw : gw + heads]
    total = back[..., gw + heads : gw + 2 * heads]
    share = jnp.exp2(peak - jnp.max(peak, axis=0))
    denom = jnp.sum(share * total, axis=0)
    numer = jnp.sum(share[..., None] * summed, axis=0)
    result = (numer / denom[..., None]).astype(BF16)
    return jnp.swapaxes(result.reshape(GROUPS, rows_q, gw), 0, 1).reshape(layers, tok_rows, width)


def solution(mesh):
    rep, seq = mesh.shape["rep"], mesh.shape["seq"]
    chips = seq // 2
    by_core = Mesh(mesh.devices.reshape(rep, chips, 2), ("rep", "chip", "core"))
    rows = ("rep", "chip", "core")
    return jax.shard_map(
        local_permutes if chips == GROUPS else local_blocks,
        mesh=by_core,
        in_specs=(P(rows, None), P(rows, None), P(None, rows, None)),
        out_specs=P(None, rows, None),
        check_vma=False,
    )
```

```python
import functools
import math

import jax
import jax.numpy as jnp
from jax import lax
from jax.experimental import pallas as pl
from jax.experimental.pallas import tpu as pltpu
from jax.sharding import Mesh, PartitionSpec as P

HEAD_DIM = 128
GROUPS = 8
SUB = 128
F32 = jnp.float32
BF16 = jnp.bfloat16
VMEM = pl.BlockSpec(memory_space=pltpu.VMEM)
HBM = pl.BlockSpec(memory_space=pltpu.HBM)
SMEM = pl.BlockSpec(memory_space=pltpu.SMEM)
FREE = pl.CostEstimate(flops=0, bytes_accessed=0, transcendentals=0)
PARAMS = pltpu.CompilerParams(vmem_limit_bytes=40 * 2**20)


def softmax_rows(q, k, v):
    factor = math.log2(math.e) / math.sqrt(HEAD_DIM)
    scores = lax.dot_general(q, k, (((1,), (1,)), ((), ())), preferred_element_type=F32)
    peak = jnp.max(scores, axis=1, keepdims=True)
    expo = jnp.exp2((scores - peak) * factor).astype(BF16)
    both = jnp.dot(expo, v, preferred_element_type=F32)
    return both[:, :HEAD_DIM], peak * factor, both[:, HEAD_DIM:]


def beside_ones(v):
    return jnp.concatenate([v, jnp.ones_like(v)], axis=1)


FIRST = (6, 2, 7)
REST = (4, 3, 1, 5, 0)
FAR = (4, 5, 6, 7)


def pack_body(rows, gw, layout, chip_ref, *refs):
    arrays, out_refs, sems = refs[:3], refs[3:-1], refs[-1]
    copies = []
    for out_ref, (k, parts) in zip(out_refs, layout):
        col = pl.ds(pl.multiple_of((chip_ref[0] ^ k) * gw, HEAD_DIM), gw)
        for at, n in enumerate(parts):
            to = out_ref.at[at * rows : (at + 1) * rows]
            copies.append(pltpu.make_async_copy(arrays[n].at[:, col], to, sems.at[len(copies)]))
    for copy in copies:
        copy.start()
    for copy in copies:
        copy.wait()


def merge_body(rows, *refs):
    kv_ref = refs[-1]
    for n, piece in enumerate(refs[:-1]):
        for which in range(2):
            kv_ref[which, n * rows : (n + 1) * rows] = piece[which * rows : (which + 1) * rows]


def unpack_body(gw, order, chip_ref, *refs):
    pieces, out_ref, sems = refs[: len(order)], refs[-2], refs[-1]
    copies = []
    for n, k in enumerate(order):
        col = pl.ds(pl.multiple_of((chip_ref[0] ^ k) * gw, HEAD_DIM), gw)
        copies.append(pltpu.make_async_copy(pieces[n], out_ref.at[:, col], sems.at[n]))
    for copy in copies:
        copy.start()
    for copy in copies:
        copy.wait()


def attend_body(count, rows, kv, *refs):
    queries, outs = refs[:count], refs[count:]
    for h in range(kv.shape[2] // HEAD_DIM):
        col = slice(h * HEAD_DIM, (h + 1) * HEAD_DIM)
        k, v = kv[0, :, col], beside_ones(kv[1, :, col])
        for first in range(0, count, 4):
            some = range(first, min(first + 4, count))
            q = jnp.concatenate([queries[n][2 * rows :, col] for n in some], axis=0)
            acc, _, total = softmax_rows(q, k, v)
            acc = (acc / total).astype(BF16)
            for n in some:
                outs[n][:, col] = acc[(n - first) * rows : (n - first + 1) * rows]


def local_permutes(keys, values, queries):
    chips = lax.axis_size("chip")
    rows, width = keys.shape
    gw = width // chips
    layers, tok_rows, _ = queries.shape
    rows_q = layers * tok_rows
    assert rows_q == rows
    chip = lax.axis_index("chip").reshape(1).astype(jnp.int32)

    def across(piece, k):
        return lax.ppermute(piece, "chip", [(i, i ^ k) for i in range(chips)]) if k else piece

    def call(body, n_in, out_shape, smem=0, **more):
        return pl.pallas_call(
            body,
            in_specs=[SMEM] * smem + [VMEM] * n_in,
            out_specs=jax.tree.map(lambda _: VMEM, out_shape),
            out_shape=out_shape,
            compiler_params=PARAMS,
            cost_estimate=FREE,
            **more,
        )

    def shape(*dims):
        return jax.ShapeDtypeStruct(dims, BF16)

    sources = [keys, values, queries.reshape(rows_q, width)]
    sources = [pltpu.with_memory_space_constraint(a, pltpu.HBM) for a in sources]

    def pack(layout, after=()):
        arrays = lax.optimization_barrier((*sources, *after))[:3] if after else sources
        return pl.pallas_call(
            functools.partial(pack_body, rows, gw, layout),
            in_specs=[SMEM, HBM, HBM, HBM],
            out_specs=[VMEM] * len(layout),
            out_shape=[shape(len(parts) * rows, gw) for _, parts in layout],
            scratch_shapes=[pltpu.SemaphoreType.DMA((sum(len(parts) for _, parts in layout),))],
            compiler_params=PARAMS,
            cost_estimate=FREE,
        )(chip, *arrays)

    layout = [(k, (0, 1, 2)) for k in FIRST + REST]
    packed = pack(layout[: len(FIRST)])
    packed += pack(layout[len(FIRST) :], packed[:1])
    got = {k: across(piece, k) for piece, k in zip(packed, FIRST + REST)}
    swapped = [lax.ppermute(p[: 2 * rows], "core", [(0, 1), (1, 0)]) for p in got.values()]
    kv = call(functools.partial(merge_body, rows), 2 * chips, shape(2, 2 * chips * rows, gw))(*got.values(), *swapped)

    def attend(ks, *after):
        pieces = lax.optimization_barrier((*[got[k] for k in ks], *after))[: len(ks)]
        body = functools.partial(attend_body, len(ks), rows)
        outs = call(body, 1 + len(ks), [shape(rows, gw)] * len(ks))(kv, *pieces)
        return dict(zip(ks, outs))

    outs = attend((4, 5))
    outs |= attend((6, 7, 1, 3, 2, 0), outs[4])

    def send(k, *after):
        return across(lax.optimization_barrier((outs[k], *after))[0], k)

    back = {k: across(outs[k], k) for k in FAR + (0, 1)}
    back |= {3: send(3, back[5]), 2: send(2, back[4])}

    def unpack(order, so_far=()):
        return pl.pallas_call(
            functools.partial(unpack_body, gw, order),
            in_specs=[SMEM] + [VMEM] * len(order) + [HBM] * len(so_far),
            out_specs=HBM,
            out_shape=shape(rows_q, width),
            scratch_shapes=[pltpu.SemaphoreType.DMA((len(order),))],
            input_output_aliases={1 + len(order): 0} if so_far else {},
            compiler_params=PARAMS,
            cost_estimate=FREE,
        )(chip, *[back[k] for k in order], *so_far)

    result = unpack((6, 7, 3, 2), (unpack((0, 4, 5, 1)),))
    return result.reshape(layers, tok_rows, width)


def partial_head(q_ref, ka_ref, va_ref, kb_ref, vb_ref, o_ref, peak_ref, total_ref):
    src, rows, _ = q_ref.shape
    q = q_ref[...].reshape(src * rows, HEAD_DIM)
    ka, va, kb, vb = (r[...].reshape(-1, HEAD_DIM) for r in (ka_ref, va_ref, kb_ref, vb_ref))
    kv = jnp.concatenate([ka, kb]), beside_ones(jnp.concatenate([va, vb]))
    outs = []
    for at in range(0, src * rows, SUB):
        acc, peak, total = softmax_rows(q[at : at + SUB], *kv)
        outs.append(acc)
        peak_ref[at : at + SUB] = jnp.broadcast_to(peak, (SUB, HEAD_DIM))
        total_ref[at : at + SUB] = total
    o_ref[...] = jnp.concatenate(outs, axis=0).reshape(o_ref.shape)


def partial_attend(got, other, rows_kv, rows_q):
    chips, _, width = got.shape
    heads = width // HEAD_DIM
    own_kv = got[:, : 2 * rows_kv].reshape(chips, 2, rows_kv, width)
    own_q = got[:, 2 * rows_kv :]
    other = other.reshape(chips, 2, rows_kv, width)

    def kv(which):
        return pl.BlockSpec((chips, None, rows_kv, HEAD_DIM), lambda h: (0, which, 0, h))

    q_spec = pl.BlockSpec((chips, rows_q, HEAD_DIM), lambda h: (0, 0, h))
    stat_spec = pl.BlockSpec((None, chips * rows_q, HEAD_DIM), lambda h: (h, 0, 0))
    stat = jax.ShapeDtypeStruct((heads, chips * rows_q, HEAD_DIM), F32)
    return pl.pallas_call(
        partial_head,
        grid=(heads,),
        in_specs=[q_spec, kv(0), kv(1), kv(0), kv(1)],
        out_specs=[q_spec, stat_spec, stat_spec],
        out_shape=[jax.ShapeDtypeStruct((chips, rows_q, width), F32), stat, stat],
        compiler_params=PARAMS,
    )(own_q, own_kv, own_kv, other, other)


def local_blocks(keys, values, queries):
    chips = lax.axis_size("chip")
    blocks = chips // GROUPS
    ctx_rows, width = keys.shape
    gw = width // GROUPS
    heads = gw // HEAD_DIM
    layers, tok_rows, _ = queries.shape
    rows_q = layers * tok_rows
    rows_kv = ctx_rows // blocks

    def by_chip(array):
        return jnp.swapaxes(array.reshape(rows_kv, chips, gw), 0, 1)

    q = jnp.swapaxes(queries.reshape(rows_q, GROUPS, gw), 0, 1)
    q = jnp.broadcast_to(q[None], (blocks, GROUPS, rows_q, gw)).reshape(chips, rows_q, gw)
    packed = jnp.concatenate([by_chip(keys), by_chip(values), q], axis=1)
    got = lax.all_to_all(packed, "chip", split_axis=0, concat_axis=0, tiled=True)
    other = lax.ppermute(got[:, : 2 * rows_kv], "core", [(0, 1), (1, 0)])
    outs = partial_attend(got, other, rows_kv, rows_q)
    stats = [jnp.moveaxis(s[:, :, 0].reshape(heads, chips, rows_q), 0, 2) for s in outs[1:]]
    stats = jnp.concatenate(stats, axis=2)
    stats = jnp.pad(stats, ((0, 0), (0, 0), (0, -2 * heads % HEAD_DIM)))
    sent = jnp.concatenate([outs[0], stats], axis=2)
    back = lax.all_to_all(sent, "chip", split_axis=0, concat_axis=0, tiled=True)
    back = back.reshape(blocks, GROUPS, rows_q, -1)
    summed = back[..., :gw].reshape(blocks, GROUPS, rows_q, heads, HEAD_DIM)
    peak = back[..., gw : gw + heads]
    total = back[..., gw + heads : gw + 2 * heads]
    share = jnp.exp2(peak - jnp.max(peak, axis=0))
    denom = jnp.sum(share * total, axis=0)
    numer = jnp.sum(share[..., None] * summed, axis=0)
    result = (numer / denom[..., None]).astype(BF16)
    return jnp.swapaxes(result.reshape(GROUPS, rows_q, gw), 0, 1).reshape(layers, tok_rows, width)


def solution(mesh):
    rep, seq = mesh.shape["rep"], mesh.shape["seq"]
    chips = seq // 2
    by_core = Mesh(mesh.devices.reshape(rep, chips, 2), ("rep", "chip", "core"))
    rows = ("rep", "chip", "core")
    return jax.shard_map(
        local_permutes if chips == GROUPS else local_blocks,
        mesh=by_core,
        in_specs=(P(rows, None), P(rows, None), P(None, rows, None)),
        out_specs=P(None, rows, None),
        check_vma=False,
    )
```

```python
import functools
import math

import jax
import jax.numpy as jnp
from jax import lax
from jax.experimental import pallas as pl
from jax.experimental.pallas import tpu as pltpu
from jax.sharding import Mesh, PartitionSpec as P

HEAD_DIM = 128
GROUPS = 8
SUB = 128
F32 = jnp.float32
BF16 = jnp.bfloat16
VMEM = pl.BlockSpec(memory_space=pltpu.VMEM)
HBM = pl.BlockSpec(memory_space=pltpu.HBM)
SMEM = pl.BlockSpec(memory_space=pltpu.SMEM)
FREE = pl.CostEstimate(flops=0, bytes_accessed=0, transcendentals=0)
PARAMS = pltpu.CompilerParams(vmem_limit_bytes=40 * 2**20)


def softmax_rows(q, ka, va, kb, vb):
    factor = math.log2(math.e) / math.sqrt(HEAD_DIM)
    nt = (((1,), (1,)), ((), ()))
    sa = lax.dot_general(q, ka, nt, preferred_element_type=F32)
    sb = lax.dot_general(q, kb, nt, preferred_element_type=F32)
    peak = jnp.max(jnp.maximum(sa, sb), axis=1, keepdims=True)
    ea = jnp.exp2((sa - peak) * factor).astype(BF16)
    eb = jnp.exp2((sb - peak) * factor).astype(BF16)
    both = jnp.dot(ea, va, preferred_element_type=F32) + jnp.dot(eb, vb, preferred_element_type=F32)
    return both[:, :HEAD_DIM], peak * factor, both[:, HEAD_DIM:]


def beside_ones(v):
    return jnp.concatenate([v, jnp.ones_like(v)], axis=1)


FIRST = (6, 2, 7)
REST = (4, 3, 1, 5, 0)
LAST = (6, 7)
NEAR = (2, 3, 1)


def pack_body(rows, gw, layout, chip_ref, *refs):
    arrays, out_refs, sems = refs[:3], refs[3:-1], refs[-1]
    copies = []
    for out_ref, (k, parts) in zip(out_refs, layout):
        col = pl.ds(pl.multiple_of((chip_ref[0] ^ k) * gw, HEAD_DIM), gw)
        for at, n in enumerate(parts):
            to = out_ref.at[at * rows : (at + 1) * rows]
            copies.append(pltpu.make_async_copy(arrays[n].at[:, col], to, sems.at[len(copies)]))
    for copy in copies:
        copy.start()
    for copy in copies:
        copy.wait()


def merge_body(rows, *refs):
    out_ref = refs[-1]
    for n, piece in enumerate(refs[:-1]):
        for which in range(2):
            out_ref[which, n * rows : (n + 1) * rows] = piece[which * rows : (which + 1) * rows]


def unpack_body(gw, order, chip_ref, *refs):
    pieces, out_ref, sems = refs[: len(order)], refs[-2], refs[-1]
    copies = []
    for n, k in enumerate(order):
        col = pl.ds(pl.multiple_of((chip_ref[0] ^ k) * gw, HEAD_DIM), gw)
        copies.append(pltpu.make_async_copy(pieces[n], out_ref.at[:, col], sems.at[n]))
    for copy in copies:
        copy.start()
    for copy in copies:
        copy.wait()


def attend_body(count, rows, own, other, *refs):
    queries, outs = refs[:count], refs[count:]
    for h in range(own.shape[2] // HEAD_DIM):
        col = slice(h * HEAD_DIM, (h + 1) * HEAD_DIM)
        q = jnp.concatenate([r[r.shape[0] - rows :, col] for r in queries], axis=0)
        va, vb = beside_ones(own[1, :, col]), beside_ones(other[1, :, col])
        acc, _, total = softmax_rows(q, own[0, :, col], va, other[0, :, col], vb)
        acc = (acc / total).astype(BF16)
        for n, out in enumerate(outs):
            out[:, col] = acc[n * rows : (n + 1) * rows]


def local_permutes(keys, values, queries):
    chips = lax.axis_size("chip")
    rows, width = keys.shape
    gw = width // chips
    layers, tok_rows, _ = queries.shape
    rows_q = layers * tok_rows
    assert rows_q == rows
    chip = lax.axis_index("chip").reshape(1).astype(jnp.int32)

    def across(piece, k):
        return lax.ppermute(piece, "chip", [(i, i ^ k) for i in range(chips)]) if k else piece

    def call(body, n_in, out_shape, smem=0, **more):
        return pl.pallas_call(
            body,
            in_specs=[SMEM] * smem + [VMEM] * n_in,
            out_specs=jax.tree.map(lambda _: VMEM, out_shape),
            out_shape=out_shape,
            compiler_params=PARAMS,
            cost_estimate=FREE,
            **more,
        )

    def shape(*dims):
        return jax.ShapeDtypeStruct(dims, BF16)

    sources = [keys, values, queries.reshape(rows_q, width)]
    sources = [pltpu.with_memory_space_constraint(a, pltpu.HBM) for a in sources]

    def pack(layout, after=()):
        arrays = lax.optimization_barrier((*sources, *after))[:3] if after else sources
        return pl.pallas_call(
            functools.partial(pack_body, rows, gw, layout),
            in_specs=[SMEM, HBM, HBM, HBM],
            out_specs=[VMEM] * len(layout),
            out_shape=[shape(len(parts) * rows, gw) for _, parts in layout],
            scratch_shapes=[pltpu.SemaphoreType.DMA((sum(len(parts) for _, parts in layout),))],
            compiler_params=PARAMS,
            cost_estimate=FREE,
        )(chip, *arrays)

    layout = [(k, (0, 1) if k in LAST else (0, 1, 2)) for k in FIRST + REST]
    layout += [(k, (2,)) for k in LAST]
    packed = pack(layout[: len(FIRST)])
    packed += pack(layout[len(FIRST) :], packed[:1])
    got = [across(piece, k) for piece, (k, _) in zip(packed, layout)]
    late = dict(zip(LAST, got[chips:]))
    got = {k: piece for piece, (k, _) in zip(got[:chips], layout)}
    own = call(functools.partial(merge_body, rows), chips, shape(2, chips * rows, gw))(*got.values())
    other = lax.ppermute(own, "core", [(0, 1), (1, 0)])

    def attend(ks, after=()):
        pieces = [late.get(k, got[k]) for k in ks]
        if after:
            pieces = lax.optimization_barrier((*pieces, *after))[: len(pieces)]
        body = functools.partial(attend_body, len(ks), rows)
        outs = call(body, 2 + len(ks), [shape(rows, gw)] * len(ks))(own, other, *pieces)
        return dict(zip(ks, outs))

    outs = attend((4, 5))
    outs |= attend(LAST, (outs[4],))
    outs |= attend(NEAR + (0,), (outs[LAST[0]],))

    def send(k, *after):
        return across(lax.optimization_barrier((outs[k], *after))[0], k)

    back = {k: across(outs[k], k) for k in (0, 4, 5, 6)}
    back[7] = send(7, outs[0])
    back |= {k: send(k, outs[0], back[before]) for k, before in ((1, 5), (3, 4), (2, 4))}

    def unpack(order, so_far=()):
        return pl.pallas_call(
            functools.partial(unpack_body, gw, order),
            in_specs=[SMEM] + [VMEM] * len(order) + [HBM] * len(so_far),
            out_specs=HBM,
            out_shape=shape(rows_q, width),
            scratch_shapes=[pltpu.SemaphoreType.DMA((len(order),))],
            input_output_aliases={1 + len(order): 0} if so_far else {},
            compiler_params=PARAMS,
            cost_estimate=FREE,
        )(chip, *[back[k] for k in order], *so_far)

    result = unpack((7, 3, 2, 1), (unpack((0, 4, 5, 6)),))
    return result.reshape(layers, tok_rows, width)


def partial_head(q_ref, ka_ref, va_ref, kb_ref, vb_ref, o_ref, peak_ref, total_ref):
    src, rows, _ = q_ref.shape
    q = q_ref[...].reshape(src * rows, HEAD_DIM)
    ka, va, kb, vb = (r[...].reshape(-1, HEAD_DIM) for r in (ka_ref, va_ref, kb_ref, vb_ref))
    kv = ka, beside_ones(va), kb, beside_ones(vb)
    outs = []
    for at in range(0, src * rows, SUB):
        acc, peak, total = softmax_rows(q[at : at + SUB], *kv)
        outs.append(acc)
        peak_ref[at : at + SUB] = jnp.broadcast_to(peak, (SUB, HEAD_DIM))
        total_ref[at : at + SUB] = total
    o_ref[...] = jnp.concatenate(outs, axis=0).reshape(o_ref.shape)


def partial_attend(got, other, rows_kv, rows_q):
    chips, _, width = got.shape
    heads = width // HEAD_DIM
    own_kv = got[:, : 2 * rows_kv].reshape(chips, 2, rows_kv, width)
    own_q = got[:, 2 * rows_kv :]
    other = other.reshape(chips, 2, rows_kv, width)

    def kv(which):
        return pl.BlockSpec((chips, None, rows_kv, HEAD_DIM), lambda h: (0, which, 0, h))

    q_spec = pl.BlockSpec((chips, rows_q, HEAD_DIM), lambda h: (0, 0, h))
    stat_spec = pl.BlockSpec((None, chips * rows_q, HEAD_DIM), lambda h: (h, 0, 0))
    stat = jax.ShapeDtypeStruct((heads, chips * rows_q, HEAD_DIM), F32)
    return pl.pallas_call(
        partial_head,
        grid=(heads,),
        in_specs=[q_spec, kv(0), kv(1), kv(0), kv(1)],
        out_specs=[q_spec, stat_spec, stat_spec],
        out_shape=[jax.ShapeDtypeStruct((chips, rows_q, width), F32), stat, stat],
        compiler_params=PARAMS,
    )(own_q, own_kv, own_kv, other, other)


def local_blocks(keys, values, queries):
    chips = lax.axis_size("chip")
    blocks = chips // GROUPS
    ctx_rows, width = keys.shape
    gw = width // GROUPS
    heads = gw // HEAD_DIM
    layers, tok_rows, _ = queries.shape
    rows_q = layers * tok_rows
    rows_kv = ctx_rows // blocks

    def by_chip(array):
        return jnp.swapaxes(array.reshape(rows_kv, chips, gw), 0, 1)

    q = jnp.swapaxes(queries.reshape(rows_q, GROUPS, gw), 0, 1)
    q = jnp.broadcast_to(q[None], (blocks, GROUPS, rows_q, gw)).reshape(chips, rows_q, gw)
    packed = jnp.concatenate([by_chip(keys), by_chip(values), q], axis=1)
    got = lax.all_to_all(packed, "chip", split_axis=0, concat_axis=0, tiled=True)
    other = lax.ppermute(got[:, : 2 * rows_kv], "core", [(0, 1), (1, 0)])
    outs = partial_attend(got, other, rows_kv, rows_q)
    stats = [jnp.moveaxis(s[:, :, 0].reshape(heads, chips, rows_q), 0, 2) for s in outs[1:]]
    stats = jnp.concatenate(stats, axis=2)
    stats = jnp.pad(stats, ((0, 0), (0, 0), (0, -2 * heads % HEAD_DIM)))
    sent = jnp.concatenate([outs[0], stats], axis=2)
    back = lax.all_to_all(sent, "chip", split_axis=0, concat_axis=0, tiled=True)
    back = back.reshape(blocks, GROUPS, rows_q, -1)
    summed = back[..., :gw].reshape(blocks, GROUPS, rows_q, heads, HEAD_DIM)
    peak = back[..., gw : gw + heads]
    total = back[..., gw + heads : gw + 2 * heads]
    share = jnp.exp2(peak - jnp.max(peak, axis=0))
    denom = jnp.sum(share * total, axis=0)
    numer = jnp.sum(share[..., None] * summed, axis=0)
    result = (numer / denom[..., None]).astype(BF16)
    return jnp.swapaxes(result.reshape(GROUPS, rows_q, gw), 0, 1).reshape(layers, tok_rows, width)


def solution(mesh):
    rep, seq = mesh.shape["rep"], mesh.shape["seq"]
    chips = seq // 2
    by_core = Mesh(mesh.devices.reshape(rep, chips, 2), ("rep", "chip", "core"))
    rows = ("rep", "chip", "core")
    return jax.shard_map(
        local_permutes if chips == GROUPS else local_blocks,
        mesh=by_core,
        in_specs=(P(rows, None), P(rows, None), P(None, rows, None)),
        out_specs=P(None, rows, None),
        check_vma=False,
    )
```

```python
import functools
import math

import jax
import jax.numpy as jnp
from jax import lax
from jax.experimental import pallas as pl
from jax.experimental.pallas import tpu as pltpu
from jax.sharding import Mesh, PartitionSpec as P

HEAD_DIM = 128
GROUPS = 8
SUB = 128
F32 = jnp.float32
BF16 = jnp.bfloat16
VMEM = pl.BlockSpec(memory_space=pltpu.VMEM)
HBM = pl.BlockSpec(memory_space=pltpu.HBM)
SMEM = pl.BlockSpec(memory_space=pltpu.SMEM)
FREE = pl.CostEstimate(flops=0, bytes_accessed=0, transcendentals=0)
PARAMS = pltpu.CompilerParams(vmem_limit_bytes=40 * 2**20)


def softmax_rows(q, ka, va, kb, vb):
    factor = math.log2(math.e) / math.sqrt(HEAD_DIM)
    nt = (((1,), (1,)), ((), ()))
    sa = lax.dot_general(q, ka, nt, preferred_element_type=F32)
    sb = lax.dot_general(q, kb, nt, preferred_element_type=F32)
    peak = jnp.max(jnp.maximum(sa, sb), axis=1, keepdims=True)
    ea = jnp.exp2((sa - peak) * factor).astype(BF16)
    eb = jnp.exp2((sb - peak) * factor).astype(BF16)
    both = jnp.dot(ea, va, preferred_element_type=F32) + jnp.dot(eb, vb, preferred_element_type=F32)
    return both[:, :HEAD_DIM], peak * factor, both[:, HEAD_DIM:]


def beside_ones(v):
    return jnp.concatenate([v, jnp.ones_like(v)], axis=1)


LAST = 3
JOINED_BY = (0, 0)
UNPACK = (2,), (LAST, 1, 0)
FIRST = ((3, 0), (1, 0), (3, 1))
REST = ((2, 0), (1, 1), (0, 0), (2, 1), (0, 1))


def columns(at_ref, dz, cross, gw):
    group = at_ref[0] ^ (2 * dz + (at_ref[1] ^ cross))
    return pl.ds(pl.multiple_of(group * gw, HEAD_DIM), gw)


def pack_body(rows, gw, layout, at_ref, *refs):
    arrays, out_refs, sems = refs[:3], refs[3:-1], refs[-1]
    copies = []
    for out_ref, (piece, parts) in zip(out_refs, layout):
        col = columns(at_ref, *piece, gw)
        for at, n in enumerate(parts):
            to = out_ref.at[at * rows : (at + 1) * rows]
            copies.append(pltpu.make_async_copy(arrays[n].at[:, col], to, sems.at[len(copies)]))
    for copy in copies:
        copy.start()
    for copy in copies:
        copy.wait()


def merge_body(rows, *refs):
    out_ref = refs[-1]
    for n, piece in enumerate(refs[:-1]):
        for which in range(2):
            out_ref[which, n * rows : (n + 1) * rows] = piece[which * rows : (which + 1) * rows]


def unpack_body(gw, order, at_ref, *refs):
    pieces, out_ref, sems = refs[: len(order)], refs[-2], refs[-1]
    rows = out_ref.shape[0]
    copies = []
    for n, piece in enumerate(order):
        to = out_ref.at[:, columns(at_ref, *piece, gw)]
        copies.append(pltpu.make_async_copy(pieces[n].at[:rows], to, sems.at[n]))
    for copy in copies:
        copy.start()
    for copy in copies:
        copy.wait()


def attend_body(count, rows, own, other, *refs):
    queries, outs = refs[:count], refs[count:]
    for h in range(own.shape[2] // HEAD_DIM):
        col = slice(h * HEAD_DIM, (h + 1) * HEAD_DIM)
        q = [r[...][:, col] if r.shape[0] == 2 * rows else r[2 * rows :, col] for r in queries]
        va, vb = beside_ones(own[1, :, col]), beside_ones(other[1, :, col])
        acc, _, total = softmax_rows(jnp.concatenate(q, axis=0), own[0, :, col], va, other[0, :, col], vb)
        acc = (acc / total).astype(BF16)
        for n, out in enumerate(outs):
            out[:, col] = acc[n * 2 * rows : (n + 1) * 2 * rows]


def local_permutes(keys, values, queries):
    chips = lax.axis_size("chip")
    rows, width = keys.shape
    gw = width // chips
    layers, tok_rows, _ = queries.shape
    rows_q = layers * tok_rows
    assert rows_q == rows
    at = jnp.stack([lax.axis_index("chip"), lax.axis_index("core")]).astype(jnp.int32)

    def across(array, dz, cross):
        senders = [(chip, core) for chip in range(chips) for core in range(2)]
        to = [(chip ^ (2 * dz + (core ^ cross)), core ^ cross) for chip, core in senders]
        pairs = [(2 * a + b, 2 * c + d) for (a, b), (c, d) in zip(senders, to)]
        return lax.ppermute(array, ("chip", "core"), pairs)

    def swap(array):
        return lax.ppermute(array, "core", [(0, 1), (1, 0)])

    def after(array, *others):
        return lax.optimization_barrier((array, *others))[0]

    def call(body, n_in, out_shape):
        return pl.pallas_call(
            body,
            in_specs=[VMEM] * n_in,
            out_specs=jax.tree.map(lambda _: VMEM, out_shape),
            out_shape=out_shape,
            compiler_params=PARAMS,
            cost_estimate=FREE,
        )

    def shape(*dims):
        return jax.ShapeDtypeStruct(dims, BF16)

    sources = [keys, values, queries.reshape(rows_q, width)]
    sources = [pltpu.with_memory_space_constraint(a, pltpu.HBM) for a in sources]

    def pack(layout, *others):
        arrays = lax.optimization_barrier((*sources, *others))[:3]
        return pl.pallas_call(
            functools.partial(pack_body, rows, gw, layout),
            in_specs=[SMEM, HBM, HBM, HBM],
            out_specs=[VMEM] * len(layout),
            out_shape=[shape(len(parts) * rows, gw) for _, parts in layout],
            scratch_shapes=[pltpu.SemaphoreType.DMA((sum(len(parts) for _, parts in layout),))],
            compiler_params=PARAMS,
            cost_estimate=FREE,
        )(at, *arrays)

    layout = [(p, (0, 1) if p[0] == LAST else (0, 1, 2)) for p in FIRST + REST]
    layout += [((LAST, cross), (2,)) for cross in range(2)]
    packed = pack(layout[: len(FIRST)])
    packed += pack(layout[len(FIRST) :], packed[0])
    late = jnp.concatenate([packed[-2], swap(packed[-1])], axis=0)
    got = {}
    for p, piece in zip(FIRST + REST, packed):
        got[p] = across(after(piece, late) if p == JOINED_BY else piece, *p)
    own = call(functools.partial(merge_body, rows), chips, shape(2, chips * rows, gw))(*got.values())
    other = swap(own)
    late = across(late, LAST, 0)

    def attend(dzs, *others):
        pieces = [late] if dzs == (LAST,) else [got[dz, cross] for dz in dzs for cross in range(2)]
        count = len(pieces)
        pieces = lax.optimization_barrier((*pieces, *others))[:count] if others else pieces
        body = functools.partial(attend_body, count, rows)
        outs = call(body, 2 + count, [shape(2 * rows, gw)] * len(dzs))(own, other, *pieces)
        return dict(zip(dzs, outs))

    outs = attend((2,))
    outs |= attend((LAST,), outs[2])
    outs |= attend((1, 0), outs[LAST])
    back = {dz: across(outs[dz], dz, 0) for dz in (2, LAST)}
    back |= {dz: across(after(outs[dz], back[2]), dz, 0) for dz in (1, 0)}
    handed = {dz: swap(back[dz][rows:]) for dz in (2, 1, 0)}

    def unpack(dzs, *so_far):
        order = [(dz, cross) for dz in dzs for cross in range(2)]
        pieces = [handed[dz] if cross else back[dz] for dz, cross in order]
        return pl.pallas_call(
            functools.partial(unpack_body, gw, order),
            in_specs=[SMEM] + [VMEM] * len(order) + [HBM] * len(so_far),
            out_specs=HBM,
            out_shape=shape(rows_q, width),
            scratch_shapes=[pltpu.SemaphoreType.DMA((len(order),))],
            input_output_aliases={1 + len(order): 0} if so_far else {},
            compiler_params=PARAMS,
            cost_estimate=FREE,
        )(at, *pieces, *so_far)

    result = unpack(UNPACK[0])
    handed[LAST] = swap(after(back[LAST], result)[rows:])
    result = unpack(UNPACK[1], result)
    return result.reshape(layers, tok_rows, width)


def partial_head(q_ref, ka_ref, va_ref, kb_ref, vb_ref, o_ref, peak_ref, total_ref):
    src, rows, _ = q_ref.shape
    q = q_ref[...].reshape(src * rows, HEAD_DIM)
    ka, va, kb, vb = (r[...].reshape(-1, HEAD_DIM) for r in (ka_ref, va_ref, kb_ref, vb_ref))
    kv = ka, beside_ones(va), kb, beside_ones(vb)
    outs = []
    for at in range(0, src * rows, SUB):
        acc, peak, total = softmax_rows(q[at : at + SUB], *kv)
        outs.append(acc)
        peak_ref[at : at + SUB] = jnp.broadcast_to(peak, (SUB, HEAD_DIM))
        total_ref[at : at + SUB] = total
    o_ref[...] = jnp.concatenate(outs, axis=0).reshape(o_ref.shape)


def partial_attend(got, other, rows_kv, rows_q):
    chips, _, width = got.shape
    heads = width // HEAD_DIM
    own_kv = got[:, : 2 * rows_kv].reshape(chips, 2, rows_kv, width)
    own_q = got[:, 2 * rows_kv :]
    other = other.reshape(chips, 2, rows_kv, width)

    def kv(which):
        return pl.BlockSpec((chips, None, rows_kv, HEAD_DIM), lambda h: (0, which, 0, h))

    q_spec = pl.BlockSpec((chips, rows_q, HEAD_DIM), lambda h: (0, 0, h))
    stat_spec = pl.BlockSpec((None, chips * rows_q, HEAD_DIM), lambda h: (h, 0, 0))
    stat = jax.ShapeDtypeStruct((heads, chips * rows_q, HEAD_DIM), F32)
    return pl.pallas_call(
        partial_head,
        grid=(heads,),
        in_specs=[q_spec, kv(0), kv(1), kv(0), kv(1)],
        out_specs=[q_spec, stat_spec, stat_spec],
        out_shape=[jax.ShapeDtypeStruct((chips, rows_q, width), F32), stat, stat],
        compiler_params=PARAMS,
    )(own_q, own_kv, own_kv, other, other)


def local_blocks(keys, values, queries):
    chips = lax.axis_size("chip")
    blocks = chips // GROUPS
    ctx_rows, width = keys.shape
    gw = width // GROUPS
    heads = gw // HEAD_DIM
    layers, tok_rows, _ = queries.shape
    rows_q = layers * tok_rows
    rows_kv = ctx_rows // blocks

    def by_chip(array):
        return jnp.swapaxes(array.reshape(rows_kv, chips, gw), 0, 1)

    q = jnp.swapaxes(queries.reshape(rows_q, GROUPS, gw), 0, 1)
    q = jnp.broadcast_to(q[None], (blocks, GROUPS, rows_q, gw)).reshape(chips, rows_q, gw)
    packed = jnp.concatenate([by_chip(keys), by_chip(values), q], axis=1)
    got = lax.all_to_all(packed, "chip", split_axis=0, concat_axis=0, tiled=True)
    other = lax.ppermute(got[:, : 2 * rows_kv], "core", [(0, 1), (1, 0)])
    outs = partial_attend(got, other, rows_kv, rows_q)
    stats = [jnp.moveaxis(s[:, :, 0].reshape(heads, chips, rows_q), 0, 2) for s in outs[1:]]
    stats = jnp.concatenate(stats, axis=2)
    stats = jnp.pad(stats, ((0, 0), (0, 0), (0, -2 * heads % HEAD_DIM)))
    sent = jnp.concatenate([outs[0], stats], axis=2)
    back = lax.all_to_all(sent, "chip", split_axis=0, concat_axis=0, tiled=True)
    back = back.reshape(blocks, GROUPS, rows_q, -1)
    summed = back[..., :gw].reshape(blocks, GROUPS, rows_q, heads, HEAD_DIM)
    peak = back[..., gw : gw + heads]
    total = back[..., gw + heads : gw + 2 * heads]
    share = jnp.exp2(peak - jnp.max(peak, axis=0))
    denom = jnp.sum(share * total, axis=0)
    numer = jnp.sum(share[..., None] * summed, axis=0)
    result = (numer / denom[..., None]).astype(BF16)
    return jnp.swapaxes(result.reshape(GROUPS, rows_q, gw), 0, 1).reshape(layers, tok_rows, width)


def solution(mesh):
    rep, seq = mesh.shape["rep"], mesh.shape["seq"]
    chips = seq // 2
    by_core = Mesh(mesh.devices.reshape(rep, chips, 2), ("rep", "chip", "core"))
    rows = ("rep", "chip", "core")
    return jax.shard_map(
        local_permutes if chips == GROUPS else local_blocks,
        mesh=by_core,
        in_specs=(P(rows, None), P(rows, None), P(None, rows, None)),
        out_specs=P(None, rows, None),
        check_vma=False,
    )
```

```python
import functools
import math

import jax
import jax.numpy as jnp
from jax import lax
from jax.experimental import pallas as pl
from jax.experimental.pallas import tpu as pltpu
from jax.sharding import Mesh, PartitionSpec as P

HEAD_DIM = 128
GROUPS = 8
SUB = 128
F32 = jnp.float32
BF16 = jnp.bfloat16
VMEM = pl.BlockSpec(memory_space=pltpu.VMEM)
HBM = pl.BlockSpec(memory_space=pltpu.HBM)
SMEM = pl.BlockSpec(memory_space=pltpu.SMEM)
FREE = pl.CostEstimate(flops=0, bytes_accessed=0, transcendentals=0)
PARAMS = pltpu.CompilerParams(vmem_limit_bytes=40 * 2**20)


def softmax_rows(q, ka, va, kb, vb):
    factor = math.log2(math.e) / math.sqrt(HEAD_DIM)
    nt = (((1,), (1,)), ((), ()))
    sa = lax.dot_general(q, ka, nt, preferred_element_type=F32)
    sb = lax.dot_general(q, kb, nt, preferred_element_type=F32)
    peak = jnp.max(jnp.maximum(sa, sb), axis=1, keepdims=True)
    ea = jnp.exp2((sa - peak) * factor).astype(BF16)
    eb = jnp.exp2((sb - peak) * factor).astype(BF16)
    both = jnp.dot(ea, va, preferred_element_type=F32) + jnp.dot(eb, vb, preferred_element_type=F32)
    return both[:, :HEAD_DIM], peak * factor, both[:, HEAD_DIM:]


def beside_ones(v):
    return jnp.concatenate([v, jnp.ones_like(v)], axis=1)


FIRST = (4, 2, 5)
REST = (6, 3, 1, 7, 0)
LAST = (4, 5)
NEAR = (2, 3, 1)


def pack_body(rows, gw, layout, chip_ref, *refs):
    arrays, out_refs, sems = refs[:3], refs[3:-1], refs[-1]
    copies = []
    for out_ref, (k, parts) in zip(out_refs, layout):
        col = pl.ds(pl.multiple_of((chip_ref[0] ^ k) * gw, HEAD_DIM), gw)
        for at, n in enumerate(parts):
            to = out_ref.at[at * rows : (at + 1) * rows]
            copies.append(pltpu.make_async_copy(arrays[n].at[:, col], to, sems.at[len(copies)]))
    for copy in copies:
        copy.start()
    for copy in copies:
        copy.wait()


def merge_body(rows, *refs):
    out_ref = refs[-1]
    for n, piece in enumerate(refs[:-1]):
        for which in range(2):
            out_ref[which, n * rows : (n + 1) * rows] = piece[which * rows : (which + 1) * rows]


def unpack_body(gw, order, chip_ref, *refs):
    pieces, out_ref, sems = refs[: len(order)], refs[-2], refs[-1]
    copies = []
    for n, k in enumerate(order):
        col = pl.ds(pl.multiple_of((chip_ref[0] ^ k) * gw, HEAD_DIM), gw)
        copies.append(pltpu.make_async_copy(pieces[n], out_ref.at[:, col], sems.at[n]))
    for copy in copies:
        copy.start()
    for copy in copies:
        copy.wait()


def attend_body(count, rows, own, other, *refs):
    queries, outs = refs[:count], refs[count:]
    for h in range(own.shape[2] // HEAD_DIM):
        col = slice(h * HEAD_DIM, (h + 1) * HEAD_DIM)
        q = jnp.concatenate([r[r.shape[0] - rows :, col] for r in queries], axis=0)
        va, vb = beside_ones(own[1, :, col]), beside_ones(other[1, :, col])
        acc, _, total = softmax_rows(q, own[0, :, col], va, other[0, :, col], vb)
        acc = (acc / total).astype(BF16)
        for n, out in enumerate(outs):
            out[:, col] = acc[n * rows : (n + 1) * rows]


def local_permutes(keys, values, queries):
    chips = lax.axis_size("chip")
    rows, width = keys.shape
    gw = width // chips
    layers, tok_rows, _ = queries.shape
    rows_q = layers * tok_rows
    assert rows_q == rows
    chip = lax.axis_index("chip").reshape(1).astype(jnp.int32)

    def across(piece, k):
        return lax.ppermute(piece, "chip", [(i, i ^ k) for i in range(chips)]) if k else piece

    def call(body, n_in, out_shape, smem=0, **more):
        return pl.pallas_call(
            body,
            in_specs=[SMEM] * smem + [VMEM] * n_in,
            out_specs=jax.tree.map(lambda _: VMEM, out_shape),
            out_shape=out_shape,
            compiler_params=PARAMS,
            cost_estimate=FREE,
            **more,
        )

    def shape(*dims):
        return jax.ShapeDtypeStruct(dims, BF16)

    sources = [keys, values, queries.reshape(rows_q, width)]
    sources = [pltpu.with_memory_space_constraint(a, pltpu.HBM) for a in sources]

    def pack(layout, after=()):
        arrays = lax.optimization_barrier((*sources, *after))[:3] if after else sources
        return pl.pallas_call(
            functools.partial(pack_body, rows, gw, layout),
            in_specs=[SMEM, HBM, HBM, HBM],
            out_specs=[VMEM] * len(layout),
            out_shape=[shape(len(parts) * rows, gw) for _, parts in layout],
            scratch_shapes=[pltpu.SemaphoreType.DMA((sum(len(parts) for _, parts in layout),))],
            compiler_params=PARAMS,
            cost_estimate=FREE,
        )(chip, *arrays)

    layout = [(k, (0, 1) if k in LAST else (0, 1, 2)) for k in FIRST + REST]
    layout += [(k, (2,)) for k in LAST]
    packed = pack(layout[: len(FIRST)])
    packed += pack(layout[len(FIRST) :], packed[:1])
    got = [across(piece, k) for piece, (k, _) in zip(packed, layout)]
    late = dict(zip(LAST, got[chips:]))
    got = {k: piece for piece, (k, _) in zip(got[:chips], layout)}
    own = call(functools.partial(merge_body, rows), chips, shape(2, chips * rows, gw))(*got.values())
    other = lax.ppermute(own, "core", [(0, 1), (1, 0)])

    def attend(ks, after=()):
        pieces = [late.get(k, got[k]) for k in ks]
        if after:
            pieces = lax.optimization_barrier((*pieces, *after))[: len(pieces)]
        body = functools.partial(attend_body, len(ks), rows)
        outs = call(body, 2 + len(ks), [shape(rows, gw)] * len(ks))(own, other, *pieces)
        return dict(zip(ks, outs))

    outs = attend((6, 7))
    outs |= attend(NEAR + (0,), (outs[6],))
    outs |= attend(LAST, (outs[0],))

    def send(k, *after):
        return across(lax.optimization_barrier((outs[k], *after))[0], k)

    back = {k: across(outs[k], k) for k in (0, 6, 7) + LAST}
    back[1] = send(1, outs[LAST[0]])
    back |= {k: send(k, outs[LAST[0]], back[before]) for k, before in ((3, 7), (2, 6))}

    def unpack(order, so_far=()):
        return pl.pallas_call(
            functools.partial(unpack_body, gw, order),
            in_specs=[SMEM] + [VMEM] * len(order) + [HBM] * len(so_far),
            out_specs=HBM,
            out_shape=shape(rows_q, width),
            scratch_shapes=[pltpu.SemaphoreType.DMA((len(order),))],
            input_output_aliases={1 + len(order): 0} if so_far else {},
            compiler_params=PARAMS,
            cost_estimate=FREE,
        )(chip, *[back[k] for k in order], *so_far)

    result = unpack(LAST + (3, 2), (unpack((0, 6, 7, 1)),))
    return result.reshape(layers, tok_rows, width)


def partial_head(q_ref, ka_ref, va_ref, kb_ref, vb_ref, o_ref, peak_ref, total_ref):
    src, rows, _ = q_ref.shape
    q = q_ref[...].reshape(src * rows, HEAD_DIM)
    ka, va, kb, vb = (r[...].reshape(-1, HEAD_DIM) for r in (ka_ref, va_ref, kb_ref, vb_ref))
    kv = ka, beside_ones(va), kb, beside_ones(vb)
    outs = []
    for at in range(0, src * rows, SUB):
        acc, peak, total = softmax_rows(q[at : at + SUB], *kv)
        outs.append(acc)
        peak_ref[at : at + SUB] = jnp.broadcast_to(peak, (SUB, HEAD_DIM))
        total_ref[at : at + SUB] = total
    o_ref[...] = jnp.concatenate(outs, axis=0).reshape(o_ref.shape)


def partial_attend(got, other, rows_kv, rows_q):
    chips, _, width = got.shape
    heads = width // HEAD_DIM
    own_kv = got[:, : 2 * rows_kv].reshape(chips, 2, rows_kv, width)
    own_q = got[:, 2 * rows_kv :]
    other = other.reshape(chips, 2, rows_kv, width)

    def kv(which):
        return pl.BlockSpec((chips, None, rows_kv, HEAD_DIM), lambda h: (0, which, 0, h))

    q_spec = pl.BlockSpec((chips, rows_q, HEAD_DIM), lambda h: (0, 0, h))
    stat_spec = pl.BlockSpec((None, chips * rows_q, HEAD_DIM), lambda h: (h, 0, 0))
    stat = jax.ShapeDtypeStruct((heads, chips * rows_q, HEAD_DIM), F32)
    return pl.pallas_call(
        partial_head,
        grid=(heads,),
        in_specs=[q_spec, kv(0), kv(1), kv(0), kv(1)],
        out_specs=[q_spec, stat_spec, stat_spec],
        out_shape=[jax.ShapeDtypeStruct((chips, rows_q, width), F32), stat, stat],
        compiler_params=PARAMS,
    )(own_q, own_kv, own_kv, other, other)


def local_blocks(keys, values, queries):
    chips = lax.axis_size("chip")
    blocks = chips // GROUPS
    ctx_rows, width = keys.shape
    gw = width // GROUPS
    heads = gw // HEAD_DIM
    layers, tok_rows, _ = queries.shape
    rows_q = layers * tok_rows
    rows_kv = ctx_rows // blocks

    def by_chip(array):
        return jnp.swapaxes(array.reshape(rows_kv, chips, gw), 0, 1)

    q = jnp.swapaxes(queries.reshape(rows_q, GROUPS, gw), 0, 1)
    q = jnp.broadcast_to(q[None], (blocks, GROUPS, rows_q, gw)).reshape(chips, rows_q, gw)
    packed = jnp.concatenate([by_chip(keys), by_chip(values), q], axis=1)
    got = lax.all_to_all(packed, "chip", split_axis=0, concat_axis=0, tiled=True)
    other = lax.ppermute(got[:, : 2 * rows_kv], "core", [(0, 1), (1, 0)])
    outs = partial_attend(got, other, rows_kv, rows_q)
    stats = [jnp.moveaxis(s[:, :, 0].reshape(heads, chips, rows_q), 0, 2) for s in outs[1:]]
    stats = jnp.concatenate(stats, axis=2)
    stats = jnp.pad(stats, ((0, 0), (0, 0), (0, -2 * heads % HEAD_DIM)))
    sent = jnp.concatenate([outs[0], stats], axis=2)
    back = lax.all_to_all(sent, "chip", split_axis=0, concat_axis=0, tiled=True)
    back = back.reshape(blocks, GROUPS, rows_q, -1)
    summed = back[..., :gw].reshape(blocks, GROUPS, rows_q, heads, HEAD_DIM)
    peak = back[..., gw : gw + heads]
    total = back[..., gw + heads : gw + 2 * heads]
    share = jnp.exp2(peak - jnp.max(peak, axis=0))
    denom = jnp.sum(share * total, axis=0)
    numer = jnp.sum(share[..., None] * summed, axis=0)
    result = (numer / denom[..., None]).astype(BF16)
    return jnp.swapaxes(result.reshape(GROUPS, rows_q, gw), 0, 1).reshape(layers, tok_rows, width)


def solution(mesh):
    rep, seq = mesh.shape["rep"], mesh.shape["seq"]
    chips = seq // 2
    by_core = Mesh(mesh.devices.reshape(rep, chips, 2), ("rep", "chip", "core"))
    rows = ("rep", "chip", "core")
    return jax.shard_map(
        local_permutes if chips == GROUPS else local_blocks,
        mesh=by_core,
        in_specs=(P(rows, None), P(rows, None), P(None, rows, None)),
        out_specs=P(None, rows, None),
        check_vma=False,
    )
```

```python
import functools
import math

import jax
import jax.numpy as jnp
from jax import lax
from jax.experimental import pallas as pl
from jax.experimental.pallas import tpu as pltpu
from jax.sharding import Mesh, PartitionSpec as P

HEAD_DIM = 128
GROUPS = 8
SUB = 128
F32 = jnp.float32
BF16 = jnp.bfloat16
VMEM = pl.BlockSpec(memory_space=pltpu.VMEM)
HBM = pl.BlockSpec(memory_space=pltpu.HBM)
SMEM = pl.BlockSpec(memory_space=pltpu.SMEM)
FREE = pl.CostEstimate(flops=0, bytes_accessed=0, transcendentals=0)
PARAMS = pltpu.CompilerParams(vmem_limit_bytes=40 * 2**20)


def softmax_rows(q, ka, va, kb, vb):
    factor = math.log2(math.e) / math.sqrt(HEAD_DIM)
    nt = (((1,), (1,)), ((), ()))
    sa = lax.dot_general(q, ka, nt, preferred_element_type=F32)
    sb = lax.dot_general(q, kb, nt, preferred_element_type=F32)
    peak = jnp.max(jnp.maximum(sa, sb), axis=1, keepdims=True)
    ea = jnp.exp2((sa - peak) * factor).astype(BF16)
    eb = jnp.exp2((sb - peak) * factor).astype(BF16)
    both = jnp.dot(ea, va, preferred_element_type=F32) + jnp.dot(eb, vb, preferred_element_type=F32)
    return both[:, :HEAD_DIM], peak * factor, both[:, HEAD_DIM:]


def beside_ones(v):
    return jnp.concatenate([v, jnp.ones_like(v)], axis=1)


LAST = 3
JOINED_BY = (0, 0)
FIRST = ((3, 0), (1, 0), (3, 1))
REST = ((2, 0), (1, 1), (0, 0), (2, 1), (0, 1))


def columns(at, dz, cross, gw):
    group = at[0][0] ^ (2 * dz + (at[1][0] ^ cross))
    return pl.ds(pl.multiple_of(group * gw, HEAD_DIM), gw)


def pack_body(rows, gw, layout, chip_ref, core_ref, *refs):
    at = chip_ref, core_ref
    arrays, out_refs, sems = refs[:3], refs[3:-1], refs[-1]
    copies = []
    for out_ref, (piece, parts) in zip(out_refs, layout):
        col = columns(at, *piece, gw)
        for first, n in enumerate(parts):
            to = out_ref.at[first * rows : (first + 1) * rows]
            copies.append(pltpu.make_async_copy(arrays[n].at[:, col], to, sems.at[len(copies)]))
    for copy in copies:
        copy.start()
    for copy in copies:
        copy.wait()


def merge_body(rows, *refs):
    out_ref = refs[-1]
    for n, piece in enumerate(refs[:-1]):
        for which in range(2):
            out_ref[which, n * rows : (n + 1) * rows] = piece[which * rows : (which + 1) * rows]


def unpack_body(gw, order, chip_ref, core_ref, *refs):
    at = chip_ref, core_ref
    pieces, out_ref, sems = refs[: len(order)], refs[-2], refs[-1]
    rows = out_ref.shape[0]
    copies = []
    for n, piece in enumerate(order):
        to = out_ref.at[:, columns(at, *piece, gw)]
        copies.append(pltpu.make_async_copy(pieces[n].at[:rows], to, sems.at[n]))
    for copy in copies:
        copy.start()
    for copy in copies:
        copy.wait()


def attend_body(count, rows, own, other, *refs):
    queries, outs = refs[:count], refs[count:]
    for h in range(own.shape[2] // HEAD_DIM):
        col = slice(h * HEAD_DIM, (h + 1) * HEAD_DIM)
        q = [r[...][:, col] if r.shape[0] == 2 * rows else r[2 * rows :, col] for r in queries]
        va, vb = beside_ones(own[1, :, col]), beside_ones(other[1, :, col])
        acc, _, total = softmax_rows(jnp.concatenate(q, axis=0), own[0, :, col], va, other[0, :, col], vb)
        acc = (acc / total).astype(BF16)
        for n, out in enumerate(outs):
            out[:, col] = acc[n * 2 * rows : (n + 1) * 2 * rows]


def local_permutes(keys, values, queries):
    chips = lax.axis_size("chip")
    rows, width = keys.shape
    gw = width // chips
    layers, tok_rows, _ = queries.shape
    rows_q = layers * tok_rows
    assert rows_q == rows
    at = [lax.axis_index(name).reshape(1).astype(jnp.int32) for name in ("chip", "core")]

    def across(array, dz, cross):
        senders = [(chip, core) for chip in range(chips) for core in range(2)]
        to = [(chip ^ (2 * dz + (core ^ cross)), core ^ cross) for chip, core in senders]
        pairs = [(2 * a + b, 2 * c + d) for (a, b), (c, d) in zip(senders, to)]
        return lax.ppermute(array, ("chip", "core"), pairs)

    def swap(array):
        return lax.ppermute(array, "core", [(0, 1), (1, 0)])

    def after(array, *others):
        return lax.optimization_barrier((array, *others))[0]

    def call(body, n_in, out_shape):
        return pl.pallas_call(
            body,
            in_specs=[VMEM] * n_in,
            out_specs=jax.tree.map(lambda _: VMEM, out_shape),
            out_shape=out_shape,
            compiler_params=PARAMS,
            cost_estimate=FREE,
        )

    def shape(*dims):
        return jax.ShapeDtypeStruct(dims, BF16)

    sources = [keys, values, queries.reshape(rows_q, width)]
    sources = [pltpu.with_memory_space_constraint(a, pltpu.HBM) for a in sources]

    def pack(layout, *others):
        arrays = lax.optimization_barrier((*sources, *others))[:3] if others else sources
        return pl.pallas_call(
            functools.partial(pack_body, rows, gw, layout),
            in_specs=[SMEM, SMEM, HBM, HBM, HBM],
            out_specs=[VMEM] * len(layout),
            out_shape=[shape(len(parts) * rows, gw) for _, parts in layout],
            scratch_shapes=[pltpu.SemaphoreType.DMA((sum(len(parts) for _, parts in layout),))],
            compiler_params=PARAMS,
            cost_estimate=FREE,
        )(*at, *arrays)

    layout = [(p, (0, 1) if p[0] == LAST else (0, 1, 2)) for p in FIRST + REST]
    layout += [((LAST, cross), (2,)) for cross in range(2)]
    packed = pack(layout[: len(FIRST)])
    packed += pack(layout[len(FIRST) :], packed[0])
    late = jnp.concatenate([packed[-2], swap(packed[-1])], axis=0)
    got = {}
    for p, piece in zip(FIRST + REST, packed):
        got[p] = across(after(piece, late) if p == JOINED_BY else piece, *p)
    own = call(functools.partial(merge_body, rows), chips, shape(2, chips * rows, gw))(*got.values())
    other = swap(own)
    late = across(late, LAST, 0)

    def attend(dzs, *others):
        pieces = [late] if dzs == (LAST,) else [got[dz, cross] for dz in dzs for cross in range(2)]
        count = len(pieces)
        pieces = lax.optimization_barrier((*pieces, *others))[:count] if others else pieces
        body = functools.partial(attend_body, count, rows)
        outs = call(body, 2 + count, [shape(2 * rows, gw)] * len(dzs))(own, other, *pieces)
        return dict(zip(dzs, outs))

    outs = attend((2,))
    outs |= attend((1, 0), outs[2])
    outs |= attend((LAST,), outs[0])
    back = {(dz, 0): across(outs[dz], dz, 0) for dz in (2, 1, 0, LAST)}
    back[2, 1] = swap(after(back[2, 0], outs[LAST])[rows:])
    back |= {(dz, 1): swap(after(back[dz, 0], back[2, 1], back[LAST, 0])[rows:]) for dz in (1, 0)}
    back[LAST, 1] = swap(back[LAST, 0][rows:])

    def unpack(dzs, *so_far):
        order = [(dz, cross) for dz in dzs for cross in range(2)]
        pieces = [back[piece] for piece in order]
        return pl.pallas_call(
            functools.partial(unpack_body, gw, order),
            in_specs=[SMEM, SMEM] + [VMEM] * len(order) + [HBM] * len(so_far),
            out_specs=HBM,
            out_shape=shape(rows_q, width),
            scratch_shapes=[pltpu.SemaphoreType.DMA((len(order),))],
            input_output_aliases={2 + len(order): 0} if so_far else {},
            compiler_params=PARAMS,
            cost_estimate=FREE,
        )(*at, *pieces, *so_far)

    result = unpack((LAST, 1, 0), unpack((2,)))
    return result.reshape(layers, tok_rows, width)


def partial_head(q_ref, ka_ref, va_ref, kb_ref, vb_ref, o_ref, peak_ref, total_ref):
    src, rows, _ = q_ref.shape
    q = q_ref[...].reshape(src * rows, HEAD_DIM)
    ka, va, kb, vb = (r[...].reshape(-1, HEAD_DIM) for r in (ka_ref, va_ref, kb_ref, vb_ref))
    kv = ka, beside_ones(va), kb, beside_ones(vb)
    outs = []
    for at in range(0, src * rows, SUB):
        acc, peak, total = softmax_rows(q[at : at + SUB], *kv)
        outs.append(acc)
        peak_ref[at : at + SUB] = jnp.broadcast_to(peak, (SUB, HEAD_DIM))
        total_ref[at : at + SUB] = total
    o_ref[...] = jnp.concatenate(outs, axis=0).reshape(o_ref.shape)


def partial_attend(got, other, rows_kv, rows_q):
    chips, _, width = got.shape
    heads = width // HEAD_DIM
    own_kv = got[:, : 2 * rows_kv].reshape(chips, 2, rows_kv, width)
    own_q = got[:, 2 * rows_kv :]
    other = other.reshape(chips, 2, rows_kv, width)

    def kv(which):
        return pl.BlockSpec((chips, None, rows_kv, HEAD_DIM), lambda h: (0, which, 0, h))

    q_spec = pl.BlockSpec((chips, rows_q, HEAD_DIM), lambda h: (0, 0, h))
    stat_spec = pl.BlockSpec((None, chips * rows_q, HEAD_DIM), lambda h: (h, 0, 0))
    stat = jax.ShapeDtypeStruct((heads, chips * rows_q, HEAD_DIM), F32)
    return pl.pallas_call(
        partial_head,
        grid=(heads,),
        in_specs=[q_spec, kv(0), kv(1), kv(0), kv(1)],
        out_specs=[q_spec, stat_spec, stat_spec],
        out_shape=[jax.ShapeDtypeStruct((chips, rows_q, width), F32), stat, stat],
        compiler_params=PARAMS,
    )(own_q, own_kv, own_kv, other, other)


def local_blocks(keys, values, queries):
    chips = lax.axis_size("chip")
    blocks = chips // GROUPS
    ctx_rows, width = keys.shape
    gw = width // GROUPS
    heads = gw // HEAD_DIM
    layers, tok_rows, _ = queries.shape
    rows_q = layers * tok_rows
    rows_kv = ctx_rows // blocks

    def by_chip(array):
        return jnp.swapaxes(array.reshape(rows_kv, chips, gw), 0, 1)

    q = jnp.swapaxes(queries.reshape(rows_q, GROUPS, gw), 0, 1)
    q = jnp.broadcast_to(q[None], (blocks, GROUPS, rows_q, gw)).reshape(chips, rows_q, gw)
    packed = jnp.concatenate([by_chip(keys), by_chip(values), q], axis=1)
    got = lax.all_to_all(packed, "chip", split_axis=0, concat_axis=0, tiled=True)
    other = lax.ppermute(got[:, : 2 * rows_kv], "core", [(0, 1), (1, 0)])
    outs = partial_attend(got, other, rows_kv, rows_q)
    stats = [jnp.moveaxis(s[:, :, 0].reshape(heads, chips, rows_q), 0, 2) for s in outs[1:]]
    stats = jnp.concatenate(stats, axis=2)
    stats = jnp.pad(stats, ((0, 0), (0, 0), (0, -2 * heads % HEAD_DIM)))
    sent = jnp.concatenate([outs[0], stats], axis=2)
    back = lax.all_to_all(sent, "chip", split_axis=0, concat_axis=0, tiled=True)
    back = back.reshape(blocks, GROUPS, rows_q, -1)
    summed = back[..., :gw].reshape(blocks, GROUPS, rows_q, heads, HEAD_DIM)
    peak = back[..., gw : gw + heads]
    total = back[..., gw + heads : gw + 2 * heads]
    share = jnp.exp2(peak - jnp.max(peak, axis=0))
    denom = jnp.sum(share * total, axis=0)
    numer = jnp.sum(share[..., None] * summed, axis=0)
    result = (numer / denom[..., None]).astype(BF16)
    return jnp.swapaxes(result.reshape(GROUPS, rows_q, gw), 0, 1).reshape(layers, tok_rows, width)


def solution(mesh):
    rep, seq = mesh.shape["rep"], mesh.shape["seq"]
    chips = seq // 2
    by_core = Mesh(mesh.devices.reshape(rep, chips, 2), ("rep", "chip", "core"))
    rows = ("rep", "chip", "core")
    return jax.shard_map(
        local_permutes if chips == GROUPS else local_blocks,
        mesh=by_core,
        in_specs=(P(rows, None), P(rows, None), P(None, rows, None)),
        out_specs=P(None, rows, None),
        check_vma=False,
    )
```

```python
import functools
import math

import jax
import jax.numpy as jnp
from jax import lax
from jax.experimental import pallas as pl
from jax.experimental.pallas import tpu as pltpu
from jax.sharding import Mesh, PartitionSpec as P

HEAD_DIM = 128
GROUPS = 8
SUB = 128
F32 = jnp.float32
BF16 = jnp.bfloat16
VMEM = pl.BlockSpec(memory_space=pltpu.VMEM)
HBM = pl.BlockSpec(memory_space=pltpu.HBM)
SMEM = pl.BlockSpec(memory_space=pltpu.SMEM)
FREE = pl.CostEstimate(flops=0, bytes_accessed=0, transcendentals=0)
PARAMS = pltpu.CompilerParams(vmem_limit_bytes=40 * 2**20)


def softmax_rows(q, ka, va, kb, vb):
    factor = math.log2(math.e) / math.sqrt(HEAD_DIM)
    nt = (((1,), (1,)), ((), ()))
    sa = lax.dot_general(q, ka, nt, preferred_element_type=F32)
    sb = lax.dot_general(q, kb, nt, preferred_element_type=F32)
    peak = jnp.max(jnp.maximum(sa, sb), axis=1, keepdims=True)
    ea = jnp.exp2((sa - peak) * factor).astype(BF16)
    eb = jnp.exp2((sb - peak) * factor).astype(BF16)
    both = jnp.dot(ea, va, preferred_element_type=F32) + jnp.dot(eb, vb, preferred_element_type=F32)
    return both[:, :HEAD_DIM], peak * factor, both[:, HEAD_DIM:]


def beside_ones(v):
    return jnp.concatenate([v, jnp.ones_like(v)], axis=1)


FIRST = (6, 7)
REST = (2, 4, 3, 1, 5, 0)
LAST = (6, 7)
NEAR = (2, 3, 1)


def pack_body(rows, gw, layout, chip_ref, *refs):
    arrays, out_refs, sems = refs[:3], refs[3:-1], refs[-1]
    copies = []
    for out_ref, (k, parts) in zip(out_refs, layout):
        col = pl.ds(pl.multiple_of((chip_ref[0] ^ k) * gw, HEAD_DIM), gw)
        for at, n in enumerate(parts):
            to = out_ref.at[at * rows : (at + 1) * rows]
            copies.append(pltpu.make_async_copy(arrays[n].at[:, col], to, sems.at[len(copies)]))
    for copy in copies:
        copy.start()
    for copy in copies:
        copy.wait()


def merge_body(rows, *refs):
    out_ref = refs[-1]
    for n, piece in enumerate(refs[:-1]):
        for which in range(2):
            out_ref[which, n * rows : (n + 1) * rows] = piece[which * rows : (which + 1) * rows]


def unpack_body(gw, order, chip_ref, *refs):
    pieces, out_ref, sems = refs[: len(order)], refs[-2], refs[-1]
    copies = []
    for n, k in enumerate(order):
        col = pl.ds(pl.multiple_of((chip_ref[0] ^ k) * gw, HEAD_DIM), gw)
        copies.append(pltpu.make_async_copy(pieces[n], out_ref.at[:, col], sems.at[n]))
    for copy in copies:
        copy.start()
    for copy in copies:
        copy.wait()


def attend_body(count, rows, own, other, *refs):
    queries, outs = refs[:count], refs[count:]
    for h in range(own.shape[2] // HEAD_DIM):
        col = slice(h * HEAD_DIM, (h + 1) * HEAD_DIM)
        q = jnp.concatenate([r[r.shape[0] - rows :, col] for r in queries], axis=0)
        va, vb = beside_ones(own[1, :, col]), beside_ones(other[1, :, col])
        acc, _, total = softmax_rows(q, own[0, :, col], va, other[0, :, col], vb)
        acc = (acc / total).astype(BF16)
        for n, out in enumerate(outs):
            out[:, col] = acc[n * rows : (n + 1) * rows]


def local_permutes(keys, values, queries):
    chips = lax.axis_size("chip")
    rows, width = keys.shape
    gw = width // chips
    layers, tok_rows, _ = queries.shape
    rows_q = layers * tok_rows
    assert rows_q == rows
    chip = lax.axis_index("chip").reshape(1).astype(jnp.int32)

    def across(piece, k):
        return lax.ppermute(piece, "chip", [(i, i ^ k) for i in range(chips)]) if k else piece

    def call(body, n_in, out_shape, smem=0, **more):
        return pl.pallas_call(
            body,
            in_specs=[SMEM] * smem + [VMEM] * n_in,
            out_specs=jax.tree.map(lambda _: VMEM, out_shape),
            out_shape=out_shape,
            compiler_params=PARAMS,
            cost_estimate=FREE,
            **more,
        )

    def shape(*dims):
        return jax.ShapeDtypeStruct(dims, BF16)

    sources = [keys, values, queries.reshape(rows_q, width)]
    sources = [pltpu.with_memory_space_constraint(a, pltpu.HBM) for a in sources]

    def pack(layout, after=()):
        arrays = lax.optimization_barrier((*sources, *after))[:3] if after else sources
        return pl.pallas_call(
            functools.partial(pack_body, rows, gw, layout),
            in_specs=[SMEM, HBM, HBM, HBM],
            out_specs=[VMEM] * len(layout),
            out_shape=[shape(len(parts) * rows, gw) for _, parts in layout],
            scratch_shapes=[pltpu.SemaphoreType.DMA((sum(len(parts) for _, parts in layout),))],
            compiler_params=PARAMS,
            cost_estimate=FREE,
        )(chip, *arrays)

    layout = [(k, (0, 1) if k in LAST else (0, 1, 2)) for k in FIRST + REST]
    layout += [(k, (2,)) for k in LAST]
    packed = pack(layout[: len(FIRST)])
    packed += pack(layout[len(FIRST) :], packed[:1])
    got = {k: across(piece, k) for piece, (k, _) in zip(packed[:chips], layout)}
    own = call(functools.partial(merge_body, rows), chips, shape(2, chips * rows, gw))(*got.values())
    other = lax.ppermute(own, "core", [(0, 1), (1, 0)])

    def after(array, *others):
        return lax.optimization_barrier((array, *others))[0]

    def attend(pieces, *others):
        ks, arrays = tuple(pieces), tuple(pieces.values())
        if others:
            arrays = lax.optimization_barrier((*arrays, *others))[: len(ks)]
        body = functools.partial(attend_body, len(ks), rows)
        outs = call(body, 2 + len(ks), [shape(rows, gw)] * len(ks))(own, other, *arrays)
        return dict(zip(ks, outs))

    late = {LAST[0]: across(packed[chips], LAST[0])}
    outs = attend({k: got[k] for k in (4, 5)})
    late[LAST[1]] = across(after(packed[chips + 1], outs[4]), LAST[1])
    outs |= attend({k: got[k] for k in NEAR + (0,)}, outs[4])
    outs |= attend(late, outs[0])
    back = {k: across(outs[k], k) for k in (0, 4, 5) + LAST}
    back[1] = across(outs[1], 1)
    for k, before in ((2, 5), (3, 4)):
        back[k] = across(after(outs[k], outs[LAST[0]], back[before]), k)

    def unpack(order, so_far=()):
        return pl.pallas_call(
            functools.partial(unpack_body, gw, order),
            in_specs=[SMEM] + [VMEM] * len(order) + [HBM] * len(so_far),
            out_specs=HBM,
            out_shape=shape(rows_q, width),
            scratch_shapes=[pltpu.SemaphoreType.DMA((len(order),))],
            input_output_aliases={1 + len(order): 0} if so_far else {},
            compiler_params=PARAMS,
            cost_estimate=FREE,
        )(chip, *[back[k] for k in order], *so_far)

    result = unpack(LAST + (3, 2), (unpack((0, 4, 5, 1)),))
    return result.reshape(layers, tok_rows, width)


def partial_head(q_ref, ka_ref, va_ref, kb_ref, vb_ref, o_ref, peak_ref, total_ref):
    src, rows, _ = q_ref.shape
    q = q_ref[...].reshape(src * rows, HEAD_DIM)
    ka, va, kb, vb = (r[...].reshape(-1, HEAD_DIM) for r in (ka_ref, va_ref, kb_ref, vb_ref))
    kv = ka, beside_ones(va), kb, beside_ones(vb)
    outs = []
    for at in range(0, src * rows, SUB):
        acc, peak, total = softmax_rows(q[at : at + SUB], *kv)
        outs.append(acc)
        peak_ref[at : at + SUB] = jnp.broadcast_to(peak, (SUB, HEAD_DIM))
        total_ref[at : at + SUB] = total
    o_ref[...] = jnp.concatenate(outs, axis=0).reshape(o_ref.shape)


def partial_attend(got, other, rows_kv, rows_q):
    chips, _, width = got.shape
    heads = width // HEAD_DIM
    own_kv = got[:, : 2 * rows_kv].reshape(chips, 2, rows_kv, width)
    own_q = got[:, 2 * rows_kv :]
    other = other.reshape(chips, 2, rows_kv, width)

    def kv(which):
        return pl.BlockSpec((chips, None, rows_kv, HEAD_DIM), lambda h: (0, which, 0, h))

    q_spec = pl.BlockSpec((chips, rows_q, HEAD_DIM), lambda h: (0, 0, h))
    stat_spec = pl.BlockSpec((None, chips * rows_q, HEAD_DIM), lambda h: (h, 0, 0))
    stat = jax.ShapeDtypeStruct((heads, chips * rows_q, HEAD_DIM), F32)
    return pl.pallas_call(
        partial_head,
        grid=(heads,),
        in_specs=[q_spec, kv(0), kv(1), kv(0), kv(1)],
        out_specs=[q_spec, stat_spec, stat_spec],
        out_shape=[jax.ShapeDtypeStruct((chips, rows_q, width), F32), stat, stat],
        compiler_params=PARAMS,
    )(own_q, own_kv, own_kv, other, other)


def local_blocks(keys, values, queries):
    chips = lax.axis_size("chip")
    blocks = chips // GROUPS
    ctx_rows, width = keys.shape
    gw = width // GROUPS
    heads = gw // HEAD_DIM
    layers, tok_rows, _ = queries.shape
    rows_q = layers * tok_rows
    rows_kv = ctx_rows // blocks

    def by_chip(array):
        return jnp.swapaxes(array.reshape(rows_kv, chips, gw), 0, 1)

    q = jnp.swapaxes(queries.reshape(rows_q, GROUPS, gw), 0, 1)
    q = jnp.broadcast_to(q[None], (blocks, GROUPS, rows_q, gw)).reshape(chips, rows_q, gw)
    packed = jnp.concatenate([by_chip(keys), by_chip(values), q], axis=1)
    got = lax.all_to_all(packed, "chip", split_axis=0, concat_axis=0, tiled=True)
    other = lax.ppermute(got[:, : 2 * rows_kv], "core", [(0, 1), (1, 0)])
    outs = partial_attend(got, other, rows_kv, rows_q)
    stats = [jnp.moveaxis(s[:, :, 0].reshape(heads, chips, rows_q), 0, 2) for s in outs[1:]]
    stats = jnp.concatenate(stats, axis=2)
    stats = jnp.pad(stats, ((0, 0), (0, 0), (0, -2 * heads % HEAD_DIM)))
    sent = jnp.concatenate([outs[0], stats], axis=2)
    back = lax.all_to_all(sent, "chip", split_axis=0, concat_axis=0, tiled=True)
    back = back.reshape(blocks, GROUPS, rows_q, -1)
    summed = back[..., :gw].reshape(blocks, GROUPS, rows_q, heads, HEAD_DIM)
    peak = back[..., gw : gw + heads]
    total = back[..., gw + heads : gw + 2 * heads]
    share = jnp.exp2(peak - jnp.max(peak, axis=0))
    denom = jnp.sum(share * total, axis=0)
    numer = jnp.sum(share[..., None] * summed, axis=0)
    result = (numer / denom[..., None]).astype(BF16)
    return jnp.swapaxes(result.reshape(GROUPS, rows_q, gw), 0, 1).reshape(layers, tok_rows, width)


def solution(mesh):
    rep, seq = mesh.shape["rep"], mesh.shape["seq"]
    chips = seq // 2
    by_core = Mesh(mesh.devices.reshape(rep, chips, 2), ("rep", "chip", "core"))
    rows = ("rep", "chip", "core")
    return jax.shard_map(
        local_permutes if chips == GROUPS else local_blocks,
        mesh=by_core,
        in_specs=(P(rows, None), P(rows, None), P(None, rows, None)),
        out_specs=P(None, rows, None),
        check_vma=False,
    )
```

```python
import functools
import math

import jax
import jax.numpy as jnp
from jax import lax
from jax.experimental import pallas as pl
from jax.experimental.pallas import tpu as pltpu
from jax.sharding import Mesh, PartitionSpec as P

HEAD_DIM = 128
GROUPS = 8
SUB = 128
F32 = jnp.float32
BF16 = jnp.bfloat16
VMEM = pl.BlockSpec(memory_space=pltpu.VMEM)
HBM = pl.BlockSpec(memory_space=pltpu.HBM)
SMEM = pl.BlockSpec(memory_space=pltpu.SMEM)
FREE = pl.CostEstimate(flops=0, bytes_accessed=0, transcendentals=0)
PARAMS = pltpu.CompilerParams(vmem_limit_bytes=40 * 2**20)


def softmax_rows(q, ka, va, kb, vb):
    factor = math.log2(math.e) / math.sqrt(HEAD_DIM)
    nt = (((1,), (1,)), ((), ()))
    sa = lax.dot_general(q, ka, nt, preferred_element_type=F32)
    sb = lax.dot_general(q, kb, nt, preferred_element_type=F32)
    peak = jnp.max(jnp.maximum(sa, sb), axis=1, keepdims=True)
    ea = jnp.exp2((sa - peak) * factor).astype(BF16)
    eb = jnp.exp2((sb - peak) * factor).astype(BF16)
    both = jnp.dot(ea, va, preferred_element_type=F32) + jnp.dot(eb, vb, preferred_element_type=F32)
    return both[:, :HEAD_DIM], peak * factor, both[:, HEAD_DIM:]


def beside_ones(v):
    return jnp.concatenate([v, jnp.ones_like(v)], axis=1)


LAST = 3
JOINED_BY = (0, 0)
FIRST = ((3, 0), (1, 0), (3, 1))
REST = ((2, 0), (1, 1), (0, 0), (2, 1), (0, 1))


def columns(at, dz, cross, gw):
    group = at[0][0] ^ (2 * dz + (at[1][0] ^ cross))
    return pl.ds(pl.multiple_of(group * gw, HEAD_DIM), gw)


def pack_body(rows, gw, layout, chip_ref, core_ref, *refs):
    at = chip_ref, core_ref
    arrays, out_refs, sems = refs[:3], refs[3:-1], refs[-1]
    copies = []
    for out_ref, (piece, parts) in zip(out_refs, layout):
        col = columns(at, *piece, gw)
        for first, n in enumerate(parts):
            to = out_ref.at[first * rows : (first + 1) * rows]
            copies.append(pltpu.make_async_copy(arrays[n].at[:, col], to, sems.at[len(copies)]))
    for copy in copies:
        copy.start()
    for copy in copies:
        copy.wait()


def merge_body(rows, *refs):
    out_ref = refs[-1]
    for n, piece in enumerate(refs[:-1]):
        for which in range(2):
            out_ref[which, n * rows : (n + 1) * rows] = piece[which * rows : (which + 1) * rows]


def unpack_body(gw, order, chip_ref, core_ref, *refs):
    at = chip_ref, core_ref
    pieces, out_ref, sems = refs[: len(order)], refs[-2], refs[-1]
    rows = out_ref.shape[0]
    copies = []
    for n, piece in enumerate(order):
        to = out_ref.at[:, columns(at, *piece, gw)]
        copies.append(pltpu.make_async_copy(pieces[n].at[:rows], to, sems.at[n]))
    for copy in copies:
        copy.start()
    for copy in copies:
        copy.wait()


def attend_body(count, rows, own, other, *refs):
    queries, outs = refs[:count], refs[count:]
    for h in range(own.shape[2] // HEAD_DIM):
        col = slice(h * HEAD_DIM, (h + 1) * HEAD_DIM)
        q = [r[...][:, col] if r.shape[0] == 2 * rows else r[2 * rows :, col] for r in queries]
        va, vb = beside_ones(own[1, :, col]), beside_ones(other[1, :, col])
        acc, _, total = softmax_rows(jnp.concatenate(q, axis=0), own[0, :, col], va, other[0, :, col], vb)
        acc = (acc / total).astype(BF16)
        for n, out in enumerate(outs):
            out[:, col] = acc[n * 2 * rows : (n + 1) * 2 * rows]


def local_permutes(keys, values, queries):
    chips = lax.axis_size("chip")
    rows, width = keys.shape
    gw = width // chips
    layers, tok_rows, _ = queries.shape
    rows_q = layers * tok_rows
    assert rows_q == rows
    at = [lax.axis_index(name).reshape(1).astype(jnp.int32) for name in ("chip", "core")]

    def across(array, dz, cross):
        senders = [(chip, core) for chip in range(chips) for core in range(2)]
        to = [(chip ^ (2 * dz + (core ^ cross)), core ^ cross) for chip, core in senders]
        pairs = [(2 * a + b, 2 * c + d) for (a, b), (c, d) in zip(senders, to)]
        return lax.ppermute(array, ("chip", "core"), pairs)

    def swap(array):
        return lax.ppermute(array, "core", [(0, 1), (1, 0)])

    def after(array, *others):
        return lax.optimization_barrier((array, *others))[0]

    def call(body, n_in, out_shape):
        return pl.pallas_call(
            body,
            in_specs=[VMEM] * n_in,
            out_specs=jax.tree.map(lambda _: VMEM, out_shape),
            out_shape=out_shape,
            compiler_params=PARAMS,
            cost_estimate=FREE,
        )

    def shape(*dims):
        return jax.ShapeDtypeStruct(dims, BF16)

    sources = [keys, values, queries.reshape(rows_q, width)]
    sources = [pltpu.with_memory_space_constraint(a, pltpu.HBM) for a in sources]

    def pack(layout, *others):
        arrays = lax.optimization_barrier((*sources, *others))[:3] if others else sources
        return pl.pallas_call(
            functools.partial(pack_body, rows, gw, layout),
            in_specs=[SMEM, SMEM, HBM, HBM, HBM],
            out_specs=[VMEM] * len(layout),
            out_shape=[shape(len(parts) * rows, gw) for _, parts in layout],
            scratch_shapes=[pltpu.SemaphoreType.DMA((sum(len(parts) for _, parts in layout),))],
            compiler_params=PARAMS,
            cost_estimate=FREE,
        )(*at, *arrays)

    layout = [(p, (0, 1) if p[0] == LAST else (0, 1, 2)) for p in FIRST + REST]
    layout += [((LAST, cross), (2,)) for cross in range(2)]
    packed = pack(layout[: len(FIRST)])
    packed += pack(layout[len(FIRST) :], packed[0])
    late = jnp.concatenate([packed[-2], swap(packed[-1])], axis=0)
    got = {}
    for p, piece in zip(FIRST + REST, packed):
        got[p] = across(after(piece, late) if p == JOINED_BY else piece, *p)
    own = call(functools.partial(merge_body, rows), chips, shape(2, chips * rows, gw))(*got.values())
    other = swap(own)
    late = across(late, LAST, 0)

    def attend(dzs, *others):
        pieces = [late] if dzs == (LAST,) else [got[dz, cross] for dz in dzs for cross in range(2)]
        count = len(pieces)
        pieces = lax.optimization_barrier((*pieces, *others))[:count] if others else pieces
        body = functools.partial(attend_body, count, rows)
        outs = call(body, 2 + count, [shape(2 * rows, gw)] * len(dzs))(own, other, *pieces)
        return dict(zip(dzs, outs))

    outs = attend((2,))
    outs |= attend((0, 1), outs[2])
    outs |= attend((LAST,), outs[0])
    back = {(dz, 0): across(outs[dz], dz, 0) for dz in (2, 0, 1, LAST)}
    back[2, 1] = swap(after(back[2, 0], outs[LAST])[rows:])
    back |= {(dz, 1): swap(after(back[dz, 0], back[2, 1])[rows:]) for dz in (0, 1)}
    back[LAST, 1] = swap(after(back[LAST, 0], back[2, 1])[rows:])

    def unpack(dzs, *so_far):
        order = [(dz, cross) for dz in dzs for cross in range(2)]
        pieces = [back[piece] for piece in order]
        return pl.pallas_call(
            functools.partial(unpack_body, gw, order),
            in_specs=[SMEM, SMEM] + [VMEM] * len(order) + [HBM] * len(so_far),
            out_specs=HBM,
            out_shape=shape(rows_q, width),
            scratch_shapes=[pltpu.SemaphoreType.DMA((len(order),))],
            input_output_aliases={2 + len(order): 0} if so_far else {},
            compiler_params=PARAMS,
            cost_estimate=FREE,
        )(*at, *pieces, *so_far)

    result = unpack((LAST, 0, 1, 2))
    return result.reshape(layers, tok_rows, width)


def partial_head(q_ref, ka_ref, va_ref, kb_ref, vb_ref, o_ref, peak_ref, total_ref):
    src, rows, _ = q_ref.shape
    q = q_ref[...].reshape(src * rows, HEAD_DIM)
    ka, va, kb, vb = (r[...].reshape(-1, HEAD_DIM) for r in (ka_ref, va_ref, kb_ref, vb_ref))
    kv = ka, beside_ones(va), kb, beside_ones(vb)
    outs = []
    for at in range(0, src * rows, SUB):
        acc, peak, total = softmax_rows(q[at : at + SUB], *kv)
        outs.append(acc)
        peak_ref[at : at + SUB] = jnp.broadcast_to(peak, (SUB, HEAD_DIM))
        total_ref[at : at + SUB] = total
    o_ref[...] = jnp.concatenate(outs, axis=0).reshape(o_ref.shape)


def partial_attend(got, other, rows_kv, rows_q):
    chips, _, width = got.shape
    heads = width // HEAD_DIM
    own_kv = got[:, : 2 * rows_kv].reshape(chips, 2, rows_kv, width)
    own_q = got[:, 2 * rows_kv :]
    other = other.reshape(chips, 2, rows_kv, width)

    def kv(which):
        return pl.BlockSpec((chips, None, rows_kv, HEAD_DIM), lambda h: (0, which, 0, h))

    q_spec = pl.BlockSpec((chips, rows_q, HEAD_DIM), lambda h: (0, 0, h))
    stat_spec = pl.BlockSpec((None, chips * rows_q, HEAD_DIM), lambda h: (h, 0, 0))
    stat = jax.ShapeDtypeStruct((heads, chips * rows_q, HEAD_DIM), F32)
    return pl.pallas_call(
        partial_head,
        grid=(heads,),
        in_specs=[q_spec, kv(0), kv(1), kv(0), kv(1)],
        out_specs=[q_spec, stat_spec, stat_spec],
        out_shape=[jax.ShapeDtypeStruct((chips, rows_q, width), F32), stat, stat],
        compiler_params=PARAMS,
    )(own_q, own_kv, own_kv, other, other)


def local_blocks(keys, values, queries):
    chips = lax.axis_size("chip")
    blocks = chips // GROUPS
    ctx_rows, width = keys.shape
    gw = width // GROUPS
    heads = gw // HEAD_DIM
    layers, tok_rows, _ = queries.shape
    rows_q = layers * tok_rows
    rows_kv = ctx_rows // blocks

    def by_chip(array):
        return jnp.swapaxes(array.reshape(rows_kv, chips, gw), 0, 1)

    q = jnp.swapaxes(queries.reshape(rows_q, GROUPS, gw), 0, 1)
    q = jnp.broadcast_to(q[None], (blocks, GROUPS, rows_q, gw)).reshape(chips, rows_q, gw)
    packed = jnp.concatenate([by_chip(keys), by_chip(values), q], axis=1)
    got = lax.all_to_all(packed, "chip", split_axis=0, concat_axis=0, tiled=True)
    other = lax.ppermute(got[:, : 2 * rows_kv], "core", [(0, 1), (1, 0)])
    outs = partial_attend(got, other, rows_kv, rows_q)
    stats = [jnp.moveaxis(s[:, :, 0].reshape(heads, chips, rows_q), 0, 2) for s in outs[1:]]
    stats = jnp.concatenate(stats, axis=2)
    stats = jnp.pad(stats, ((0, 0), (0, 0), (0, -2 * heads % HEAD_DIM)))
    sent = jnp.concatenate([outs[0], stats], axis=2)
    back = lax.all_to_all(sent, "chip", split_axis=0, concat_axis=0, tiled=True)
    back = back.reshape(blocks, GROUPS, rows_q, -1)
    summed = back[..., :gw].reshape(blocks, GROUPS, rows_q, heads, HEAD_DIM)
    peak = back[..., gw : gw + heads]
    total = back[..., gw + heads : gw + 2 * heads]
    share = jnp.exp2(peak - jnp.max(peak, axis=0))
    denom = jnp.sum(share * total, axis=0)
    numer = jnp.sum(share[..., None] * summed, axis=0)
    result = (numer / denom[..., None]).astype(BF16)
    return jnp.swapaxes(result.reshape(GROUPS, rows_q, gw), 0, 1).reshape(layers, tok_rows, width)


def solution(mesh):
    rep, seq = mesh.shape["rep"], mesh.shape["seq"]
    chips = seq // 2
    by_core = Mesh(mesh.devices.reshape(rep, chips, 2), ("rep", "chip", "core"))
    rows = ("rep", "chip", "core")
    return jax.shard_map(
        local_permutes if chips == GROUPS else local_blocks,
        mesh=by_core,
        in_specs=(P(rows, None), P(rows, None), P(None, rows, None)),
        out_specs=P(None, rows, None),
        check_vma=False,
    )
```

```python
import functools
import math

import jax
import jax.numpy as jnp
from jax import lax
from jax.experimental import pallas as pl
from jax.experimental.pallas import tpu as pltpu
from jax.sharding import Mesh, PartitionSpec as P

HEAD_DIM = 128
GROUPS = 8
SUB = 128
F32 = jnp.float32
BF16 = jnp.bfloat16
VMEM = pl.BlockSpec(memory_space=pltpu.VMEM)
HBM = pl.BlockSpec(memory_space=pltpu.HBM)
SMEM = pl.BlockSpec(memory_space=pltpu.SMEM)
FREE = pl.CostEstimate(flops=0, bytes_accessed=0, transcendentals=0)
PARAMS = pltpu.CompilerParams(vmem_limit_bytes=40 * 2**20)


def softmax_rows(q, ka, va, kb, vb):
    factor = math.log2(math.e) / math.sqrt(HEAD_DIM)
    nt = (((1,), (1,)), ((), ()))
    sa = lax.dot_general(q, ka, nt, preferred_element_type=F32)
    sb = lax.dot_general(q, kb, nt, preferred_element_type=F32)
    peak = jnp.max(jnp.maximum(sa, sb), axis=1, keepdims=True)
    ea = jnp.exp2((sa - peak) * factor).astype(BF16)
    eb = jnp.exp2((sb - peak) * factor).astype(BF16)
    both = jnp.dot(ea, va, preferred_element_type=F32) + jnp.dot(eb, vb, preferred_element_type=F32)
    return both[:, :HEAD_DIM], peak * factor, both[:, HEAD_DIM:]


def beside_ones(v):
    return jnp.concatenate([v, jnp.ones_like(v)], axis=1)


LAST = 3
JOINED_BY = (0, 0)
FIRST = ((3, 0), (1, 0), (3, 1))
REST = ((2, 0), (1, 1), (0, 0), (2, 1), (0, 1))


def columns(at, dz, cross, gw):
    group = at[0][0] ^ (2 * dz + (at[1][0] ^ cross))
    return pl.ds(pl.multiple_of(group * gw, HEAD_DIM), gw)


def pack_body(rows, gw, layout, chip_ref, core_ref, *refs):
    at = chip_ref, core_ref
    arrays, out_refs, sems = refs[:3], refs[3:-1], refs[-1]
    copies = []
    for out_ref, (piece, parts) in zip(out_refs, layout):
        col = columns(at, *piece, gw)
        for first, n in enumerate(parts):
            to = out_ref.at[first * rows : (first + 1) * rows]
            copies.append(pltpu.make_async_copy(arrays[n].at[:, col], to, sems.at[len(copies)]))
    for copy in copies:
        copy.start()
    for copy in copies:
        copy.wait()


def merge_body(rows, *refs):
    out_ref = refs[-1]
    for n, piece in enumerate(refs[:-1]):
        for which in range(2):
            out_ref[which, n * rows : (n + 1) * rows] = piece[which * rows : (which + 1) * rows]


def unpack_body(gw, order, chip_ref, core_ref, *refs):
    at = chip_ref, core_ref
    pieces, out_ref, sems = refs[: len(order)], refs[-2], refs[-1]
    rows = out_ref.shape[0]
    copies = []
    for n, piece in enumerate(order):
        to = out_ref.at[:, columns(at, *piece, gw)]
        copies.append(pltpu.make_async_copy(pieces[n].at[:rows], to, sems.at[n]))
    for copy in copies:
        copy.start()
    for copy in copies:
        copy.wait()


def attend_body(count, rows, own, other, *refs):
    queries, outs = refs[:count], refs[count:]
    for h in range(own.shape[2] // HEAD_DIM):
        col = slice(h * HEAD_DIM, (h + 1) * HEAD_DIM)
        q = [r[...][:, col] if r.shape[0] == 2 * rows else r[2 * rows :, col] for r in queries]
        va, vb = beside_ones(own[1, :, col]), beside_ones(other[1, :, col])
        acc, _, total = softmax_rows(jnp.concatenate(q, axis=0), own[0, :, col], va, other[0, :, col], vb)
        acc = (acc / total).astype(BF16)
        for n, out in enumerate(outs):
            out[:, col] = acc[n * 2 * rows : (n + 1) * 2 * rows]


def local_permutes(keys, values, queries):
    chips = lax.axis_size("chip")
    rows, width = keys.shape
    gw = width // chips
    layers, tok_rows, _ = queries.shape
    rows_q = layers * tok_rows
    assert rows_q == rows
    at = [lax.axis_index(name).reshape(1).astype(jnp.int32) for name in ("chip", "core")]

    def across(array, dz, cross, back=False):
        senders = [(chip, core) for chip in range(chips) for core in range(2)]
        to = [(chip ^ (2 * dz + (core if back else core ^ cross)), core ^ cross) for chip, core in senders]
        pairs = [(2 * a + b, 2 * c + d) for (a, b), (c, d) in zip(senders, to)]
        return lax.ppermute(array, ("chip", "core"), pairs)

    def swap(array):
        return lax.ppermute(array, "core", [(0, 1), (1, 0)])

    def after(array, *others):
        return lax.optimization_barrier((array, *others))[0]

    def call(body, n_in, out_shape):
        return pl.pallas_call(
            body,
            in_specs=[VMEM] * n_in,
            out_specs=jax.tree.map(lambda _: VMEM, out_shape),
            out_shape=out_shape,
            compiler_params=PARAMS,
            cost_estimate=FREE,
        )

    def shape(*dims):
        return jax.ShapeDtypeStruct(dims, BF16)

    sources = [keys, values, queries.reshape(rows_q, width)]
    sources = [pltpu.with_memory_space_constraint(a, pltpu.HBM) for a in sources]

    def pack(layout, *others):
        arrays = lax.optimization_barrier((*sources, *others))[:3] if others else sources
        return pl.pallas_call(
            functools.partial(pack_body, rows, gw, layout),
            in_specs=[SMEM, SMEM, HBM, HBM, HBM],
            out_specs=[VMEM] * len(layout),
            out_shape=[shape(len(parts) * rows, gw) for _, parts in layout],
            scratch_shapes=[pltpu.SemaphoreType.DMA((sum(len(parts) for _, parts in layout),))],
            compiler_params=PARAMS,
            cost_estimate=FREE,
        )(*at, *arrays)

    layout = [(p, (0, 1) if p[0] == LAST else (0, 1, 2)) for p in FIRST + REST]
    layout += [((LAST, cross), (2,)) for cross in range(2)]
    packed = pack(layout[: len(FIRST)])
    packed += pack(layout[len(FIRST) :], packed[0])
    late = jnp.concatenate([packed[-2], swap(packed[-1])], axis=0)
    got = {}
    for p, piece in zip(FIRST + REST, packed):
        got[p] = across(after(piece, late) if p == JOINED_BY else piece, *p)
    own = call(functools.partial(merge_body, rows), chips, shape(2, chips * rows, gw))(*got.values())
    other = swap(own)
    late = across(late, LAST, 0)

    def attend(dzs, *others):
        pieces = [late] if dzs == (LAST,) else [got[dz, cross] for dz in dzs for cross in range(2)]
        count = len(pieces)
        pieces = lax.optimization_barrier((*pieces, *others))[:count] if others else pieces
        body = functools.partial(attend_body, count, rows)
        outs = call(body, 2 + count, [shape(2 * rows, gw)] * len(dzs))(own, other, *pieces)
        return dict(zip(dzs, outs))

    outs = attend((2,))
    outs |= attend((0, 1), outs[2])
    outs |= attend((LAST,), outs[0])
    back = {(dz, 0): across(outs[dz], dz, 0) for dz in (2, 0, 1)}
    for cross in (1, 0):
        back[LAST, cross] = across(outs[LAST][cross * rows : (cross + 1) * rows], LAST, cross, True)
    back |= {(dz, 1): swap(back[dz, 0][rows:]) for dz in (0, 1, 2)}

    def unpack(dzs, *so_far):
        order = [(dz, cross) for dz in dzs for cross in range(2)]
        pieces = [back[piece] for piece in order]
        return pl.pallas_call(
            functools.partial(unpack_body, gw, order),
            in_specs=[SMEM, SMEM] + [VMEM] * len(order) + [HBM] * len(so_far),
            out_specs=HBM,
            out_shape=shape(rows_q, width),
            scratch_shapes=[pltpu.SemaphoreType.DMA((len(order),))],
            input_output_aliases={2 + len(order): 0} if so_far else {},
            compiler_params=PARAMS,
            cost_estimate=FREE,
        )(*at, *pieces, *so_far)

    result = unpack((LAST, 0, 1, 2))
    return result.reshape(layers, tok_rows, width)


def partial_head(q_ref, ka_ref, va_ref, kb_ref, vb_ref, o_ref, peak_ref, total_ref):
    src, rows, _ = q_ref.shape
    q = q_ref[...].reshape(src * rows, HEAD_DIM)
    ka, va, kb, vb = (r[...].reshape(-1, HEAD_DIM) for r in (ka_ref, va_ref, kb_ref, vb_ref))
    kv = ka, beside_ones(va), kb, beside_ones(vb)
    outs = []
    for at in range(0, src * rows, SUB):
        acc, peak, total = softmax_rows(q[at : at + SUB], *kv)
        outs.append(acc)
        peak_ref[at : at + SUB] = jnp.broadcast_to(peak, (SUB, HEAD_DIM))
        total_ref[at : at + SUB] = total
    o_ref[...] = jnp.concatenate(outs, axis=0).reshape(o_ref.shape)


def partial_attend(got, other, rows_kv, rows_q):
    chips, _, width = got.shape
    heads = width // HEAD_DIM
    own_kv = got[:, : 2 * rows_kv].reshape(chips, 2, rows_kv, width)
    own_q = got[:, 2 * rows_kv :]
    other = other.reshape(chips, 2, rows_kv, width)

    def kv(which):
        return pl.BlockSpec((chips, None, rows_kv, HEAD_DIM), lambda h: (0, which, 0, h))

    q_spec = pl.BlockSpec((chips, rows_q, HEAD_DIM), lambda h: (0, 0, h))
    stat_spec = pl.BlockSpec((None, chips * rows_q, HEAD_DIM), lambda h: (h, 0, 0))
    stat = jax.ShapeDtypeStruct((heads, chips * rows_q, HEAD_DIM), F32)
    return pl.pallas_call(
        partial_head,
        grid=(heads,),
        in_specs=[q_spec, kv(0), kv(1), kv(0), kv(1)],
        out_specs=[q_spec, stat_spec, stat_spec],
        out_shape=[jax.ShapeDtypeStruct((chips, rows_q, width), F32), stat, stat],
        compiler_params=PARAMS,
    )(own_q, own_kv, own_kv, other, other)


def local_blocks(keys, values, queries):
    chips = lax.axis_size("chip")
    blocks = chips // GROUPS
    ctx_rows, width = keys.shape
    gw = width // GROUPS
    heads = gw // HEAD_DIM
    layers, tok_rows, _ = queries.shape
    rows_q = layers * tok_rows
    rows_kv = ctx_rows // blocks

    def by_chip(array):
        return jnp.swapaxes(array.reshape(rows_kv, chips, gw), 0, 1)

    q = jnp.swapaxes(queries.reshape(rows_q, GROUPS, gw), 0, 1)
    q = jnp.broadcast_to(q[None], (blocks, GROUPS, rows_q, gw)).reshape(chips, rows_q, gw)
    packed = jnp.concatenate([by_chip(keys), by_chip(values), q], axis=1)
    got = lax.all_to_all(packed, "chip", split_axis=0, concat_axis=0, tiled=True)
    other = lax.ppermute(got[:, : 2 * rows_kv], "core", [(0, 1), (1, 0)])
    outs = partial_attend(got, other, rows_kv, rows_q)
    stats = [jnp.moveaxis(s[:, :, 0].reshape(heads, chips, rows_q), 0, 2) for s in outs[1:]]
    stats = jnp.concatenate(stats, axis=2)
    stats = jnp.pad(stats, ((0, 0), (0, 0), (0, -2 * heads % HEAD_DIM)))
    sent = jnp.concatenate([outs[0], stats], axis=2)
    back = lax.all_to_all(sent, "chip", split_axis=0, concat_axis=0, tiled=True)
    back = back.reshape(blocks, GROUPS, rows_q, -1)
    summed = back[..., :gw].reshape(blocks, GROUPS, rows_q, heads, HEAD_DIM)
    peak = back[..., gw : gw + heads]
    total = back[..., gw + heads : gw + 2 * heads]
    share = jnp.exp2(peak - jnp.max(peak, axis=0))
    denom = jnp.sum(share * total, axis=0)
    numer = jnp.sum(share[..., None] * summed, axis=0)
    result = (numer / denom[..., None]).astype(BF16)
    return jnp.swapaxes(result.reshape(GROUPS, rows_q, gw), 0, 1).reshape(layers, tok_rows, width)


def solution(mesh):
    rep, seq = mesh.shape["rep"], mesh.shape["seq"]
    chips = seq // 2
    by_core = Mesh(mesh.devices.reshape(rep, chips, 2), ("rep", "chip", "core"))
    rows = ("rep", "chip", "core")
    return jax.shard_map(
        local_permutes if chips == GROUPS else local_blocks,
        mesh=by_core,
        in_specs=(P(rows, None), P(rows, None), P(None, rows, None)),
        out_specs=P(None, rows, None),
        check_vma=False,
    )
```

```python
import functools
import math

import jax
import jax.numpy as jnp
from jax import lax
from jax.experimental import pallas as pl
from jax.experimental.pallas import tpu as pltpu
from jax.sharding import Mesh, PartitionSpec as P

HEAD_DIM = 128
GROUPS = 8
SUB = 128
F32 = jnp.float32
BF16 = jnp.bfloat16
VMEM = pl.BlockSpec(memory_space=pltpu.VMEM)
HBM = pl.BlockSpec(memory_space=pltpu.HBM)
SMEM = pl.BlockSpec(memory_space=pltpu.SMEM)
FREE = pl.CostEstimate(flops=0, bytes_accessed=0, transcendentals=0)
PARAMS = pltpu.CompilerParams(vmem_limit_bytes=40 * 2**20)


def softmax_rows(q, ka, va, kb, vb):
    factor = math.log2(math.e) / math.sqrt(HEAD_DIM)
    nt = (((1,), (1,)), ((), ()))
    sa = lax.dot_general(q, ka, nt, preferred_element_type=F32)
    sb = lax.dot_general(q, kb, nt, preferred_element_type=F32)
    peak = jnp.max(jnp.maximum(sa, sb), axis=1, keepdims=True)
    ea = jnp.exp2((sa - peak) * factor).astype(BF16)
    eb = jnp.exp2((sb - peak) * factor).astype(BF16)
    both = jnp.dot(ea, va, preferred_element_type=F32) + jnp.dot(eb, vb, preferred_element_type=F32)
    return both[:, :HEAD_DIM], peak * factor, both[:, HEAD_DIM:]


def beside_ones(v):
    return jnp.concatenate([v, jnp.ones_like(v)], axis=1)


LAST = 3
JOINED_BY = (0, 0)
FIRST = ((3, 0), (1, 0), (3, 1))
REST = ((2, 0), (1, 1), (0, 0), (2, 1), (0, 1))


def columns(at, dz, cross, gw):
    group = at[0][0] ^ (2 * dz + (at[1][0] ^ cross))
    return pl.ds(pl.multiple_of(group * gw, HEAD_DIM), gw)


def pack_body(rows, gw, layout, chip_ref, core_ref, *refs):
    at = chip_ref, core_ref
    arrays, out_refs, sems = refs[:3], refs[3:-1], refs[-1]
    copies = []
    for out_ref, (piece, parts) in zip(out_refs, layout):
        col = columns(at, *piece, gw)
        for first, n in enumerate(parts):
            to = out_ref.at[first * rows : (first + 1) * rows]
            copies.append(pltpu.make_async_copy(arrays[n].at[:, col], to, sems.at[len(copies)]))
    for copy in copies:
        copy.start()
    for copy in copies:
        copy.wait()


def merge_body(rows, *refs):
    out_ref = refs[-1]
    for n, piece in enumerate(refs[:-1]):
        for which in range(2):
            out_ref[which, n * rows : (n + 1) * rows] = piece[which * rows : (which + 1) * rows]


def unpack_body(gw, order, chip_ref, core_ref, *refs):
    at = chip_ref, core_ref
    pieces, out_ref, sems = refs[: len(order)], refs[-2], refs[-1]
    rows = out_ref.shape[0]
    copies = []
    for n, piece in enumerate(order):
        to = out_ref.at[:, columns(at, *piece, gw)]
        copies.append(pltpu.make_async_copy(pieces[n].at[:rows], to, sems.at[n]))
    for copy in copies:
        copy.start()
    for copy in copies:
        copy.wait()


def attend_body(count, rows, own, other, *refs):
    queries, outs = refs[:count], refs[count:]
    for h in range(own.shape[2] // HEAD_DIM):
        col = slice(h * HEAD_DIM, (h + 1) * HEAD_DIM)
        q = [r[...][:, col] if r.shape[0] == 2 * rows else r[2 * rows :, col] for r in queries]
        va, vb = beside_ones(own[1, :, col]), beside_ones(other[1, :, col])
        acc, _, total = softmax_rows(jnp.concatenate(q, axis=0), own[0, :, col], va, other[0, :, col], vb)
        acc = (acc / total).astype(BF16)
        for n, out in enumerate(outs):
            out[:, col] = acc[n * 2 * rows : (n + 1) * 2 * rows]


def local_permutes(keys, values, queries):
    chips = lax.axis_size("chip")
    rows, width = keys.shape
    gw = width // chips
    layers, tok_rows, _ = queries.shape
    rows_q = layers * tok_rows
    assert rows_q == rows
    at = [lax.axis_index(name).reshape(1).astype(jnp.int32) for name in ("chip", "core")]

    def across(array, dz, cross, back=False):
        senders = [(chip, core) for chip in range(chips) for core in range(2)]
        to = [(chip ^ (2 * dz + (core if back else core ^ cross)), core ^ cross) for chip, core in senders]
        pairs = [(2 * a + b, 2 * c + d) for (a, b), (c, d) in zip(senders, to)]
        return lax.ppermute(array, ("chip", "core"), pairs)

    def swap(array):
        return lax.ppermute(array, "core", [(0, 1), (1, 0)])

    def after(array, *others):
        return lax.optimization_barrier((array, *others))[0]

    def call(body, n_in, out_shape):
        return pl.pallas_call(
            body,
            in_specs=[VMEM] * n_in,
            out_specs=jax.tree.map(lambda _: VMEM, out_shape),
            out_shape=out_shape,
            compiler_params=PARAMS,
            cost_estimate=FREE,
        )

    def shape(*dims):
        return jax.ShapeDtypeStruct(dims, BF16)

    sources = [keys, values, queries.reshape(rows_q, width)]
    sources = [pltpu.with_memory_space_constraint(a, pltpu.HBM) for a in sources]

    def pack(layout, *others):
        arrays = lax.optimization_barrier((*sources, *others))[:3] if others else sources
        return pl.pallas_call(
            functools.partial(pack_body, rows, gw, layout),
            in_specs=[SMEM, SMEM, HBM, HBM, HBM],
            out_specs=[VMEM] * len(layout),
            out_shape=[shape(len(parts) * rows, gw) for _, parts in layout],
            scratch_shapes=[pltpu.SemaphoreType.DMA((sum(len(parts) for _, parts in layout),))],
            compiler_params=PARAMS,
            cost_estimate=FREE,
        )(*at, *arrays)

    layout = [(p, (0, 1) if p[0] == LAST else (0, 1, 2)) for p in FIRST + REST]
    layout += [((LAST, cross), (2,)) for cross in range(2)]
    packed = pack(layout[: len(FIRST)])
    packed += pack(layout[len(FIRST) :], packed[0])
    late = jnp.concatenate([packed[-2], swap(packed[-1])], axis=0)
    got = {}
    for p, piece in zip(FIRST + REST, packed):
        got[p] = across(after(piece, late) if p == JOINED_BY else piece, *p)
    own = call(functools.partial(merge_body, rows), chips, shape(2, chips * rows, gw))(*got.values())
    other = swap(own)
    late = across(late, LAST, 0)

    def attend(dzs, *others):
        pieces = [late] if dzs == (LAST,) else [got[dz, cross] for dz in dzs for cross in range(2)]
        count = len(pieces)
        pieces = lax.optimization_barrier((*pieces, *others))[:count] if others else pieces
        body = functools.partial(attend_body, count, rows)
        outs = call(body, 2 + count, [shape(2 * rows, gw)] * len(dzs))(own, other, *pieces)
        return dict(zip(dzs, outs))

    outs = attend((2,))
    outs |= attend((1, 0), outs[2])
    back = {(dz, 0): across(outs[dz], dz, 0) for dz in (2, 1, 0)}
    outs |= attend((LAST,), back[0, 0])
    for cross in (1, 0):
        back[LAST, cross] = across(outs[LAST][cross * rows : (cross + 1) * rows], LAST, cross, True)
    back |= {(dz, 1): swap(back[dz, 0][rows:]) for dz in (1, 0, 2)}

    def unpack(dzs, *so_far):
        order = [(dz, cross) for dz in dzs for cross in range(2)]
        pieces = [back[piece] for piece in order]
        return pl.pallas_call(
            functools.partial(unpack_body, gw, order),
            in_specs=[SMEM, SMEM] + [VMEM] * len(order) + [HBM] * len(so_far),
            out_specs=HBM,
            out_shape=shape(rows_q, width),
            scratch_shapes=[pltpu.SemaphoreType.DMA((len(order),))],
            input_output_aliases={2 + len(order): 0} if so_far else {},
            compiler_params=PARAMS,
            cost_estimate=FREE,
        )(*at, *pieces, *so_far)

    result = unpack((LAST, 1, 0, 2))
    return result.reshape(layers, tok_rows, width)


def partial_head(q_ref, ka_ref, va_ref, kb_ref, vb_ref, o_ref, peak_ref, total_ref):
    src, rows, _ = q_ref.shape
    q = q_ref[...].reshape(src * rows, HEAD_DIM)
    ka, va, kb, vb = (r[...].reshape(-1, HEAD_DIM) for r in (ka_ref, va_ref, kb_ref, vb_ref))
    kv = ka, beside_ones(va), kb, beside_ones(vb)
    outs = []
    for at in range(0, src * rows, SUB):
        acc, peak, total = softmax_rows(q[at : at + SUB], *kv)
        outs.append(acc)
        peak_ref[at : at + SUB] = jnp.broadcast_to(peak, (SUB, HEAD_DIM))
        total_ref[at : at + SUB] = total
    o_ref[...] = jnp.concatenate(outs, axis=0).reshape(o_ref.shape)


def partial_attend(got, other, rows_kv, rows_q):
    chips, _, width = got.shape
    heads = width // HEAD_DIM
    own_kv = got[:, : 2 * rows_kv].reshape(chips, 2, rows_kv, width)
    own_q = got[:, 2 * rows_kv :]
    other = other.reshape(chips, 2, rows_kv, width)

    def kv(which):
        return pl.BlockSpec((chips, None, rows_kv, HEAD_DIM), lambda h: (0, which, 0, h))

    q_spec = pl.BlockSpec((chips, rows_q, HEAD_DIM), lambda h: (0, 0, h))
    stat_spec = pl.BlockSpec((None, chips * rows_q, HEAD_DIM), lambda h: (h, 0, 0))
    stat = jax.ShapeDtypeStruct((heads, chips * rows_q, HEAD_DIM), F32)
    return pl.pallas_call(
        partial_head,
        grid=(heads,),
        in_specs=[q_spec, kv(0), kv(1), kv(0), kv(1)],
        out_specs=[q_spec, stat_spec, stat_spec],
        out_shape=[jax.ShapeDtypeStruct((chips, rows_q, width), F32), stat, stat],
        compiler_params=PARAMS,
    )(own_q, own_kv, own_kv, other, other)


def local_blocks(keys, values, queries):
    chips = lax.axis_size("chip")
    blocks = chips // GROUPS
    ctx_rows, width = keys.shape
    gw = width // GROUPS
    heads = gw // HEAD_DIM
    layers, tok_rows, _ = queries.shape
    rows_q = layers * tok_rows
    rows_kv = ctx_rows // blocks

    def by_chip(array):
        return jnp.swapaxes(array.reshape(rows_kv, chips, gw), 0, 1)

    q = jnp.swapaxes(queries.reshape(rows_q, GROUPS, gw), 0, 1)
    q = jnp.broadcast_to(q[None], (blocks, GROUPS, rows_q, gw)).reshape(chips, rows_q, gw)
    packed = jnp.concatenate([by_chip(keys), by_chip(values), q], axis=1)
    got = lax.all_to_all(packed, "chip", split_axis=0, concat_axis=0, tiled=True)
    other = lax.ppermute(got[:, : 2 * rows_kv], "core", [(0, 1), (1, 0)])
    outs = partial_attend(got, other, rows_kv, rows_q)
    stats = [jnp.moveaxis(s[:, :, 0].reshape(heads, chips, rows_q), 0, 2) for s in outs[1:]]
    stats = jnp.concatenate(stats, axis=2)
    stats = jnp.pad(stats, ((0, 0), (0, 0), (0, -2 * heads % HEAD_DIM)))
    sent = jnp.concatenate([outs[0], stats], axis=2)
    back = lax.all_to_all(sent, "chip", split_axis=0, concat_axis=0, tiled=True)
    back = back.reshape(blocks, GROUPS, rows_q, -1)
    summed = back[..., :gw].reshape(blocks, GROUPS, rows_q, heads, HEAD_DIM)
    peak = back[..., gw : gw + heads]
    total = back[..., gw + heads : gw + 2 * heads]
    share = jnp.exp2(peak - jnp.max(peak, axis=0))
    denom = jnp.sum(share * total, axis=0)
    numer = jnp.sum(share[..., None] * summed, axis=0)
    result = (numer / denom[..., None]).astype(BF16)
    return jnp.swapaxes(result.reshape(GROUPS, rows_q, gw), 0, 1).reshape(layers, tok_rows, width)


def solution(mesh):
    rep, seq = mesh.shape["rep"], mesh.shape["seq"]
    chips = seq // 2
    by_core = Mesh(mesh.devices.reshape(rep, chips, 2), ("rep", "chip", "core"))
    rows = ("rep", "chip", "core")
    return jax.shard_map(
        local_permutes if chips == GROUPS else local_blocks,
        mesh=by_core,
        in_specs=(P(rows, None), P(rows, None), P(None, rows, None)),
        out_specs=P(None, rows, None),
        check_vma=False,
    )
```

```python
import functools
import math

import jax
import jax.numpy as jnp
from jax import lax
from jax.experimental import pallas as pl
from jax.experimental.pallas import tpu as pltpu
from jax.sharding import Mesh, PartitionSpec as P

HEAD_DIM = 128
GROUPS = 8
SUB = 128
F32 = jnp.float32
BF16 = jnp.bfloat16
VMEM = pl.BlockSpec(memory_space=pltpu.VMEM)
HBM = pl.BlockSpec(memory_space=pltpu.HBM)
SMEM = pl.BlockSpec(memory_space=pltpu.SMEM)
FREE = pl.CostEstimate(flops=0, bytes_accessed=0, transcendentals=0)
PARAMS = pltpu.CompilerParams(vmem_limit_bytes=40 * 2**20)


def softmax_rows(q, ka, va, kb, vb):
    factor = math.log2(math.e) / math.sqrt(HEAD_DIM)
    nt = (((1,), (1,)), ((), ()))
    sa = lax.dot_general(q, ka, nt, preferred_element_type=F32)
    sb = lax.dot_general(q, kb, nt, preferred_element_type=F32)
    peak = jnp.max(jnp.maximum(sa, sb), axis=1, keepdims=True)
    ea = jnp.exp2((sa - peak) * factor).astype(BF16)
    eb = jnp.exp2((sb - peak) * factor).astype(BF16)
    both = jnp.dot(ea, va, preferred_element_type=F32) + jnp.dot(eb, vb, preferred_element_type=F32)
    return both[:, :HEAD_DIM], peak * factor, both[:, HEAD_DIM:]


def beside_ones(v):
    return jnp.concatenate([v, jnp.ones_like(v)], axis=1)


LAST = 3
JOINED_BY = (0, 0)
FIRST = ((3, 0), (1, 0), (3, 1))
REST = ((2, 0), (1, 1), (0, 0), (2, 1), (0, 1))


def columns(at, dz, cross, gw):
    group = at[0][0] ^ (2 * dz + (at[1][0] ^ cross))
    return pl.ds(pl.multiple_of(group * gw, HEAD_DIM), gw)


def pack_body(rows, gw, layout, chip_ref, core_ref, *refs):
    at = chip_ref, core_ref
    arrays, out_refs, sems = refs[:3], refs[3:-1], refs[-1]
    copies = []
    for out_ref, (piece, parts) in zip(out_refs, layout):
        col = columns(at, *piece, gw)
        for first, n in enumerate(parts):
            to = out_ref.at[first * rows : (first + 1) * rows]
            copies.append(pltpu.make_async_copy(arrays[n].at[:, col], to, sems.at[len(copies)]))
    for copy in copies:
        copy.start()
    for copy in copies:
        copy.wait()


def merge_body(rows, *refs):
    out_ref = refs[-1]
    for n, piece in enumerate(refs[:-1]):
        for which in range(2):
            out_ref[which, n * rows : (n + 1) * rows] = piece[which * rows : (which + 1) * rows]


def unpack_body(gw, order, chip_ref, core_ref, *refs):
    at = chip_ref, core_ref
    pieces, out_ref, sems = refs[: len(order)], refs[-2], refs[-1]
    rows = out_ref.shape[0]
    copies = []
    for n, piece in enumerate(order):
        to = out_ref.at[:, columns(at, *piece, gw)]
        copies.append(pltpu.make_async_copy(pieces[n].at[:rows], to, sems.at[n]))
    for copy in copies:
        copy.start()
    for copy in copies:
        copy.wait()


def attend_body(count, rows, own, other, *refs):
    queries, outs = refs[:count], refs[count:]
    for h in range(own.shape[2] // HEAD_DIM):
        col = slice(h * HEAD_DIM, (h + 1) * HEAD_DIM)
        q = [r[...][:, col] if r.shape[0] == 2 * rows else r[2 * rows :, col] for r in queries]
        va, vb = beside_ones(own[1, :, col]), beside_ones(other[1, :, col])
        acc, _, total = softmax_rows(jnp.concatenate(q, axis=0), own[0, :, col], va, other[0, :, col], vb)
        acc = (acc / total).astype(BF16)
        for n, out in enumerate(outs):
            out[:, col] = acc[n * 2 * rows : (n + 1) * 2 * rows]


def local_permutes(keys, values, queries):
    chips = lax.axis_size("chip")
    rows, width = keys.shape
    gw = width // chips
    layers, tok_rows, _ = queries.shape
    rows_q = layers * tok_rows
    assert rows_q == rows
    at = [lax.axis_index(name).reshape(1).astype(jnp.int32) for name in ("chip", "core")]

    def across(array, dz, cross, back=False):
        senders = [(chip, core) for chip in range(chips) for core in range(2)]
        to = [(chip ^ (2 * dz + (core if back else core ^ cross)), core ^ cross) for chip, core in senders]
        pairs = [(2 * a + b, 2 * c + d) for (a, b), (c, d) in zip(senders, to)]
        return lax.ppermute(array, ("chip", "core"), pairs)

    def swap(array):
        return lax.ppermute(array, "core", [(0, 1), (1, 0)])

    def after(array, *others):
        return lax.optimization_barrier((array, *others))[0]

    def call(body, n_in, out_shape):
        return pl.pallas_call(
            body,
            in_specs=[VMEM] * n_in,
            out_specs=jax.tree.map(lambda _: VMEM, out_shape),
            out_shape=out_shape,
            compiler_params=PARAMS,
            cost_estimate=FREE,
        )

    def shape(*dims):
        return jax.ShapeDtypeStruct(dims, BF16)

    sources = [keys, values, queries.reshape(rows_q, width)]
    sources = [pltpu.with_memory_space_constraint(a, pltpu.HBM) for a in sources]

    def pack(layout, *others):
        arrays = lax.optimization_barrier((*sources, *others))[:3] if others else sources
        return pl.pallas_call(
            functools.partial(pack_body, rows, gw, layout),
            in_specs=[SMEM, SMEM, HBM, HBM, HBM],
            out_specs=[VMEM] * len(layout),
            out_shape=[shape(len(parts) * rows, gw) for _, parts in layout],
            scratch_shapes=[pltpu.SemaphoreType.DMA((sum(len(parts) for _, parts in layout),))],
            compiler_params=PARAMS,
            cost_estimate=FREE,
        )(*at, *arrays)

    layout = [(p, (0, 1) if p[0] == LAST else (0, 1, 2)) for p in FIRST + REST]
    layout += [((LAST, cross), (2,)) for cross in range(2)]
    packed = pack(layout[: len(FIRST)])
    packed += pack(layout[len(FIRST) :], packed[0])
    late = jnp.concatenate([packed[-2], swap(packed[-1])], axis=0)
    got = {}
    for p, piece in zip(FIRST + REST, packed):
        got[p] = across(after(piece, late) if p == JOINED_BY else piece, *p)
    own = call(functools.partial(merge_body, rows), chips, shape(2, chips * rows, gw))(*got.values())
    other = swap(own)
    late = across(late, LAST, 0)

    def attend(dzs, *others):
        pieces = [late] if dzs == (LAST,) else [got[dz, cross] for dz in dzs for cross in range(2)]
        count = len(pieces)
        pieces = lax.optimization_barrier((*pieces, *others))[:count] if others else pieces
        body = functools.partial(attend_body, count, rows)
        outs = call(body, 2 + count, [shape(2 * rows, gw)] * len(dzs))(own, other, *pieces)
        return dict(zip(dzs, outs))

    outs = attend((2,))
    outs |= attend((1, 0), outs[2])
    back = {(dz, 0): across(outs[dz], dz, 0) for dz in (2, 1, 0)}
    outs |= attend((LAST,), back[0, 0])
    for cross in (1, 0):
        back[LAST, cross] = across(outs[LAST][cross * rows : (cross + 1) * rows], LAST, cross, True)
    back |= {(dz, 1): swap(after(back[dz, 0], back[2, 0])[rows:]) for dz in (1, 0)}
    back[2, 1] = swap(back[2, 0][rows:])

    def unpack(dzs, *so_far):
        order = [(dz, cross) for dz in dzs for cross in range(2)]
        pieces = [back[piece] for piece in order]
        return pl.pallas_call(
            functools.partial(unpack_body, gw, order),
            in_specs=[SMEM, SMEM] + [VMEM] * len(order) + [HBM] * len(so_far),
            out_specs=HBM,
            out_shape=shape(rows_q, width),
            scratch_shapes=[pltpu.SemaphoreType.DMA((len(order),))],
            input_output_aliases={2 + len(order): 0} if so_far else {},
            compiler_params=PARAMS,
            cost_estimate=FREE,
        )(*at, *pieces, *so_far)

    result = unpack((LAST, 1, 0, 2))
    return result.reshape(layers, tok_rows, width)


def partial_head(q_ref, ka_ref, va_ref, kb_ref, vb_ref, o_ref, peak_ref, total_ref):
    src, rows, _ = q_ref.shape
    q = q_ref[...].reshape(src * rows, HEAD_DIM)
    ka, va, kb, vb = (r[...].reshape(-1, HEAD_DIM) for r in (ka_ref, va_ref, kb_ref, vb_ref))
    kv = ka, beside_ones(va), kb, beside_ones(vb)
    outs = []
    for at in range(0, src * rows, SUB):
        acc, peak, total = softmax_rows(q[at : at + SUB], *kv)
        outs.append(acc)
        peak_ref[at : at + SUB] = jnp.broadcast_to(peak, (SUB, HEAD_DIM))
        total_ref[at : at + SUB] = total
    o_ref[...] = jnp.concatenate(outs, axis=0).reshape(o_ref.shape)


def partial_attend(got, other, rows_kv, rows_q):
    chips, _, width = got.shape
    heads = width // HEAD_DIM
    own_kv = got[:, : 2 * rows_kv].reshape(chips, 2, rows_kv, width)
    own_q = got[:, 2 * rows_kv :]
    other = other.reshape(chips, 2, rows_kv, width)

    def kv(which):
        return pl.BlockSpec((chips, None, rows_kv, HEAD_DIM), lambda h: (0, which, 0, h))

    q_spec = pl.BlockSpec((chips, rows_q, HEAD_DIM), lambda h: (0, 0, h))
    stat_spec = pl.BlockSpec((None, chips * rows_q, HEAD_DIM), lambda h: (h, 0, 0))
    stat = jax.ShapeDtypeStruct((heads, chips * rows_q, HEAD_DIM), F32)
    return pl.pallas_call(
        partial_head,
        grid=(heads,),
        in_specs=[q_spec, kv(0), kv(1), kv(0), kv(1)],
        out_specs=[q_spec, stat_spec, stat_spec],
        out_shape=[jax.ShapeDtypeStruct((chips, rows_q, width), F32), stat, stat],
        compiler_params=PARAMS,
    )(own_q, own_kv, own_kv, other, other)


def local_blocks(keys, values, queries):
    chips = lax.axis_size("chip")
    blocks = chips // GROUPS
    ctx_rows, width = keys.shape
    gw = width // GROUPS
    heads = gw // HEAD_DIM
    layers, tok_rows, _ = queries.shape
    rows_q = layers * tok_rows
    rows_kv = ctx_rows // blocks

    def by_chip(array):
        return jnp.swapaxes(array.reshape(rows_kv, chips, gw), 0, 1)

    q = jnp.swapaxes(queries.reshape(rows_q, GROUPS, gw), 0, 1)
    q = jnp.broadcast_to(q[None], (blocks, GROUPS, rows_q, gw)).reshape(chips, rows_q, gw)
    packed = jnp.concatenate([by_chip(keys), by_chip(values), q], axis=1)
    got = lax.all_to_all(packed, "chip", split_axis=0, concat_axis=0, tiled=True)
    other = lax.ppermute(got[:, : 2 * rows_kv], "core", [(0, 1), (1, 0)])
    outs = partial_attend(got, other, rows_kv, rows_q)
    stats = [jnp.moveaxis(s[:, :, 0].reshape(heads, chips, rows_q), 0, 2) for s in outs[1:]]
    stats = jnp.concatenate(stats, axis=2)
    stats = jnp.pad(stats, ((0, 0), (0, 0), (0, -2 * heads % HEAD_DIM)))
    sent = jnp.concatenate([outs[0], stats], axis=2)
    back = lax.all_to_all(sent, "chip", split_axis=0, concat_axis=0, tiled=True)
    back = back.reshape(blocks, GROUPS, rows_q, -1)
    summed = back[..., :gw].reshape(blocks, GROUPS, rows_q, heads, HEAD_DIM)
    peak = back[..., gw : gw + heads]
    total = back[..., gw + heads : gw + 2 * heads]
    share = jnp.exp2(peak - jnp.max(peak, axis=0))
    denom = jnp.sum(share * total, axis=0)
    numer = jnp.sum(share[..., None] * summed, axis=0)
    result = (numer / denom[..., None]).astype(BF16)
    return jnp.swapaxes(result.reshape(GROUPS, rows_q, gw), 0, 1).reshape(layers, tok_rows, width)


def solution(mesh):
    rep, seq = mesh.shape["rep"], mesh.shape["seq"]
    chips = seq // 2
    by_core = Mesh(mesh.devices.reshape(rep, chips, 2), ("rep", "chip", "core"))
    rows = ("rep", "chip", "core")
    return jax.shard_map(
        local_permutes if chips == GROUPS else local_blocks,
        mesh=by_core,
        in_specs=(P(rows, None), P(rows, None), P(None, rows, None)),
        out_specs=P(None, rows, None),
        check_vma=False,
    )
```

```python
import functools
import math

import jax
import jax.numpy as jnp
from jax import lax
from jax.experimental import pallas as pl
from jax.experimental.pallas import tpu as pltpu
from jax.sharding import Mesh, PartitionSpec as P

HEAD_DIM = 128
GROUPS = 8
SUB = 128
F32 = jnp.float32
BF16 = jnp.bfloat16
VMEM = pl.BlockSpec(memory_space=pltpu.VMEM)
HBM = pl.BlockSpec(memory_space=pltpu.HBM)
SMEM = pl.BlockSpec(memory_space=pltpu.SMEM)
FREE = pl.CostEstimate(flops=0, bytes_accessed=0, transcendentals=0)
PARAMS = pltpu.CompilerParams(vmem_limit_bytes=40 * 2**20)


def softmax_rows(q, ka, va, kb, vb):
    factor = math.log2(math.e) / math.sqrt(HEAD_DIM)
    nt = (((1,), (1,)), ((), ()))
    sa = lax.dot_general(q, ka, nt, preferred_element_type=F32)
    sb = lax.dot_general(q, kb, nt, preferred_element_type=F32)
    peak = jnp.max(jnp.maximum(sa, sb), axis=1, keepdims=True)
    ea = jnp.exp2((sa - peak) * factor).astype(BF16)
    eb = jnp.exp2((sb - peak) * factor).astype(BF16)
    both = jnp.dot(ea, va, preferred_element_type=F32) + jnp.dot(eb, vb, preferred_element_type=F32)
    return both[:, :HEAD_DIM], peak * factor, both[:, HEAD_DIM:]


def beside_ones(v):
    return jnp.concatenate([v, jnp.ones_like(v)], axis=1)


LAST = 3
JOINED_BY = (0, 0)
FIRST = ((3, 0), (1, 0), (3, 1))
REST = ((2, 0), (1, 1), (0, 0), (2, 1), (0, 1))


def columns(at, dz, cross, gw):
    group = at[0][0] ^ (2 * dz + (at[1][0] ^ cross))
    return pl.ds(pl.multiple_of(group * gw, HEAD_DIM), gw)


def pack_body(rows, gw, layout, chip_ref, core_ref, *refs):
    at = chip_ref, core_ref
    arrays, out_refs, sems = refs[:3], refs[3:-1], refs[-1]
    copies = []
    for out_ref, (piece, parts) in zip(out_refs, layout):
        col = columns(at, *piece, gw)
        for first, n in enumerate(parts):
            to = out_ref.at[first * rows : (first + 1) * rows]
            copies.append(pltpu.make_async_copy(arrays[n].at[:, col], to, sems.at[len(copies)]))
    for copy in copies:
        copy.start()
    for copy in copies:
        copy.wait()


def merge_body(rows, *refs):
    out_ref = refs[-1]
    for n, piece in enumerate(refs[:-1]):
        for which in range(2):
            out_ref[which, n * rows : (n + 1) * rows] = piece[which * rows : (which + 1) * rows]


def unpack_body(gw, order, chip_ref, core_ref, *refs):
    at = chip_ref, core_ref
    pieces, out_ref, sems = refs[: len(order)], refs[-2], refs[-1]
    rows = out_ref.shape[0]
    copies = []
    for n, piece in enumerate(order):
        to = out_ref.at[:, columns(at, *piece, gw)]
        copies.append(pltpu.make_async_copy(pieces[n].at[:rows], to, sems.at[n]))
    for copy in copies:
        copy.start()
    for copy in copies:
        copy.wait()


def attend_body(count, rows, own, other, *refs):
    queries, outs = refs[:count], refs[count:]
    for h in range(own.shape[2] // HEAD_DIM):
        col = slice(h * HEAD_DIM, (h + 1) * HEAD_DIM)
        q = [r[...][:, col] if r.shape[0] == 2 * rows else r[2 * rows :, col] for r in queries]
        va, vb = beside_ones(own[1, :, col]), beside_ones(other[1, :, col])
        acc, _, total = softmax_rows(jnp.concatenate(q, axis=0), own[0, :, col], va, other[0, :, col], vb)
        acc = (acc / total).astype(BF16)
        for n, out in enumerate(outs):
            out[:, col] = acc[n * 2 * rows : (n + 1) * 2 * rows]


def local_permutes(keys, values, queries):
    chips = lax.axis_size("chip")
    rows, width = keys.shape
    gw = width // chips
    layers, tok_rows, _ = queries.shape
    rows_q = layers * tok_rows
    assert rows_q == rows
    at = [lax.axis_index(name).reshape(1).astype(jnp.int32) for name in ("chip", "core")]

    def across(array, dz, cross, back=False):
        senders = [(chip, core) for chip in range(chips) for core in range(2)]
        to = [(chip ^ (2 * dz + (core if back else core ^ cross)), core ^ cross) for chip, core in senders]
        pairs = [(2 * a + b, 2 * c + d) for (a, b), (c, d) in zip(senders, to)]
        return lax.ppermute(array, ("chip", "core"), pairs)

    def swap(array):
        return lax.ppermute(array, "core", [(0, 1), (1, 0)])

    def after(array, *others):
        return lax.optimization_barrier((array, *others))[0]

    def call(body, n_in, out_shape):
        return pl.pallas_call(
            body,
            in_specs=[VMEM] * n_in,
            out_specs=jax.tree.map(lambda _: VMEM, out_shape),
            out_shape=out_shape,
            compiler_params=PARAMS,
            cost_estimate=FREE,
        )

    def shape(*dims):
        return jax.ShapeDtypeStruct(dims, BF16)

    sources = [keys, values, queries.reshape(rows_q, width)]
    sources = [pltpu.with_memory_space_constraint(a, pltpu.HBM) for a in sources]

    def pack(layout, *others):
        arrays = lax.optimization_barrier((*sources, *others))[:3] if others else sources
        return pl.pallas_call(
            functools.partial(pack_body, rows, gw, layout),
            in_specs=[SMEM, SMEM, HBM, HBM, HBM],
            out_specs=[VMEM] * len(layout),
            out_shape=[shape(len(parts) * rows, gw) for _, parts in layout],
            scratch_shapes=[pltpu.SemaphoreType.DMA((sum(len(parts) for _, parts in layout),))],
            compiler_params=PARAMS,
            cost_estimate=FREE,
        )(*at, *arrays)

    layout = [(p, (0, 1) if p[0] == LAST else (0, 1, 2)) for p in FIRST + REST]
    layout += [((LAST, cross), (2,)) for cross in range(2)]
    packed = pack(layout[: len(FIRST)])
    packed += pack(layout[len(FIRST) :], packed[0])
    late = jnp.concatenate([packed[-2], swap(packed[-1])], axis=0)
    got = {}
    for p, piece in zip(FIRST + REST, packed):
        got[p] = across(after(piece, late) if p == JOINED_BY else piece, *p)
    own = call(functools.partial(merge_body, rows), chips, shape(2, chips * rows, gw))(*got.values())
    other = swap(own)
    late = across(late, LAST, 0)

    def attend(dzs, *others):
        pieces = [late] if dzs == (LAST,) else [got[dz, cross] for dz in dzs for cross in range(2)]
        count = len(pieces)
        pieces = lax.optimization_barrier((*pieces, *others))[:count] if others else pieces
        body = functools.partial(attend_body, count, rows)
        outs = call(body, 2 + count, [shape(2 * rows, gw)] * len(dzs))(own, other, *pieces)
        return dict(zip(dzs, outs))

    outs = attend((2,))
    outs |= attend((1, 0), outs[2])
    back = {(dz, 0): across(outs[dz], dz, 0) for dz in (2, 1, 0)}
    outs |= attend((LAST,), back[0, 0])
    back[LAST, 0] = across(outs[LAST], LAST, 0)
    back |= {(dz, 1): swap(after(back[dz, 0], back[2, 0])[rows:]) for dz in (1, 0)}
    back[2, 1] = swap(back[2, 0][rows:])

    def unpack(dzs, *so_far):
        order = [(dz, cross) for dz in dzs for cross in range(2)]
        pieces = [back[piece] for piece in order]
        return pl.pallas_call(
            functools.partial(unpack_body, gw, order),
            in_specs=[SMEM, SMEM] + [VMEM] * len(order) + [HBM] * len(so_far),
            out_specs=HBM,
            out_shape=shape(rows_q, width),
            scratch_shapes=[pltpu.SemaphoreType.DMA((len(order),))],
            input_output_aliases={2 + len(order): 0} if so_far else {},
            compiler_params=PARAMS,
            cost_estimate=FREE,
        )(*at, *pieces, *so_far)

    result = unpack((1, 0, 2))
    back[LAST, 1] = swap(after(back[LAST, 0], result)[rows:])
    result = unpack((LAST,), result)
    return result.reshape(layers, tok_rows, width)


def partial_head(q_ref, ka_ref, va_ref, kb_ref, vb_ref, o_ref, peak_ref, total_ref):
    src, rows, _ = q_ref.shape
    q = q_ref[...].reshape(src * rows, HEAD_DIM)
    ka, va, kb, vb = (r[...].reshape(-1, HEAD_DIM) for r in (ka_ref, va_ref, kb_ref, vb_ref))
    kv = ka, beside_ones(va), kb, beside_ones(vb)
    outs = []
    for at in range(0, src * rows, SUB):
        acc, peak, total = softmax_rows(q[at : at + SUB], *kv)
        outs.append(acc)
        peak_ref[at : at + SUB] = jnp.broadcast_to(peak, (SUB, HEAD_DIM))
        total_ref[at : at + SUB] = total
    o_ref[...] = jnp.concatenate(outs, axis=0).reshape(o_ref.shape)


def partial_attend(got, other, rows_kv, rows_q):
    chips, _, width = got.shape
    heads = width // HEAD_DIM
    own_kv = got[:, : 2 * rows_kv].reshape(chips, 2, rows_kv, width)
    own_q = got[:, 2 * rows_kv :]
    other = other.reshape(chips, 2, rows_kv, width)

    def kv(which):
        return pl.BlockSpec((chips, None, rows_kv, HEAD_DIM), lambda h: (0, which, 0, h))

    q_spec = pl.BlockSpec((chips, rows_q, HEAD_DIM), lambda h: (0, 0, h))
    stat_spec = pl.BlockSpec((None, chips * rows_q, HEAD_DIM), lambda h: (h, 0, 0))
    stat = jax.ShapeDtypeStruct((heads, chips * rows_q, HEAD_DIM), F32)
    return pl.pallas_call(
        partial_head,
        grid=(heads,),
        in_specs=[q_spec, kv(0), kv(1), kv(0), kv(1)],
        out_specs=[q_spec, stat_spec, stat_spec],
        out_shape=[jax.ShapeDtypeStruct((chips, rows_q, width), F32), stat, stat],
        compiler_params=PARAMS,
    )(own_q, own_kv, own_kv, other, other)


def local_blocks(keys, values, queries):
    chips = lax.axis_size("chip")
    blocks = chips // GROUPS
    ctx_rows, width = keys.shape
    gw = width // GROUPS
    heads = gw // HEAD_DIM
    layers, tok_rows, _ = queries.shape
    rows_q = layers * tok_rows
    rows_kv = ctx_rows // blocks

    def by_chip(array):
        return jnp.swapaxes(array.reshape(rows_kv, chips, gw), 0, 1)

    q = jnp.swapaxes(queries.reshape(rows_q, GROUPS, gw), 0, 1)
    q = jnp.broadcast_to(q[None], (blocks, GROUPS, rows_q, gw)).reshape(chips, rows_q, gw)
    packed = jnp.concatenate([by_chip(keys), by_chip(values), q], axis=1)
    got = lax.all_to_all(packed, "chip", split_axis=0, concat_axis=0, tiled=True)
    other = lax.ppermute(got[:, : 2 * rows_kv], "core", [(0, 1), (1, 0)])
    outs = partial_attend(got, other, rows_kv, rows_q)
    stats = [jnp.moveaxis(s[:, :, 0].reshape(heads, chips, rows_q), 0, 2) for s in outs[1:]]
    stats = jnp.concatenate(stats, axis=2)
    stats = jnp.pad(stats, ((0, 0), (0, 0), (0, -2 * heads % HEAD_DIM)))
    sent = jnp.concatenate([outs[0], stats], axis=2)
    back = lax.all_to_all(sent, "chip", split_axis=0, concat_axis=0, tiled=True)
    back = back.reshape(blocks, GROUPS, rows_q, -1)
    summed = back[..., :gw].reshape(blocks, GROUPS, rows_q, heads, HEAD_DIM)
    peak = back[..., gw : gw + heads]
    total = back[..., gw + heads : gw + 2 * heads]
    share = jnp.exp2(peak - jnp.max(peak, axis=0))
    denom = jnp.sum(share * total, axis=0)
    numer = jnp.sum(share[..., None] * summed, axis=0)
    result = (numer / denom[..., None]).astype(BF16)
    return jnp.swapaxes(result.reshape(GROUPS, rows_q, gw), 0, 1).reshape(layers, tok_rows, width)


def solution(mesh):
    rep, seq = mesh.shape["rep"], mesh.shape["seq"]
    chips = seq // 2
    by_core = Mesh(mesh.devices.reshape(rep, chips, 2), ("rep", "chip", "core"))
    rows = ("rep", "chip", "core")
    return jax.shard_map(
        local_permutes if chips == GROUPS else local_blocks,
        mesh=by_core,
        in_specs=(P(rows, None), P(rows, None), P(None, rows, None)),
        out_specs=P(None, rows, None),
        check_vma=False,
    )
```

```python
import functools
import math

import jax
import jax.numpy as jnp
from jax import lax
from jax.experimental import pallas as pl
from jax.experimental.pallas import tpu as pltpu
from jax.sharding import Mesh, PartitionSpec as P

HEAD_DIM = 128
GROUPS = 8
SUB = 128
F32 = jnp.float32
BF16 = jnp.bfloat16
VMEM = pl.BlockSpec(memory_space=pltpu.VMEM)
HBM = pl.BlockSpec(memory_space=pltpu.HBM)
SMEM = pl.BlockSpec(memory_space=pltpu.SMEM)
FREE = pl.CostEstimate(flops=0, bytes_accessed=0, transcendentals=0)
PARAMS = pltpu.CompilerParams(vmem_limit_bytes=40 * 2**20)


def softmax_rows(q, ka, va, kb, vb):
    factor = math.log2(math.e) / math.sqrt(HEAD_DIM)
    nt = (((1,), (1,)), ((), ()))
    sa = lax.dot_general(q, ka, nt, preferred_element_type=F32)
    sb = lax.dot_general(q, kb, nt, preferred_element_type=F32)
    peak = jnp.max(jnp.maximum(sa, sb), axis=1, keepdims=True)
    ea = jnp.exp2((sa - peak) * factor).astype(BF16)
    eb = jnp.exp2((sb - peak) * factor).astype(BF16)
    both = jnp.dot(ea, va, preferred_element_type=F32) + jnp.dot(eb, vb, preferred_element_type=F32)
    return both[:, :HEAD_DIM], peak * factor, both[:, HEAD_DIM:]


def beside_ones(v):
    return jnp.concatenate([v, jnp.ones_like(v)], axis=1)


FIRST = (6, 2, 7)
REST = (4, 3, 1, 5, 0)
LAST = (6, 7)
NEAR = (2, 3, 1)


def pack_body(rows, gw, layout, chip_ref, *refs):
    arrays, out_refs, sems = refs[:3], refs[3:-1], refs[-1]
    copies = []
    for out_ref, (k, parts) in zip(out_refs, layout):
        col = pl.ds(pl.multiple_of((chip_ref[0] ^ k) * gw, HEAD_DIM), gw)
        for at, n in enumerate(parts):
            to = out_ref.at[at * rows : (at + 1) * rows]
            copies.append(pltpu.make_async_copy(arrays[n].at[:, col], to, sems.at[len(copies)]))
    for copy in copies:
        copy.start()
    for copy in copies:
        copy.wait()


def merge_body(rows, *refs):
    out_ref = refs[-1]
    for n, piece in enumerate(refs[:-1]):
        for which in range(2):
            out_ref[which, n * rows : (n + 1) * rows] = piece[which * rows : (which + 1) * rows]


def unpack_body(gw, order, chip_ref, *refs):
    pieces, out_ref, sems = refs[: len(order)], refs[-2], refs[-1]
    copies = []
    for n, k in enumerate(order):
        col = pl.ds(pl.multiple_of((chip_ref[0] ^ k) * gw, HEAD_DIM), gw)
        copies.append(pltpu.make_async_copy(pieces[n], out_ref.at[:, col], sems.at[n]))
    for copy in copies:
        copy.start()
    for copy in copies:
        copy.wait()


def attend_body(count, rows, own, other, *refs):
    queries, outs = refs[:count], refs[count:]
    for h in range(own.shape[2] // HEAD_DIM):
        col = slice(h * HEAD_DIM, (h + 1) * HEAD_DIM)
        q = jnp.concatenate([r[r.shape[0] - rows :, col] for r in queries], axis=0)
        va, vb = beside_ones(own[1, :, col]), beside_ones(other[1, :, col])
        acc, _, total = softmax_rows(q, own[0, :, col], va, other[0, :, col], vb)
        acc = (acc / total).astype(BF16)
        for n, out in enumerate(outs):
            out[:, col] = acc[n * rows : (n + 1) * rows]


def local_permutes(keys, values, queries):
    chips = lax.axis_size("chip")
    rows, width = keys.shape
    gw = width // chips
    layers, tok_rows, _ = queries.shape
    rows_q = layers * tok_rows
    assert rows_q == rows
    chip = lax.axis_index("chip").reshape(1).astype(jnp.int32)

    def across(piece, k):
        return lax.ppermute(piece, "chip", [(i, i ^ k) for i in range(chips)]) if k else piece

    def call(body, n_in, out_shape, smem=0, **more):
        return pl.pallas_call(
            body,
            in_specs=[SMEM] * smem + [VMEM] * n_in,
            out_specs=jax.tree.map(lambda _: VMEM, out_shape),
            out_shape=out_shape,
            compiler_params=PARAMS,
            cost_estimate=FREE,
            **more,
        )

    def shape(*dims):
        return jax.ShapeDtypeStruct(dims, BF16)

    sources = [keys, values, queries.reshape(rows_q, width)]
    sources = [pltpu.with_memory_space_constraint(a, pltpu.HBM) for a in sources]

    def pack(layout, after=()):
        arrays = lax.optimization_barrier((*sources, *after))[:3] if after else sources
        return pl.pallas_call(
            functools.partial(pack_body, rows, gw, layout),
            in_specs=[SMEM, HBM, HBM, HBM],
            out_specs=[VMEM] * len(layout),
            out_shape=[shape(len(parts) * rows, gw) for _, parts in layout],
            scratch_shapes=[pltpu.SemaphoreType.DMA((sum(len(parts) for _, parts in layout),))],
            compiler_params=PARAMS,
            cost_estimate=FREE,
        )(chip, *arrays)

    layout = [(k, (0, 1) if k in LAST else (0, 1, 2)) for k in FIRST + REST]
    layout += [(k, (2,)) for k in LAST]
    packed = pack(layout[: len(FIRST)])
    packed += pack(layout[len(FIRST) :], packed[:1])
    got = [across(piece, k) for piece, (k, _) in zip(packed, layout)]
    late = dict(zip(LAST, got[chips:]))
    got = {k: piece for piece, (k, _) in zip(got[:chips], layout)}
    own = call(functools.partial(merge_body, rows), chips, shape(2, chips * rows, gw))(*got.values())
    other = lax.ppermute(own, "core", [(0, 1), (1, 0)])

    def attend(ks, after=()):
        pieces = [late.get(k, got[k]) for k in ks]
        if after:
            pieces = lax.optimization_barrier((*pieces, *after))[: len(pieces)]
        body = functools.partial(attend_body, len(ks), rows)
        outs = call(body, 2 + len(ks), [shape(rows, gw)] * len(ks))(own, other, *pieces)
        return dict(zip(ks, outs))

    outs = attend((4, 5))
    outs |= attend(NEAR + (0,), (outs[4],))
    outs |= attend(LAST, (outs[0],))
    back = {k: across(outs[k], k) for k in (4, 5, 1) + LAST + (0,)}
    def after(array, *others):
        return lax.optimization_barrier((array, *others))[0]

    back[2] = across(after(outs[2], outs[LAST[0]]), 2)
    back[3] = across(after(outs[3], outs[LAST[0]], back[5]), 3)

    def unpack(order, so_far=()):
        return pl.pallas_call(
            functools.partial(unpack_body, gw, order),
            in_specs=[SMEM] + [VMEM] * len(order) + [HBM] * len(so_far),
            out_specs=HBM,
            out_shape=shape(rows_q, width),
            scratch_shapes=[pltpu.SemaphoreType.DMA((len(order),))],
            input_output_aliases={1 + len(order): 0} if so_far else {},
            compiler_params=PARAMS,
            cost_estimate=FREE,
        )(chip, *[back[k] for k in order], *so_far)

    result = unpack(LAST + (3, 2), (unpack((0, 4, 5, 1)),))
    return result.reshape(layers, tok_rows, width)


def partial_head(q_ref, ka_ref, va_ref, kb_ref, vb_ref, o_ref, peak_ref, total_ref):
    src, rows, _ = q_ref.shape
    q = q_ref[...].reshape(src * rows, HEAD_DIM)
    ka, va, kb, vb = (r[...].reshape(-1, HEAD_DIM) for r in (ka_ref, va_ref, kb_ref, vb_ref))
    kv = ka, beside_ones(va), kb, beside_ones(vb)
    outs = []
    for at in range(0, src * rows, SUB):
        acc, peak, total = softmax_rows(q[at : at + SUB], *kv)
        outs.append(acc)
        peak_ref[at : at + SUB] = jnp.broadcast_to(peak, (SUB, HEAD_DIM))
        total_ref[at : at + SUB] = total
    o_ref[...] = jnp.concatenate(outs, axis=0).reshape(o_ref.shape)


def partial_attend(got, other, rows_kv, rows_q):
    chips, _, width = got.shape
    heads = width // HEAD_DIM
    own_kv = got[:, : 2 * rows_kv].reshape(chips, 2, rows_kv, width)
    own_q = got[:, 2 * rows_kv :]
    other = other.reshape(chips, 2, rows_kv, width)

    def kv(which):
        return pl.BlockSpec((chips, None, rows_kv, HEAD_DIM), lambda h: (0, which, 0, h))

    q_spec = pl.BlockSpec((chips, rows_q, HEAD_DIM), lambda h: (0, 0, h))
    stat_spec = pl.BlockSpec((None, chips * rows_q, HEAD_DIM), lambda h: (h, 0, 0))
    stat = jax.ShapeDtypeStruct((heads, chips * rows_q, HEAD_DIM), F32)
    return pl.pallas_call(
        partial_head,
        grid=(heads,),
        in_specs=[q_spec, kv(0), kv(1), kv(0), kv(1)],
        out_specs=[q_spec, stat_spec, stat_spec],
        out_shape=[jax.ShapeDtypeStruct((chips, rows_q, width), F32), stat, stat],
        compiler_params=PARAMS,
    )(own_q, own_kv, own_kv, other, other)


def local_blocks(keys, values, queries):
    chips = lax.axis_size("chip")
    blocks = chips // GROUPS
    ctx_rows, width = keys.shape
    gw = width // GROUPS
    heads = gw // HEAD_DIM
    layers, tok_rows, _ = queries.shape
    rows_q = layers * tok_rows
    rows_kv = ctx_rows // blocks

    def by_chip(array):
        return jnp.swapaxes(array.reshape(rows_kv, chips, gw), 0, 1)

    q = jnp.swapaxes(queries.reshape(rows_q, GROUPS, gw), 0, 1)
    q = jnp.broadcast_to(q[None], (blocks, GROUPS, rows_q, gw)).reshape(chips, rows_q, gw)
    packed = jnp.concatenate([by_chip(keys), by_chip(values), q], axis=1)
    got = lax.all_to_all(packed, "chip", split_axis=0, concat_axis=0, tiled=True)
    other = lax.ppermute(got[:, : 2 * rows_kv], "core", [(0, 1), (1, 0)])
    outs = partial_attend(got, other, rows_kv, rows_q)
    stats = [jnp.moveaxis(s[:, :, 0].reshape(heads, chips, rows_q), 0, 2) for s in outs[1:]]
    stats = jnp.concatenate(stats, axis=2)
    stats = jnp.pad(stats, ((0, 0), (0, 0), (0, -2 * heads % HEAD_DIM)))
    sent = jnp.concatenate([outs[0], stats], axis=2)
    back = lax.all_to_all(sent, "chip", split_axis=0, concat_axis=0, tiled=True)
    back = back.reshape(blocks, GROUPS, rows_q, -1)
    summed = back[..., :gw].reshape(blocks, GROUPS, rows_q, heads, HEAD_DIM)
    peak = back[..., gw : gw + heads]
    total = back[..., gw + heads : gw + 2 * heads]
    share = jnp.exp2(peak - jnp.max(peak, axis=0))
    denom = jnp.sum(share * total, axis=0)
    numer = jnp.sum(share[..., None] * summed, axis=0)
    result = (numer / denom[..., None]).astype(BF16)
    return jnp.swapaxes(result.reshape(GROUPS, rows_q, gw), 0, 1).reshape(layers, tok_rows, width)


def solution(mesh):
    rep, seq = mesh.shape["rep"], mesh.shape["seq"]
    chips = seq // 2
    by_core = Mesh(mesh.devices.reshape(rep, chips, 2), ("rep", "chip", "core"))
    rows = ("rep", "chip", "core")
    return jax.shard_map(
        local_permutes if chips == GROUPS else local_blocks,
        mesh=by_core,
        in_specs=(P(rows, None), P(rows, None), P(None, rows, None)),
        out_specs=P(None, rows, None),
        check_vma=False,
    )
```

```python
import functools
import math

import jax
import jax.numpy as jnp
from jax import lax
from jax.experimental import pallas as pl
from jax.experimental.pallas import tpu as pltpu
from jax.sharding import Mesh, PartitionSpec as P

HEAD_DIM = 128
GROUPS = 8
SUB = 128
F32 = jnp.float32
BF16 = jnp.bfloat16
VMEM = pl.BlockSpec(memory_space=pltpu.VMEM)
HBM = pl.BlockSpec(memory_space=pltpu.HBM)
SMEM = pl.BlockSpec(memory_space=pltpu.SMEM)
FREE = pl.CostEstimate(flops=0, bytes_accessed=0, transcendentals=0)
PARAMS = pltpu.CompilerParams(vmem_limit_bytes=40 * 2**20)


def softmax_rows(q, ka, va, kb, vb):
    factor = math.log2(math.e) / math.sqrt(HEAD_DIM)
    nt = (((1,), (1,)), ((), ()))
    sa = lax.dot_general(q, ka, nt, preferred_element_type=F32)
    sb = lax.dot_general(q, kb, nt, preferred_element_type=F32)
    peak = jnp.max(jnp.maximum(sa, sb), axis=1, keepdims=True)
    ea = jnp.exp2((sa - peak) * factor).astype(BF16)
    eb = jnp.exp2((sb - peak) * factor).astype(BF16)
    both = jnp.dot(ea, va, preferred_element_type=F32) + jnp.dot(eb, vb, preferred_element_type=F32)
    return both[:, :HEAD_DIM], peak * factor, both[:, HEAD_DIM:]


def beside_ones(v):
    return jnp.concatenate([v, jnp.ones_like(v)], axis=1)


FIRST = (6, 2, 7)
REST = (4, 5, 3, 1, 0)
LAST = (6, 7)
NEAR = (2, 3, 1)


def pack_body(rows, gw, layout, chip_ref, *refs):
    arrays, out_refs, sems = refs[:3], refs[3:-1], refs[-1]
    copies = []
    for out_ref, (k, parts) in zip(out_refs, layout):
        col = pl.ds(pl.multiple_of((chip_ref[0] ^ k) * gw, HEAD_DIM), gw)
        for at, n in enumerate(parts):
            to = out_ref.at[at * rows : (at + 1) * rows]
            copies.append(pltpu.make_async_copy(arrays[n].at[:, col], to, sems.at[len(copies)]))
    for copy in copies:
        copy.start()
    for copy in copies:
        copy.wait()


def merge_body(rows, *refs):
    out_ref = refs[-1]
    for n, piece in enumerate(refs[:-1]):
        for which in range(2):
            out_ref[which, n * rows : (n + 1) * rows] = piece[which * rows : (which + 1) * rows]


def unpack_body(gw, order, chip_ref, *refs):
    pieces, out_ref, sems = refs[: len(order)], refs[-2], refs[-1]
    copies = []
    for n, k in enumerate(order):
        col = pl.ds(pl.multiple_of((chip_ref[0] ^ k) * gw, HEAD_DIM), gw)
        copies.append(pltpu.make_async_copy(pieces[n], out_ref.at[:, col], sems.at[n]))
    for copy in copies:
        copy.start()
    for copy in copies:
        copy.wait()


def attend_body(count, rows, own, other, *refs):
    queries, outs = refs[:count], refs[count:]
    for h in range(own.shape[2] // HEAD_DIM):
        col = slice(h * HEAD_DIM, (h + 1) * HEAD_DIM)
        q = jnp.concatenate([r[r.shape[0] - rows :, col] for r in queries], axis=0)
        va, vb = beside_ones(own[1, :, col]), beside_ones(other[1, :, col])
        acc, _, total = softmax_rows(q, own[0, :, col], va, other[0, :, col], vb)
        acc = (acc / total).astype(BF16)
        for n, out in enumerate(outs):
            out[:, col] = acc[n * rows : (n + 1) * rows]


def local_permutes(keys, values, queries):
    chips = lax.axis_size("chip")
    rows, width = keys.shape
    gw = width // chips
    layers, tok_rows, _ = queries.shape
    rows_q = layers * tok_rows
    assert rows_q == rows
    chip = lax.axis_index("chip").reshape(1).astype(jnp.int32)

    def across(piece, k):
        return lax.ppermute(piece, "chip", [(i, i ^ k) for i in range(chips)]) if k else piece

    def call(body, n_in, out_shape, smem=0, **more):
        return pl.pallas_call(
            body,
            in_specs=[SMEM] * smem + [VMEM] * n_in,
            out_specs=jax.tree.map(lambda _: VMEM, out_shape),
            out_shape=out_shape,
            compiler_params=PARAMS,
            cost_estimate=FREE,
            **more,
        )

    def shape(*dims):
        return jax.ShapeDtypeStruct(dims, BF16)

    sources = [keys, values, queries.reshape(rows_q, width)]
    sources = [pltpu.with_memory_space_constraint(a, pltpu.HBM) for a in sources]

    def pack(layout, after=()):
        arrays = lax.optimization_barrier((*sources, *after))[:3] if after else sources
        return pl.pallas_call(
            functools.partial(pack_body, rows, gw, layout),
            in_specs=[SMEM, HBM, HBM, HBM],
            out_specs=[VMEM] * len(layout),
            out_shape=[shape(len(parts) * rows, gw) for _, parts in layout],
            scratch_shapes=[pltpu.SemaphoreType.DMA((sum(len(parts) for _, parts in layout),))],
            compiler_params=PARAMS,
            cost_estimate=FREE,
        )(chip, *arrays)

    layout = [(k, (0, 1) if k in LAST else (0, 1, 2)) for k in FIRST + REST]
    layout += [(k, (2,)) for k in LAST]
    packed = pack(layout[: len(FIRST)])
    packed += pack(layout[len(FIRST) :], packed[:1])
    got = [across(piece, k) for piece, (k, _) in zip(packed, layout)]
    late = dict(zip(LAST, got[chips:]))
    got = {k: piece for piece, (k, _) in zip(got[:chips], layout)}
    own = call(functools.partial(merge_body, rows), chips, shape(2, chips * rows, gw))(*got.values())
    other = lax.ppermute(own, "core", [(0, 1), (1, 0)])

    def attend(ks, after=()):
        pieces = [late.get(k, got[k]) for k in ks]
        if after:
            pieces = lax.optimization_barrier((*pieces, *after))[: len(pieces)]
        body = functools.partial(attend_body, len(ks), rows)
        outs = call(body, 2 + len(ks), [shape(rows, gw)] * len(ks))(own, other, *pieces)
        return dict(zip(ks, outs))

    outs = attend((4, 5))
    outs |= attend(NEAR + (0,), (outs[4],))
    outs |= attend(LAST, (outs[0],))
    back = {k: across(outs[k], k) for k in (4, 5, 1) + LAST + (0,)}
    def after(array, *others):
        return lax.optimization_barrier((array, *others))[0]

    back[2] = across(after(outs[2], outs[LAST[0]]), 2)
    back[3] = across(after(outs[3], outs[LAST[0]], back[5]), 3)

    def unpack(order, so_far=()):
        return pl.pallas_call(
            functools.partial(unpack_body, gw, order),
            in_specs=[SMEM] + [VMEM] * len(order) + [HBM] * len(so_far),
            out_specs=HBM,
            out_shape=shape(rows_q, width),
            scratch_shapes=[pltpu.SemaphoreType.DMA((len(order),))],
            input_output_aliases={1 + len(order): 0} if so_far else {},
            compiler_params=PARAMS,
            cost_estimate=FREE,
        )(chip, *[back[k] for k in order], *so_far)

    result = unpack(LAST + (3, 2), (unpack((0, 4, 5, 1)),))
    return result.reshape(layers, tok_rows, width)


def partial_head(q_ref, ka_ref, va_ref, kb_ref, vb_ref, o_ref, peak_ref, total_ref):
    src, rows, _ = q_ref.shape
    q = q_ref[...].reshape(src * rows, HEAD_DIM)
    ka, va, kb, vb = (r[...].reshape(-1, HEAD_DIM) for r in (ka_ref, va_ref, kb_ref, vb_ref))
    kv = ka, beside_ones(va), kb, beside_ones(vb)
    outs = []
    for at in range(0, src * rows, SUB):
        acc, peak, total = softmax_rows(q[at : at + SUB], *kv)
        outs.append(acc)
        peak_ref[at : at + SUB] = jnp.broadcast_to(peak, (SUB, HEAD_DIM))
        total_ref[at : at + SUB] = total
    o_ref[...] = jnp.concatenate(outs, axis=0).reshape(o_ref.shape)


def partial_attend(got, other, rows_kv, rows_q):
    chips, _, width = got.shape
    heads = width // HEAD_DIM
    own_kv = got[:, : 2 * rows_kv].reshape(chips, 2, rows_kv, width)
    own_q = got[:, 2 * rows_kv :]
    other = other.reshape(chips, 2, rows_kv, width)

    def kv(which):
        return pl.BlockSpec((chips, None, rows_kv, HEAD_DIM), lambda h: (0, which, 0, h))

    q_spec = pl.BlockSpec((chips, rows_q, HEAD_DIM), lambda h: (0, 0, h))
    stat_spec = pl.BlockSpec((None, chips * rows_q, HEAD_DIM), lambda h: (h, 0, 0))
    stat = jax.ShapeDtypeStruct((heads, chips * rows_q, HEAD_DIM), F32)
    return pl.pallas_call(
        partial_head,
        grid=(heads,),
        in_specs=[q_spec, kv(0), kv(1), kv(0), kv(1)],
        out_specs=[q_spec, stat_spec, stat_spec],
        out_shape=[jax.ShapeDtypeStruct((chips, rows_q, width), F32), stat, stat],
        compiler_params=PARAMS,
    )(own_q, own_kv, own_kv, other, other)


def local_blocks(keys, values, queries):
    chips = lax.axis_size("chip")
    blocks = chips // GROUPS
    ctx_rows, width = keys.shape
    gw = width // GROUPS
    heads = gw // HEAD_DIM
    layers, tok_rows, _ = queries.shape
    rows_q = layers * tok_rows
    rows_kv = ctx_rows // blocks

    def by_chip(array):
        return jnp.swapaxes(array.reshape(rows_kv, chips, gw), 0, 1)

    q = jnp.swapaxes(queries.reshape(rows_q, GROUPS, gw), 0, 1)
    q = jnp.broadcast_to(q[None], (blocks, GROUPS, rows_q, gw)).reshape(chips, rows_q, gw)
    packed = jnp.concatenate([by_chip(keys), by_chip(values), q], axis=1)
    got = lax.all_to_all(packed, "chip", split_axis=0, concat_axis=0, tiled=True)
    other = lax.ppermute(got[:, : 2 * rows_kv], "core", [(0, 1), (1, 0)])
    outs = partial_attend(got, other, rows_kv, rows_q)
    stats = [jnp.moveaxis(s[:, :, 0].reshape(heads, chips, rows_q), 0, 2) for s in outs[1:]]
    stats = jnp.concatenate(stats, axis=2)
    stats = jnp.pad(stats, ((0, 0), (0, 0), (0, -2 * heads % HEAD_DIM)))
    sent = jnp.concatenate([outs[0], stats], axis=2)
    back = lax.all_to_all(sent, "chip", split_axis=0, concat_axis=0, tiled=True)
    back = back.reshape(blocks, GROUPS, rows_q, -1)
    summed = back[..., :gw].reshape(blocks, GROUPS, rows_q, heads, HEAD_DIM)
    peak = back[..., gw : gw + heads]
    total = back[..., gw + heads : gw + 2 * heads]
    share = jnp.exp2(peak - jnp.max(peak, axis=0))
    denom = jnp.sum(share * total, axis=0)
    numer = jnp.sum(share[..., None] * summed, axis=0)
    result = (numer / denom[..., None]).astype(BF16)
    return jnp.swapaxes(result.reshape(GROUPS, rows_q, gw), 0, 1).reshape(layers, tok_rows, width)


def solution(mesh):
    rep, seq = mesh.shape["rep"], mesh.shape["seq"]
    chips = seq // 2
    by_core = Mesh(mesh.devices.reshape(rep, chips, 2), ("rep", "chip", "core"))
    rows = ("rep", "chip", "core")
    return jax.shard_map(
        local_permutes if chips == GROUPS else local_blocks,
        mesh=by_core,
        in_specs=(P(rows, None), P(rows, None), P(None, rows, None)),
        out_specs=P(None, rows, None),
        check_vma=False,
    )
```

```python
import functools
import math

import jax
import jax.numpy as jnp
from jax import lax
from jax.experimental import pallas as pl
from jax.experimental.pallas import tpu as pltpu
from jax.sharding import Mesh, PartitionSpec as P

HEAD_DIM = 128
GROUPS = 8
SUB = 128
F32 = jnp.float32
BF16 = jnp.bfloat16
VMEM = pl.BlockSpec(memory_space=pltpu.VMEM)
HBM = pl.BlockSpec(memory_space=pltpu.HBM)
SMEM = pl.BlockSpec(memory_space=pltpu.SMEM)
FREE = pl.CostEstimate(flops=0, bytes_accessed=0, transcendentals=0)
PARAMS = pltpu.CompilerParams(vmem_limit_bytes=40 * 2**20)


def softmax_rows(q, ka, va, kb, vb):
    factor = math.log2(math.e) / math.sqrt(HEAD_DIM)
    nt = (((1,), (1,)), ((), ()))
    sa = lax.dot_general(q, ka, nt, preferred_element_type=F32)
    sb = lax.dot_general(q, kb, nt, preferred_element_type=F32)
    peak = jnp.max(jnp.maximum(sa, sb), axis=1, keepdims=True)
    ea = jnp.exp2((sa - peak) * factor).astype(BF16)
    eb = jnp.exp2((sb - peak) * factor).astype(BF16)
    both = jnp.dot(ea, va, preferred_element_type=F32) + jnp.dot(eb, vb, preferred_element_type=F32)
    return both[:, :HEAD_DIM], peak * factor, both[:, HEAD_DIM:]


def beside_ones(v):
    return jnp.concatenate([v, jnp.ones_like(v)], axis=1)


FIRST = (6, 7)
REST = (2, 4, 5, 3, 1, 0)
LAST = (6, 7)
NEAR = (2, 3, 1)


def pack_body(rows, gw, layout, chip_ref, *refs):
    arrays, out_refs, sems = refs[:3], refs[3:-1], refs[-1]
    copies = []
    for out_ref, (k, parts) in zip(out_refs, layout):
        col = pl.ds(pl.multiple_of((chip_ref[0] ^ k) * gw, HEAD_DIM), gw)
        for at, n in enumerate(parts):
            to = out_ref.at[at * rows : (at + 1) * rows]
            copies.append(pltpu.make_async_copy(arrays[n].at[:, col], to, sems.at[len(copies)]))
    for copy in copies:
        copy.start()
    for copy in copies:
        copy.wait()


def merge_body(rows, *refs):
    out_ref = refs[-1]
    for n, piece in enumerate(refs[:-1]):
        for which in range(2):
            out_ref[which, n * rows : (n + 1) * rows] = piece[which * rows : (which + 1) * rows]


def unpack_body(gw, order, chip_ref, *refs):
    pieces, out_ref, sems = refs[: len(order)], refs[-2], refs[-1]
    copies = []
    for n, k in enumerate(order):
        col = pl.ds(pl.multiple_of((chip_ref[0] ^ k) * gw, HEAD_DIM), gw)
        copies.append(pltpu.make_async_copy(pieces[n], out_ref.at[:, col], sems.at[n]))
    for copy in copies:
        copy.start()
    for copy in copies:
        copy.wait()


def attend_body(count, rows, own, other, *refs):
    queries, outs = refs[:count], refs[count:]
    for h in range(own.shape[2] // HEAD_DIM):
        col = slice(h * HEAD_DIM, (h + 1) * HEAD_DIM)
        q = jnp.concatenate([r[r.shape[0] - rows :, col] for r in queries], axis=0)
        va, vb = beside_ones(own[1, :, col]), beside_ones(other[1, :, col])
        acc, _, total = softmax_rows(q, own[0, :, col], va, other[0, :, col], vb)
        acc = (acc / total).astype(BF16)
        for n, out in enumerate(outs):
            out[:, col] = acc[n * rows : (n + 1) * rows]


def local_permutes(keys, values, queries):
    chips = lax.axis_size("chip")
    rows, width = keys.shape
    gw = width // chips
    layers, tok_rows, _ = queries.shape
    rows_q = layers * tok_rows
    assert rows_q == rows
    chip = lax.axis_index("chip").reshape(1).astype(jnp.int32)

    def across(piece, k):
        return lax.ppermute(piece, "chip", [(i, i ^ k) for i in range(chips)]) if k else piece

    def call(body, n_in, out_shape, smem=0, **more):
        return pl.pallas_call(
            body,
            in_specs=[SMEM] * smem + [VMEM] * n_in,
            out_specs=jax.tree.map(lambda _: VMEM, out_shape),
            out_shape=out_shape,
            compiler_params=PARAMS,
            cost_estimate=FREE,
            **more,
        )

    def shape(*dims):
        return jax.ShapeDtypeStruct(dims, BF16)

    sources = [keys, values, queries.reshape(rows_q, width)]
    sources = [pltpu.with_memory_space_constraint(a, pltpu.HBM) for a in sources]

    def pack(layout, after=()):
        arrays = lax.optimization_barrier((*sources, *after))[:3] if after else sources
        return pl.pallas_call(
            functools.partial(pack_body, rows, gw, layout),
            in_specs=[SMEM, HBM, HBM, HBM],
            out_specs=[VMEM] * len(layout),
            out_shape=[shape(len(parts) * rows, gw) for _, parts in layout],
            scratch_shapes=[pltpu.SemaphoreType.DMA((sum(len(parts) for _, parts in layout),))],
            compiler_params=PARAMS,
            cost_estimate=FREE,
        )(chip, *arrays)

    layout = [(k, (0, 1) if k in LAST else (0, 1, 2)) for k in FIRST + REST]
    layout += [(k, (2,)) for k in LAST]
    packed = pack(layout[: len(FIRST)])
    packed += pack(layout[len(FIRST) :], packed[:1])
    got = [across(piece, k) for piece, (k, _) in zip(packed, layout)]
    late = dict(zip(LAST, got[chips:]))
    got = {k: piece for piece, (k, _) in zip(got[:chips], layout)}
    own = call(functools.partial(merge_body, rows), chips, shape(2, chips * rows, gw))(*got.values())
    other = lax.ppermute(own, "core", [(0, 1), (1, 0)])

    def attend(ks, after=()):
        pieces = [late.get(k, got[k]) for k in ks]
        if after:
            pieces = lax.optimization_barrier((*pieces, *after))[: len(pieces)]
        body = functools.partial(attend_body, len(ks), rows)
        outs = call(body, 2 + len(ks), [shape(rows, gw)] * len(ks))(own, other, *pieces)
        return dict(zip(ks, outs))

    outs = attend((4, 5))
    outs |= attend(NEAR + (0,), (outs[4],))
    outs |= attend(LAST, (outs[0],))
    back = {k: across(outs[k], k) for k in (4, 5, 1) + LAST + (0,)}
    def after(array, *others):
        return lax.optimization_barrier((array, *others))[0]

    back[2] = across(after(outs[2], outs[LAST[0]]), 2)
    back[3] = across(after(outs[3], outs[LAST[0]], back[5]), 3)

    def unpack(order, so_far=()):
        return pl.pallas_call(
            functools.partial(unpack_body, gw, order),
            in_specs=[SMEM] + [VMEM] * len(order) + [HBM] * len(so_far),
            out_specs=HBM,
            out_shape=shape(rows_q, width),
            scratch_shapes=[pltpu.SemaphoreType.DMA((len(order),))],
            input_output_aliases={1 + len(order): 0} if so_far else {},
            compiler_params=PARAMS,
            cost_estimate=FREE,
        )(chip, *[back[k] for k in order], *so_far)

    result = unpack(LAST + (3,), (unpack((0, 4, 5, 1, 2)),))
    return result.reshape(layers, tok_rows, width)


def partial_head(q_ref, ka_ref, va_ref, kb_ref, vb_ref, o_ref, peak_ref, total_ref):
    src, rows, _ = q_ref.shape
    q = q_ref[...].reshape(src * rows, HEAD_DIM)
    ka, va, kb, vb = (r[...].reshape(-1, HEAD_DIM) for r in (ka_ref, va_ref, kb_ref, vb_ref))
    kv = ka, beside_ones(va), kb, beside_ones(vb)
    outs = []
    for at in range(0, src * rows, SUB):
        acc, peak, total = softmax_rows(q[at : at + SUB], *kv)
        outs.append(acc)
        peak_ref[at : at + SUB] = jnp.broadcast_to(peak, (SUB, HEAD_DIM))
        total_ref[at : at + SUB] = total
    o_ref[...] = jnp.concatenate(outs, axis=0).reshape(o_ref.shape)


def partial_attend(got, other, rows_kv, rows_q):
    chips, _, width = got.shape
    heads = width // HEAD_DIM
    own_kv = got[:, : 2 * rows_kv].reshape(chips, 2, rows_kv, width)
    own_q = got[:, 2 * rows_kv :]
    other = other.reshape(chips, 2, rows_kv, width)

    def kv(which):
        return pl.BlockSpec((chips, None, rows_kv, HEAD_DIM), lambda h: (0, which, 0, h))

    q_spec = pl.BlockSpec((chips, rows_q, HEAD_DIM), lambda h: (0, 0, h))
    stat_spec = pl.BlockSpec((None, chips * rows_q, HEAD_DIM), lambda h: (h, 0, 0))
    stat = jax.ShapeDtypeStruct((heads, chips * rows_q, HEAD_DIM), F32)
    return pl.pallas_call(
        partial_head,
        grid=(heads,),
        in_specs=[q_spec, kv(0), kv(1), kv(0), kv(1)],
        out_specs=[q_spec, stat_spec, stat_spec],
        out_shape=[jax.ShapeDtypeStruct((chips, rows_q, width), F32), stat, stat],
        compiler_params=PARAMS,
    )(own_q, own_kv, own_kv, other, other)


def local_blocks(keys, values, queries):
    chips = lax.axis_size("chip")
    blocks = chips // GROUPS
    ctx_rows, width = keys.shape
    gw = width // GROUPS
    heads = gw // HEAD_DIM
    layers, tok_rows, _ = queries.shape
    rows_q = layers * tok_rows
    rows_kv = ctx_rows // blocks

    def by_chip(array):
        return jnp.swapaxes(array.reshape(rows_kv, chips, gw), 0, 1)

    q = jnp.swapaxes(queries.reshape(rows_q, GROUPS, gw), 0, 1)
    q = jnp.broadcast_to(q[None], (blocks, GROUPS, rows_q, gw)).reshape(chips, rows_q, gw)
    packed = jnp.concatenate([by_chip(keys), by_chip(values), q], axis=1)
    got = lax.all_to_all(packed, "chip", split_axis=0, concat_axis=0, tiled=True)
    other = lax.ppermute(got[:, : 2 * rows_kv], "core", [(0, 1), (1, 0)])
    outs = partial_attend(got, other, rows_kv, rows_q)
    stats = [jnp.moveaxis(s[:, :, 0].reshape(heads, chips, rows_q), 0, 2) for s in outs[1:]]
    stats = jnp.concatenate(stats, axis=2)
    stats = jnp.pad(stats, ((0, 0), (0, 0), (0, -2 * heads % HEAD_DIM)))
    sent = jnp.concatenate([outs[0], stats], axis=2)
    back = lax.all_to_all(sent, "chip", split_axis=0, concat_axis=0, tiled=True)
    back = back.reshape(blocks, GROUPS, rows_q, -1)
    summed = back[..., :gw].reshape(blocks, GROUPS, rows_q, heads, HEAD_DIM)
    peak = back[..., gw : gw + heads]
    total = back[..., gw + heads : gw + 2 * heads]
    share = jnp.exp2(peak - jnp.max(peak, axis=0))
    denom = jnp.sum(share * total, axis=0)
    numer = jnp.sum(share[..., None] * summed, axis=0)
    result = (numer / denom[..., None]).astype(BF16)
    return jnp.swapaxes(result.reshape(GROUPS, rows_q, gw), 0, 1).reshape(layers, tok_rows, width)


def solution(mesh):
    rep, seq = mesh.shape["rep"], mesh.shape["seq"]
    chips = seq // 2
    by_core = Mesh(mesh.devices.reshape(rep, chips, 2), ("rep", "chip", "core"))
    rows = ("rep", "chip", "core")
    return jax.shard_map(
        local_permutes if chips == GROUPS else local_blocks,
        mesh=by_core,
        in_specs=(P(rows, None), P(rows, None), P(None, rows, None)),
        out_specs=P(None, rows, None),
        check_vma=False,
    )
```

```python
import functools
import math

import jax
import jax.numpy as jnp
from jax import lax
from jax.experimental import pallas as pl
from jax.experimental.pallas import tpu as pltpu
from jax.sharding import Mesh, PartitionSpec as P

HEAD_DIM = 128
GROUPS = 8
SUB = 128
F32 = jnp.float32
BF16 = jnp.bfloat16
VMEM = pl.BlockSpec(memory_space=pltpu.VMEM)
HBM = pl.BlockSpec(memory_space=pltpu.HBM)
SMEM = pl.BlockSpec(memory_space=pltpu.SMEM)
FREE = pl.CostEstimate(flops=0, bytes_accessed=0, transcendentals=0)
PARAMS = pltpu.CompilerParams(vmem_limit_bytes=40 * 2**20)


def softmax_rows(q, ka, va, kb, vb):
    factor = math.log2(math.e) / math.sqrt(HEAD_DIM)
    nt = (((1,), (1,)), ((), ()))
    sa = lax.dot_general(q, ka, nt, preferred_element_type=F32)
    sb = lax.dot_general(q, kb, nt, preferred_element_type=F32)
    peak = jnp.max(jnp.maximum(sa, sb), axis=1, keepdims=True)
    ea = jnp.exp2((sa - peak) * factor).astype(BF16)
    eb = jnp.exp2((sb - peak) * factor).astype(BF16)
    both = jnp.dot(ea, va, preferred_element_type=F32) + jnp.dot(eb, vb, preferred_element_type=F32)
    return both[:, :HEAD_DIM], peak * factor, both[:, HEAD_DIM:]


def beside_ones(v):
    return jnp.concatenate([v, jnp.ones_like(v)], axis=1)


FIRST = (6, 7)
REST = (2, 4, 5, 3, 1, 0)
LAST = (6, 7)
NEAR = (2, 3, 1)


def pack_body(rows, gw, layout, chip_ref, *refs):
    arrays, out_refs, sems = refs[:3], refs[3:-1], refs[-1]
    copies = []
    for out_ref, (k, parts) in zip(out_refs, layout):
        col = pl.ds(pl.multiple_of((chip_ref[0] ^ k) * gw, HEAD_DIM), gw)
        for at, n in enumerate(parts):
            to = out_ref.at[at * rows : (at + 1) * rows]
            copies.append(pltpu.make_async_copy(arrays[n].at[:, col], to, sems.at[len(copies)]))
    for copy in copies:
        copy.start()
    for copy in copies:
        copy.wait()


def merge_body(rows, *refs):
    out_ref = refs[-1]
    for n, piece in enumerate(refs[:-1]):
        for which in range(2):
            out_ref[which, n * rows : (n + 1) * rows] = piece[which * rows : (which + 1) * rows]


def unpack_body(gw, order, chip_ref, *refs):
    pieces, out_ref, sems = refs[: len(order)], refs[-2], refs[-1]
    copies = []
    for n, k in enumerate(order):
        col = pl.ds(pl.multiple_of((chip_ref[0] ^ k) * gw, HEAD_DIM), gw)
        copies.append(pltpu.make_async_copy(pieces[n], out_ref.at[:, col], sems.at[n]))
    for copy in copies:
        copy.start()
    for copy in copies:
        copy.wait()


def attend_body(count, rows, own, other, *refs):
    queries, outs = refs[:count], refs[count:]
    for h in range(own.shape[2] // HEAD_DIM):
        col = slice(h * HEAD_DIM, (h + 1) * HEAD_DIM)
        q = jnp.concatenate([r[r.shape[0] - rows :, col] for r in queries], axis=0)
        va, vb = beside_ones(own[1, :, col]), beside_ones(other[1, :, col])
        acc, _, total = softmax_rows(q, own[0, :, col], va, other[0, :, col], vb)
        acc = (acc / total).astype(BF16)
        for n, out in enumerate(outs):
            out[:, col] = acc[n * rows : (n + 1) * rows]


def local_permutes(keys, values, queries):
    chips = lax.axis_size("chip")
    rows, width = keys.shape
    gw = width // chips
    layers, tok_rows, _ = queries.shape
    rows_q = layers * tok_rows
    assert rows_q == rows
    chip = lax.axis_index("chip").reshape(1).astype(jnp.int32)

    def across(piece, k):
        return lax.ppermute(piece, "chip", [(i, i ^ k) for i in range(chips)]) if k else piece

    def call(body, n_in, out_shape, smem=0, **more):
        return pl.pallas_call(
            body,
            in_specs=[SMEM] * smem + [VMEM] * n_in,
            out_specs=jax.tree.map(lambda _: VMEM, out_shape),
            out_shape=out_shape,
            compiler_params=PARAMS,
            cost_estimate=FREE,
            **more,
        )

    def shape(*dims):
        return jax.ShapeDtypeStruct(dims, BF16)

    sources = [keys, values, queries.reshape(rows_q, width)]
    sources = [pltpu.with_memory_space_constraint(a, pltpu.HBM) for a in sources]

    def pack(layout, after=()):
        arrays = lax.optimization_barrier((*sources, *after))[:3] if after else sources
        return pl.pallas_call(
            functools.partial(pack_body, rows, gw, layout),
            in_specs=[SMEM, HBM, HBM, HBM],
            out_specs=[VMEM] * len(layout),
            out_shape=[shape(len(parts) * rows, gw) for _, parts in layout],
            scratch_shapes=[pltpu.SemaphoreType.DMA((sum(len(parts) for _, parts in layout),))],
            compiler_params=PARAMS,
            cost_estimate=FREE,
        )(chip, *arrays)

    layout = [(k, (0, 1) if k in LAST else (0, 1, 2)) for k in FIRST + REST]
    layout += [(k, (2,)) for k in LAST]
    packed = pack(layout[: len(FIRST)])
    packed += pack(layout[len(FIRST) :], packed[:1])
    got = [across(piece, k) for piece, (k, _) in zip(packed, layout)]
    late = dict(zip(LAST, got[chips:]))
    got = {k: piece for piece, (k, _) in zip(got[:chips], layout)}
    own = call(functools.partial(merge_body, rows), chips, shape(2, chips * rows, gw))(*got.values())
    other = lax.ppermute(own, "core", [(0, 1), (1, 0)])

    def attend(ks, after=()):
        pieces = [late.get(k, got[k]) for k in ks]
        if after:
            pieces = lax.optimization_barrier((*pieces, *after))[: len(pieces)]
        body = functools.partial(attend_body, len(ks), rows)
        outs = call(body, 2 + len(ks), [shape(rows, gw)] * len(ks))(own, other, *pieces)
        return dict(zip(ks, outs))

    outs = attend((4, 5))
    outs |= attend(NEAR + (0,), (outs[4],))
    outs |= attend(LAST, (outs[0],))
    back = {k: across(outs[k], k) for k in (4, 5, 1) + LAST + (0,)}
    def after(array, *others):
        return lax.optimization_barrier((array, *others))[0]

    back[2] = across(after(outs[2], outs[LAST[0]]), 2)
    back[3] = across(after(outs[3], outs[LAST[0]], back[5]), 3)

    def unpack(order, so_far=()):
        return pl.pallas_call(
            functools.partial(unpack_body, gw, order),
            in_specs=[SMEM] + [VMEM] * len(order) + [HBM] * len(so_far),
            out_specs=HBM,
            out_shape=shape(rows_q, width),
            scratch_shapes=[pltpu.SemaphoreType.DMA((len(order),))],
            input_output_aliases={1 + len(order): 0} if so_far else {},
            compiler_params=PARAMS,
            cost_estimate=FREE,
        )(chip, *[back[k] for k in order], *so_far)

    result = unpack(LAST + (3, 2), (unpack((0, 4, 5, 1)),))
    return result.reshape(layers, tok_rows, width)


def partial_head(q_ref, ka_ref, va_ref, kb_ref, vb_ref, o_ref, peak_ref, total_ref):
    src, rows, _ = q_ref.shape
    q = q_ref[...].reshape(src * rows, HEAD_DIM)
    ka, va, kb, vb = (r[...].reshape(-1, HEAD_DIM) for r in (ka_ref, va_ref, kb_ref, vb_ref))
    kv = ka, beside_ones(va), kb, beside_ones(vb)
    outs = []
    for at in range(0, src * rows, SUB):
        acc, peak, total = softmax_rows(q[at : at + SUB], *kv)
        outs.append(acc)
        peak_ref[at : at + SUB] = jnp.broadcast_to(peak, (SUB, HEAD_DIM))
        total_ref[at : at + SUB] = total
    o_ref[...] = jnp.concatenate(outs, axis=0).reshape(o_ref.shape)


def partial_attend(got, other, rows_kv, rows_q):
    chips, _, width = got.shape
    heads = width // HEAD_DIM
    own_kv = got[:, : 2 * rows_kv].reshape(chips, 2, rows_kv, width)
    own_q = got[:, 2 * rows_kv :]
    other = other.reshape(chips, 2, rows_kv, width)

    def kv(which):
        return pl.BlockSpec((chips, None, rows_kv, HEAD_DIM), lambda h: (0, which, 0, h))

    q_spec = pl.BlockSpec((chips, rows_q, HEAD_DIM), lambda h: (0, 0, h))
    stat_spec = pl.BlockSpec((None, chips * rows_q, HEAD_DIM), lambda h: (h, 0, 0))
    stat = jax.ShapeDtypeStruct((heads, chips * rows_q, HEAD_DIM), F32)
    return pl.pallas_call(
        partial_head,
        grid=(heads,),
        in_specs=[q_spec, kv(0), kv(1), kv(0), kv(1)],
        out_specs=[q_spec, stat_spec, stat_spec],
        out_shape=[jax.ShapeDtypeStruct((chips, rows_q, width), F32), stat, stat],
        compiler_params=PARAMS,
    )(own_q, own_kv, own_kv, other, other)


def local_blocks(keys, values, queries):
    chips = lax.axis_size("chip")
    blocks = chips // GROUPS
    ctx_rows, width = keys.shape
    gw = width // GROUPS
    heads = gw // HEAD_DIM
    layers, tok_rows, _ = queries.shape
    rows_q = layers * tok_rows
    rows_kv = ctx_rows // blocks

    def by_chip(array):
        return jnp.swapaxes(array.reshape(rows_kv, chips, gw), 0, 1)

    q = jnp.swapaxes(queries.reshape(rows_q, GROUPS, gw), 0, 1)
    q = jnp.broadcast_to(q[None], (blocks, GROUPS, rows_q, gw)).reshape(chips, rows_q, gw)
    packed = jnp.concatenate([by_chip(keys), by_chip(values), q], axis=1)
    got = lax.all_to_all(packed, "chip", split_axis=0, concat_axis=0, tiled=True)
    other = lax.ppermute(got[:, : 2 * rows_kv], "core", [(0, 1), (1, 0)])
    outs = partial_attend(got, other, rows_kv, rows_q)
    stats = [jnp.moveaxis(s[:, :, 0].reshape(heads, chips, rows_q), 0, 2) for s in outs[1:]]
    stats = jnp.concatenate(stats, axis=2)
    stats = jnp.pad(stats, ((0, 0), (0, 0), (0, -2 * heads % HEAD_DIM)))
    sent = jnp.concatenate([outs[0], stats], axis=2)
    back = lax.all_to_all(sent, "chip", split_axis=0, concat_axis=0, tiled=True)
    back = back.reshape(blocks, GROUPS, rows_q, -1)
    summed = back[..., :gw].reshape(blocks, GROUPS, rows_q, heads, HEAD_DIM)
    peak = back[..., gw : gw + heads]
    total = back[..., gw + heads : gw + 2 * heads]
    share = jnp.exp2(peak - jnp.max(peak, axis=0))
    denom = jnp.sum(share * total, axis=0)
    numer = jnp.sum(share[..., None] * summed, axis=0)
    result = (numer / denom[..., None]).astype(BF16)
    return jnp.swapaxes(result.reshape(GROUPS, rows_q, gw), 0, 1).reshape(layers, tok_rows, width)


def solution(mesh):
    rep, seq = mesh.shape["rep"], mesh.shape["seq"]
    chips = seq // 2
    by_core = Mesh(mesh.devices.reshape(rep, chips, 2), ("rep", "chip", "core"))
    rows = ("rep", "chip", "core")
    return jax.shard_map(
        local_permutes if chips == GROUPS else local_blocks,
        mesh=by_core,
        in_specs=(P(rows, None), P(rows, None), P(None, rows, None)),
        out_specs=P(None, rows, None),
        check_vma=False,
    )
```

```python
import functools
import math

import jax
import jax.numpy as jnp
from jax import lax
from jax.experimental import pallas as pl
from jax.experimental.pallas import tpu as pltpu
from jax.sharding import Mesh, PartitionSpec as P

HEAD_DIM = 128
GROUPS = 8
SUB = 128
F32 = jnp.float32
BF16 = jnp.bfloat16
VMEM = pl.BlockSpec(memory_space=pltpu.VMEM)
HBM = pl.BlockSpec(memory_space=pltpu.HBM)
SMEM = pl.BlockSpec(memory_space=pltpu.SMEM)
FREE = pl.CostEstimate(flops=0, bytes_accessed=0, transcendentals=0)
PARAMS = pltpu.CompilerParams(vmem_limit_bytes=40 * 2**20)


def softmax_rows(q, ka, va, kb, vb):
    factor = math.log2(math.e) / math.sqrt(HEAD_DIM)
    nt = (((1,), (1,)), ((), ()))
    sa = lax.dot_general(q, ka, nt, preferred_element_type=F32)
    sb = lax.dot_general(q, kb, nt, preferred_element_type=F32)
    peak = jnp.max(jnp.maximum(sa, sb), axis=1, keepdims=True)
    ea = jnp.exp2((sa - peak) * factor).astype(BF16)
    eb = jnp.exp2((sb - peak) * factor).astype(BF16)
    both = jnp.dot(ea, va, preferred_element_type=F32) + jnp.dot(eb, vb, preferred_element_type=F32)
    return both[:, :HEAD_DIM], peak * factor, both[:, HEAD_DIM:]


def beside_ones(v):
    return jnp.concatenate([v, jnp.ones_like(v)], axis=1)


FIRST = (6, 7)
REST = (4, 5, 2, 3, 1, 0)
LAST = (6, 7)
NEAR = (2, 3, 1)


def pack_body(rows, gw, layout, chip_ref, *refs):
    arrays, out_refs, sems = refs[:3], refs[3:-1], refs[-1]
    copies = []
    for out_ref, (k, parts) in zip(out_refs, layout):
        col = pl.ds(pl.multiple_of((chip_ref[0] ^ k) * gw, HEAD_DIM), gw)
        for at, n in enumerate(parts):
            to = out_ref.at[at * rows : (at + 1) * rows]
            copies.append(pltpu.make_async_copy(arrays[n].at[:, col], to, sems.at[len(copies)]))
    for copy in copies:
        copy.start()
    for copy in copies:
        copy.wait()


def merge_body(rows, *refs):
    out_ref = refs[-1]
    for n, piece in enumerate(refs[:-1]):
        for which in range(2):
            out_ref[which, n * rows : (n + 1) * rows] = piece[which * rows : (which + 1) * rows]


def unpack_body(gw, order, chip_ref, *refs):
    pieces, out_ref, sems = refs[: len(order)], refs[-2], refs[-1]
    copies = []
    for n, k in enumerate(order):
        col = pl.ds(pl.multiple_of((chip_ref[0] ^ k) * gw, HEAD_DIM), gw)
        copies.append(pltpu.make_async_copy(pieces[n], out_ref.at[:, col], sems.at[n]))
    for copy in copies:
        copy.start()
    for copy in copies:
        copy.wait()


def attend_body(count, rows, own, other, *refs):
    queries, outs = refs[:count], refs[count:]
    for h in range(own.shape[2] // HEAD_DIM):
        col = slice(h * HEAD_DIM, (h + 1) * HEAD_DIM)
        q = jnp.concatenate([r[r.shape[0] - rows :, col] for r in queries], axis=0)
        va, vb = beside_ones(own[1, :, col]), beside_ones(other[1, :, col])
        acc, _, total = softmax_rows(q, own[0, :, col], va, other[0, :, col], vb)
        acc = (acc / total).astype(BF16)
        for n, out in enumerate(outs):
            out[:, col] = acc[n * rows : (n + 1) * rows]


def local_permutes(keys, values, queries):
    chips = lax.axis_size("chip")
    rows, width = keys.shape
    gw = width // chips
    layers, tok_rows, _ = queries.shape
    rows_q = layers * tok_rows
    assert rows_q == rows
    chip = lax.axis_index("chip").reshape(1).astype(jnp.int32)

    def across(piece, k):
        return lax.ppermute(piece, "chip", [(i, i ^ k) for i in range(chips)]) if k else piece

    def call(body, n_in, out_shape, smem=0, **more):
        return pl.pallas_call(
            body,
            in_specs=[SMEM] * smem + [VMEM] * n_in,
            out_specs=jax.tree.map(lambda _: VMEM, out_shape),
            out_shape=out_shape,
            compiler_params=PARAMS,
            cost_estimate=FREE,
            **more,
        )

    def shape(*dims):
        return jax.ShapeDtypeStruct(dims, BF16)

    sources = [keys, values, queries.reshape(rows_q, width)]
    sources = [pltpu.with_memory_space_constraint(a, pltpu.HBM) for a in sources]

    def pack(layout, after=()):
        arrays = lax.optimization_barrier((*sources, *after))[:3] if after else sources
        return pl.pallas_call(
            functools.partial(pack_body, rows, gw, layout),
            in_specs=[SMEM, HBM, HBM, HBM],
            out_specs=[VMEM] * len(layout),
            out_shape=[shape(len(parts) * rows, gw) for _, parts in layout],
            scratch_shapes=[pltpu.SemaphoreType.DMA((sum(len(parts) for _, parts in layout),))],
            compiler_params=PARAMS,
            cost_estimate=FREE,
        )(chip, *arrays)

    layout = [(k, (0, 1) if k in LAST else (0, 1, 2)) for k in FIRST + REST]
    layout += [(k, (2,)) for k in LAST]
    packed = pack(layout[: len(FIRST)])
    packed += pack(layout[len(FIRST) :], packed[:1])
    got = [across(piece, k) for piece, (k, _) in zip(packed, layout)]
    late = dict(zip(LAST, got[chips:]))
    got = {k: piece for piece, (k, _) in zip(got[:chips], layout)}
    own = call(functools.partial(merge_body, rows), chips, shape(2, chips * rows, gw))(*got.values())
    other = lax.ppermute(own, "core", [(0, 1), (1, 0)])

    def attend(ks, after=()):
        pieces = [late.get(k, got[k]) for k in ks]
        if after:
            pieces = lax.optimization_barrier((*pieces, *after))[: len(pieces)]
        body = functools.partial(attend_body, len(ks), rows)
        outs = call(body, 2 + len(ks), [shape(rows, gw)] * len(ks))(own, other, *pieces)
        return dict(zip(ks, outs))

    outs = attend((4, 5))
    outs |= attend(NEAR + (0,), (outs[4],))
    outs |= attend(LAST, (outs[0],))
    back = {k: across(outs[k], k) for k in (4, 5, 1) + LAST + (0,)}
    def after(array, *others):
        return lax.optimization_barrier((array, *others))[0]

    back[2] = across(after(outs[2], outs[LAST[0]]), 2)
    back[3] = across(after(outs[3], outs[LAST[0]], back[5]), 3)

    def unpack(order, so_far=()):
        return pl.pallas_call(
            functools.partial(unpack_body, gw, order),
            in_specs=[SMEM] + [VMEM] * len(order) + [HBM] * len(so_far),
            out_specs=HBM,
            out_shape=shape(rows_q, width),
            scratch_shapes=[pltpu.SemaphoreType.DMA((len(order),))],
            input_output_aliases={1 + len(order): 0} if so_far else {},
            compiler_params=PARAMS,
            cost_estimate=FREE,
        )(chip, *[back[k] for k in order], *so_far)

    result = unpack(LAST + (3, 2), (unpack((0, 4, 5, 1)),))
    return result.reshape(layers, tok_rows, width)


def partial_head(q_ref, ka_ref, va_ref, kb_ref, vb_ref, o_ref, peak_ref, total_ref):
    src, rows, _ = q_ref.shape
    q = q_ref[...].reshape(src * rows, HEAD_DIM)
    ka, va, kb, vb = (r[...].reshape(-1, HEAD_DIM) for r in (ka_ref, va_ref, kb_ref, vb_ref))
    kv = ka, beside_ones(va), kb, beside_ones(vb)
    outs = []
    for at in range(0, src * rows, SUB):
        acc, peak, total = softmax_rows(q[at : at + SUB], *kv)
        outs.append(acc)
        peak_ref[at : at + SUB] = jnp.broadcast_to(peak, (SUB, HEAD_DIM))
        total_ref[at : at + SUB] = total
    o_ref[...] = jnp.concatenate(outs, axis=0).reshape(o_ref.shape)


def partial_attend(got, other, rows_kv, rows_q):
    chips, _, width = got.shape
    heads = width // HEAD_DIM
    own_kv = got[:, : 2 * rows_kv].reshape(chips, 2, rows_kv, width)
    own_q = got[:, 2 * rows_kv :]
    other = other.reshape(chips, 2, rows_kv, width)

    def kv(which):
        return pl.BlockSpec((chips, None, rows_kv, HEAD_DIM), lambda h: (0, which, 0, h))

    q_spec = pl.BlockSpec((chips, rows_q, HEAD_DIM), lambda h: (0, 0, h))
    stat_spec = pl.BlockSpec((None, chips * rows_q, HEAD_DIM), lambda h: (h, 0, 0))
    stat = jax.ShapeDtypeStruct((heads, chips * rows_q, HEAD_DIM), F32)
    return pl.pallas_call(
        partial_head,
        grid=(heads,),
        in_specs=[q_spec, kv(0), kv(1), kv(0), kv(1)],
        out_specs=[q_spec, stat_spec, stat_spec],
        out_shape=[jax.ShapeDtypeStruct((chips, rows_q, width), F32), stat, stat],
        compiler_params=PARAMS,
    )(own_q, own_kv, own_kv, other, other)


def local_blocks(keys, values, queries):
    chips = lax.axis_size("chip")
    blocks = chips // GROUPS
    ctx_rows, width = keys.shape
    gw = width // GROUPS
    heads = gw // HEAD_DIM
    layers, tok_rows, _ = queries.shape
    rows_q = layers * tok_rows
    rows_kv = ctx_rows // blocks

    def by_chip(array):
        return jnp.swapaxes(array.reshape(rows_kv, chips, gw), 0, 1)

    q = jnp.swapaxes(queries.reshape(rows_q, GROUPS, gw), 0, 1)
    q = jnp.broadcast_to(q[None], (blocks, GROUPS, rows_q, gw)).reshape(chips, rows_q, gw)
    packed = jnp.concatenate([by_chip(keys), by_chip(values), q], axis=1)
    got = lax.all_to_all(packed, "chip", split_axis=0, concat_axis=0, tiled=True)
    other = lax.ppermute(got[:, : 2 * rows_kv], "core", [(0, 1), (1, 0)])
    outs = partial_attend(got, other, rows_kv, rows_q)
    stats = [jnp.moveaxis(s[:, :, 0].reshape(heads, chips, rows_q), 0, 2) for s in outs[1:]]
    stats = jnp.concatenate(stats, axis=2)
    stats = jnp.pad(stats, ((0, 0), (0, 0), (0, -2 * heads % HEAD_DIM)))
    sent = jnp.concatenate([outs[0], stats], axis=2)
    back = lax.all_to_all(sent, "chip", split_axis=0, concat_axis=0, tiled=True)
    back = back.reshape(blocks, GROUPS, rows_q, -1)
    summed = back[..., :gw].reshape(blocks, GROUPS, rows_q, heads, HEAD_DIM)
    peak = back[..., gw : gw + heads]
    total = back[..., gw + heads : gw + 2 * heads]
    share = jnp.exp2(peak - jnp.max(peak, axis=0))
    denom = jnp.sum(share * total, axis=0)
    numer = jnp.sum(share[..., None] * summed, axis=0)
    result = (numer / denom[..., None]).astype(BF16)
    return jnp.swapaxes(result.reshape(GROUPS, rows_q, gw), 0, 1).reshape(layers, tok_rows, width)


def solution(mesh):
    rep, seq = mesh.shape["rep"], mesh.shape["seq"]
    chips = seq // 2
    by_core = Mesh(mesh.devices.reshape(rep, chips, 2), ("rep", "chip", "core"))
    rows = ("rep", "chip", "core")
    return jax.shard_map(
        local_permutes if chips == GROUPS else local_blocks,
        mesh=by_core,
        in_specs=(P(rows, None), P(rows, None), P(None, rows, None)),
        out_specs=P(None, rows, None),
        check_vma=False,
    )
```
